32 devices in a mesh: dp: 8 (over y, x, core), tensor: 4 (over z).
Axes of the slice: x: 2, y: 2, z: 4, core: 2. Of those that a mesh axis runs over, the one named last changes fastest.
Arguments:
- media_tokens: bfloat16 [32, 1280, 1024], P('dp'), may hold values from -6 to 6
- latents: bfloat16 [32, 64, 1024], P('dp'), may hold values from -6 to 6
- image_counts: int32 [32], P('dp'), may hold values from 1 to 5, as said below
- media_gain: float32 [1024], replicated, may hold values from 0.1 to 1.9
- media_shift: float32 [1024], replicated, may hold values from -1.2 to 1.2
- latent_gain: float32 [1024], replicated, may hold values from 0.1 to 1.9
- latent_shift: float32 [1024], replicated, may hold values from -1.2 to 1.2
- feed_gain: float32 [1024], replicated, may hold values from 0.1 to 1.9
- feed_shift: float32 [1024], replicated, may hold values from -1.2 to 1.2
- query_weight: bfloat16 [1024, 512], P(None, 'tensor'), may hold values from -0.1875 to 0.1875
- key_weight: bfloat16 [1024, 512], P(None, 'tensor'), may hold values from -0.1875 to 0.1875
- value_weight: bfloat16 [1024, 512], P(None, 'tensor'), may hold values from -0.1875 to 0.1875
- output_weight: bfloat16 [512, 1024], P('tensor'), may hold values from -4 to 4
- up_weight: bfloat16 [1024, 4096], P('dp', 'tensor'), may hold values from -0.1875 to 0.1875
- down_weight: bfloat16 [4096, 1024], P('tensor', 'dp'), may hold values from -0.09375 to 0.09375
- cotangent: bfloat16 [32, 64, 1024], P('dp'), may hold values from -6 to 6
Outputs:
- new_latents: bfloat16 [32, 64, 1024], P('dp')
- media_grad: bfloat16 [32, 1280, 1024], P('dp', 'tensor')
- latent_grad: bfloat16 [32, 64, 1024], P('dp')
- query_grad: float32 [1024, 512], P('dp', 'tensor')
- key_grad: float32 [1024, 512], P('dp', 'tensor')
- value_grad: float32 [1024, 512], P('dp', 'tensor')
- output_grad: float32 [512, 1024], P('tensor', 'dp')
- up_grad: float32 [1024, 4096], P('dp', 'tensor')
- down_grad: float32 [4096, 1024], P('tensor', 'dp')
- media_gain_grad: float32 [1024], replicated
- media_shift_grad: float32 [1024], replicated
- latent_gain_grad: float32 [1024], P('dp')
- latent_shift_grad: float32 [1024], P('dp')
- feed_gain_grad: float32 [1024], P('dp')
- feed_shift_grad: float32 [1024], P('dp')
The draws below stay inside these ranges and needn't reach their ends.
Inputs may be any that keep to these rules, and one draw needn't show every extreme that they name: `image_counts`: images of each sample; in every draw all 4 samples of some index of dp hold 5 images and some sample holds 1.
All inputs are finite; a program needn't handle non-finite values.
Results may differ from the reference program's by a relative error of at most 0.014.
Values may be sent and summed in bfloat16 or wider, within the bound.
A program may use at most 192 MiB of HBM per device.

```python
import jax
import jax.numpy as jnp
from jax import lax

D = 1024
HEAD_DIM = 64
FF = 4096
LAT = 64
PATCH = 256
S_DEV = 4
INNER = 512
SLOTS = 1280
KEYS = 1344
SAMPLES = 32


def draw_image_counts(key, part):
    key = jax.random.fold_in(key, 7)
    key_first, key_second, key_group = jax.random.split(key, 3)
    first_pick = jax.random.randint(key_first, (SAMPLES,), 0, 5)
    second_pick = jax.random.randint(key_second, (SAMPLES,), 1, 5)
    counts = 1 + jnp.minimum(first_pick, second_pick)
    groups = SAMPLES // S_DEV
    full_group = jax.random.randint(key_group, (), 0, groups)
    sample_ids = jnp.arange(SAMPLES)
    group_ids = sample_ids // S_DEV
    counts = jnp.where(group_ids == full_group, 5, counts)
    counts = jnp.where(sample_ids == (full_group + 1) % groups * S_DEV, 1, counts)
    return counts.astype(jnp.int32)


def levels(own_key, dims, shards, least, top_value):
    loudness = 1.0
    for dim, blocks in shards:
        heights = jax.random.uniform(jax.random.fold_in(jax.random.fold_in(own_key, 6), dim), (blocks,), jnp.float32, least / len(shards), top_value / len(shards))
        loudness = loudness * jnp.repeat(jnp.exp(heights), dims[dim] // blocks).reshape((-1,) + (1,) * (len(dims) - 1 - dim))
    return loudness


def bell_draw(stream_key, shape, scale, limit, shards=(), dtype=jnp.bfloat16):
    array = jax.random.normal(stream_key, shape, jnp.float32) * scale
    if len(shards) > 0:
        array = levels(stream_key, shape, shards, -0.22, 0.18) * array
    return jnp.clip(array, min=-limit, max=limit).astype(dtype)


def setup_inputs(seed: int = 0) -> dict:
    keys = jax.random.split(jax.random.key(seed), 17)
    return {
        "media_tokens": bell_draw(keys[0], (SAMPLES, SLOTS, D), 1.0, 6.0, ((0, 8),)),
        "latents": bell_draw(keys[1], (SAMPLES, LAT, D), 1.0, 6.0, ((0, 8),)),
        "image_counts": draw_image_counts(jax.random.fold_in(keys[16], 71), 0),
        "media_gain": jnp.clip(1.0 + 0.18 * jax.random.normal(keys[3], (D,), jnp.float32), 0.1, 1.9),
        "media_shift": bell_draw(keys[4], (D,), 0.3, 1.2, (), jnp.float32),
        "latent_gain": jnp.clip(1.0 + 0.18 * jax.random.normal(keys[5], (D,), jnp.float32), 0.1, 1.9),
        "latent_shift": bell_draw(keys[6], (D,), 0.3, 1.2, (), jnp.float32),
        "feed_gain": jnp.clip(1.0 + 0.18 * jax.random.normal(keys[7], (D,), jnp.float32), 0.1, 1.9),
        "feed_shift": bell_draw(keys[8], (D,), 0.3, 1.2, (), jnp.float32),
        "query_weight": bell_draw(keys[9], (D, INNER), D ** -0.5, 0.1875, ((1, 4),)),
        "key_weight": bell_draw(keys[10], (D, INNER), D ** -0.5, 0.1875, ((1, 4),)),
        "value_weight": bell_draw(keys[11], (D, INNER), D ** -0.5, 0.1875, ((1, 4),)),
        "output_weight": bell_draw(keys[12], (INNER, D), (max(INNER // 256, 1)) ** -0.5, 4.0, ((0, 4),)),
        "up_weight": bell_draw(keys[13], (D, FF), D ** -0.5, 0.1875, ((0, 8), (1, 4))),
        "down_weight": bell_draw(keys[14], (FF, D), FF ** -0.5, 0.09375, ((0, 4), (1, 8))),
        "cotangent": bell_draw(keys[15], (SAMPLES, LAT, D), 1.0, 6.0, ((0, 8),)),
    }


EPSILON = 1e-05
NEGATIVE = -1e+30
HIGHEST = lax.Precision.HIGHEST

@jax.custom_vjp
def low(v):
    return lax.optimization_barrier(v.astype(jnp.bfloat16)).astype(jnp.float32)

@jax.custom_vjp
def low_back(v):
    return v

def low_keep(v):
    return (low(v), None)

def low_pass(kept, grad):
    return (grad,)

def back_keep(v):
    return (v, None)

def back_low(kept, grad):
    return (low(grad),)
low.defvjp(low_keep, low_pass)
low_back.defvjp(back_keep, back_low)

def layer_norm(inputs, gain, shift):
    centre = inputs - lax.optimization_barrier(jnp.mean(inputs, axis=-1, keepdims=True))
    spread = lax.optimization_barrier(jnp.mean(centre * centre, axis=-1, keepdims=True))
    return centre * lax.rsqrt(spread + EPSILON) * gain + shift

def project(inputs, weight):
    return jnp.einsum('...i,ij->...j', inputs, weight, precision=HIGHEST)

def block_forward(media_group, latent_group, slot_valid, params):
    media_gain, media_shift, latent_gain, latent_shift, feed_gain, feed_shift, query_weight, key_weight, value_weight, output_weight, up_weight, down_weight = params
    samples = media_group.shape[0]
    heads_all = query_weight.shape[1] // HEAD_DIM
    media_normed = low(layer_norm(media_group, media_gain, media_shift))
    latent_normed = low(layer_norm(latent_group, latent_gain, latent_shift))
    context = jnp.concatenate([media_normed, latent_normed], axis=1)
    queries = low_back(low(project(latent_normed, query_weight))).reshape(samples, LAT, heads_all, HEAD_DIM)
    keys_all = low_back(low(project(context, key_weight))).reshape(samples, KEYS, heads_all, HEAD_DIM)
    values_all = low_back(low(project(context, value_weight))).reshape(samples, KEYS, heads_all, HEAD_DIM)
    scores = jnp.einsum('slhd,skhd->shlk', queries, keys_all, precision=HIGHEST) * HEAD_DIM ** (-0.5)
    scores = low_back(scores)
    scores = jnp.where(slot_valid[:, None, None, :], scores, NEGATIVE)
    largest = lax.optimization_barrier(jnp.max(scores, axis=-1, keepdims=True))
    exps = jnp.exp(scores - largest)
    probs = low(exps / lax.optimization_barrier(jnp.sum(exps, axis=-1, keepdims=True)))
    attended = jnp.einsum('shlk,skhd->slhd', probs, values_all, precision=HIGHEST)
    attended = attended.reshape(samples, LAT, heads_all * HEAD_DIM)
    attended = low_back(low(attended))
    residual = latent_group + low_back(project(attended, output_weight))
    hidden_in = low(layer_norm(residual, feed_gain, feed_shift))
    before = low_back(project(hidden_in, up_weight))
    activated = low_back(low(jax.nn.gelu(before, approximate=False)))
    return residual + low_back(project(activated, down_weight))

def add_terms(first_term, second_term):
    return first_term + second_term

def reference(media_tokens, latents, image_counts, media_gain, media_shift, latent_gain, latent_shift, feed_gain, feed_shift, query_weight, key_weight, value_weight, output_weight, up_weight, down_weight, cotangent):
    params = tuple((weight_in.astype(jnp.float32) for weight_in in (media_gain, media_shift, latent_gain, latent_shift, feed_gain, feed_shift, query_weight, key_weight, value_weight, output_weight, up_weight, down_weight)))
    groups = SAMPLES // S_DEV
    slot_ids = jnp.arange(KEYS).astype(jnp.int32)
    media_blocks = media_tokens.reshape(groups, S_DEV, SLOTS, D)
    latent_blocks = latents.reshape(groups, S_DEV, LAT, D)
    count_blocks = image_counts.reshape(groups, S_DEV).astype(jnp.int32)
    cot_blocks = cotangent.reshape(groups, S_DEV, LAT, D)

    def one_block(totals, inputs):
        media_group, latent_group, counts, cot_group = inputs
        slot_valid = (slot_ids[None, :] < counts[:, None] * PATCH) | (slot_ids[None, :] >= SLOTS)

        def forward(media_in, latent_in, param_in):
            return block_forward(media_in, latent_in, slot_valid, param_in)
        output, pullback = jax.vjp(forward, media_group.astype(jnp.float32), latent_group.astype(jnp.float32), params)
        media_back, latent_back, param_back = pullback(cot_group.astype(jnp.float32))
        totals = jax.tree.map(add_terms, totals, param_back)
        return (totals, (output.astype(jnp.bfloat16), media_back.astype(jnp.bfloat16), latent_back.astype(jnp.bfloat16)))
    zeros = jax.tree.map(jnp.zeros_like, params)
    totals, stacked = lax.scan(one_block, zeros, (media_blocks, latent_blocks, count_blocks, cot_blocks))
    new_latents = stacked[0].reshape(SAMPLES, LAT, D)
    media_grad = stacked[1].reshape(SAMPLES, SLOTS, D)
    latent_grad = stacked[2].reshape(SAMPLES, LAT, D)
    media_gain_grad, media_shift_grad, latent_gain_grad, latent_shift_grad, feed_gain_grad, feed_shift_grad, query_grad, key_grad, value_grad, output_grad, up_grad, down_grad = totals
    return (new_latents, media_grad, latent_grad, query_grad, key_grad, value_grad, output_grad, up_grad, down_grad, media_gain_grad, media_shift_grad, latent_gain_grad, latent_shift_grad, feed_gain_grad, feed_shift_grad)
```

```python
import functools

import jax
import jax.numpy as jnp
from jax import lax
from jax.experimental import pallas as pl
from jax.experimental.pallas import tpu as pltpu
from jax.sharding import PartitionSpec as P

HEAD_DIM = 64
PATCH = 256
EPSILON = 1e-05
NEGATIVE = -1e30
SQRT_HALF = 0.7071067811865476
INV_ROOT_TWO_PI = 0.3989422804014327
F32 = jnp.float32
BF16 = jnp.bfloat16
MESH = pl.DeviceIdType.MESH
BLOCK = 256
ROWS = 32
SLOTS_IN_FLIGHT = 3


def nn(left, right):
    return lax.dot_general(left, right, (((1,), (0,)), ((), ())), preferred_element_type=F32)


def nt(left, right):
    return lax.dot_general(left, right, (((1,), (1,)), ((), ())), preferred_element_type=F32)


def tn(left, right):
    return lax.dot_general(left, right, (((0,), (0,)), ((), ())), preferred_element_type=F32)


def unit_rows(x):
    centre = x - jnp.mean(x, axis=-1, keepdims=True)
    scale_inv = lax.rsqrt(jnp.mean(centre * centre, axis=-1, keepdims=True) + EPSILON)
    return centre * scale_inv, scale_inv


def norm_back(unit, scale_inv, gain, upstream):
    scaled = upstream * gain
    inner = scaled - jnp.mean(scaled, axis=-1, keepdims=True)
    inner = inner - unit * jnp.mean(scaled * unit, axis=-1, keepdims=True)
    return inner * scale_inv


def fold(x):
    return jnp.sum(x.reshape(x.shape[0] // 8, 8, x.shape[1]), axis=0)


class Sizes:
    def __init__(self, tensor, dp, samples, lat, slots, width, hidden, inner):
        self.T, self.N, self.C = tensor, dp, dp // 2
        self.S, self.L, self.M, self.D = samples, lat, slots, width
        self.F, self.I = hidden, inner
        self.R = width // dp
        self.Lt, self.Mt = lat // tensor, slots // tensor
        self.Kt = self.Lt + self.Mt
        self.K = lat + slots
        self.H = inner // HEAD_DIM
        self.q = self.H * lat


def layer_kernel(
    z,
    counts,
    media,
    lat,
    cot,
    mgain,
    mshift,
    lgain,
    lshift,
    fgain,
    fshift,
    wqkv,
    wo,
    up,
    dn,
    new_lat,
    media_grad,
    lat_grad,
    g_qkv,
    g_o,
    g_up,
    g_dn,
    g_vec,
    wq_b,
    wo_b,
    up_b,
    dn_b,
    mbuf,
    mown,
    xn,
    kvown,
    ctx,
    latn,
    att,
    lse,
    qall,
    kvall,
    pall,
    dkv,
    res,
    hin,
    act,
    bgr,
    hg,
    hgr,
    fp,
    fpr,
    og,
    rgr,
    dob,
    dqb,
    dqr,
    st_up,
    st_dn,
    st_o,
    st_qkv,
    cr_up,
    cr_dn,
    cr_o,
    cr_qkv,
    xr_up,
    xr_dn,
    xr_o,
    xr_qkv,
    zr_o,
    zr_qkv,
    mg,
    mgl,
    acc,
    vst,
    vcr,
    vx,
    vz,
    msem,
    osem,
    zs,
    zr,
    xs,
    xr,
    cs,
    cr,
):
    T, N, C, S, L, M, D = z.T, z.N, z.C, z.S, z.L, z.M, z.D
    F, I, R, Lt, Mt, Kt, H = z.F, z.I, z.R, z.Lt, z.Mt, z.Kt, z.H
    scale_factor = HEAD_DIM ** (-0.5)
    t = lax.axis_index("tensor")
    d = lax.axis_index("dp")
    c = lax.div(d, 2)
    core = lax.rem(d, 2)
    other = 1 - core
    sib = d + 1 - 2 * core
    n = BLOCK // (2 * R)

    def z_dev(k):
        return (d, lax.rem(t + k, T))

    def x_chip(j):
        return lax.rem(c + j, C)

    def x_dev(j):
        return (2 * x_chip(j) + core, t)

    core_dev = (sib, t)

    def head(k):
        return lax.rem(t - k + T, T)

    def my_rows(k=0):
        return pl.ds(pl.multiple_of(lax.rem(t + k, T) * Lt, Lt), Lt)

    def remote(src, dst, send, recv, dev):
        return pltpu.make_async_remote_copy(
            src_ref=src, dst_ref=dst, send_sem=send, recv_sem=recv, device_id=dev, device_id_type=MESH
        )

    def over_chips(body):
        lax.fori_loop(1, C, lambda j, carry: (body(j), carry)[1], 0)

    def gather_z(i, src, buf):
        return [
            remote(src.at[c, core], buf.at[k, c, core], zs.at[i, k - 1], zr.at[i, k - 1], z_dev(k))
            for k in range(1, T)
        ]

    def gather_x(i, src, dst):
        def one(j):
            return remote(src, dst, xs.at[i, j - 1], xr.at[i, j - 1], x_dev(j))

        return one

    wo_z = gather_z(0, wo, wo_b)
    wq_z = gather_z(1, wqkv, wq_b)
    wo_x = gather_x(0, wo_b.at[pl.ds(1, T - 1), c, core], wo_b.at[pl.ds(1, T - 1), c, core])
    wq_x = gather_x(1, wq_b.at[pl.ds(1, T - 1), c, core], wq_b.at[pl.ds(1, T - 1), c, core])
    up_x = gather_x(2, up, up_b.at[c, core])
    dn_x = gather_x(3, dn, dn_b.at[c, core])

    def relay(i, ref):
        return remote(ref, ref, cs.at[i], cr.at[i], core_dev)

    wo_c = relay(0, wo_b.at[pl.ds(1, T - 1), :, core])
    wq_c = relay(1, wq_b.at[pl.ds(1, T - 1), :, core])
    up_c = relay(2, up_b.at[:, core])
    dn_c = relay(3, dn_b.at[:, core])

    n_tiles = S * T

    def tile_copy(i):
        slot = lax.rem(i, SLOTS_IN_FLIGHT)
        s, r = lax.div(i, T), lax.rem(i, T)
        return pltpu.make_async_copy(
            media.at[s, pl.ds(pl.multiple_of(r * Mt, Mt), Mt)], mbuf.at[slot], msem.at[slot]
        )

    own_copy = pltpu.make_async_copy(
        media.at[:, pl.ds(pl.multiple_of(t * Mt, Mt), Mt)], mown, msem.at[SLOTS_IN_FLIGHT]
    )
    for i in range(min(SLOTS_IN_FLIGHT, n_tiles)):
        tile_copy(i).start()
    own_copy.start()

    barrier = pltpu.get_barrier_semaphore()

    def greet(dev):
        pl.semaphore_signal(barrier, inc=1, device_id=dev, device_id_type=MESH)

    for k in range(1, T):
        greet(z_dev(k))
    over_chips(lambda j: greet(x_dev(j)))
    greet(core_dev)
    pl.semaphore_wait(barrier, T + C - 1)

    for copy in wo_z + wq_z:
        copy.start()
    over_chips(lambda j: up_x(j).start())
    over_chips(lambda j: dn_x(j).start())
    wo_b[0] = wo[...]
    wq_b[0] = wqkv[...]
    up_b[c, core] = up[...]
    dn_b[c, core] = dn[...]

    def lat_norm(b, carry):
        rows = pl.ds(pl.multiple_of(b * ROWS, ROWS), ROWS)
        unit, _ = unit_rows(lat[rows, :].astype(F32))
        latn[rows, :] = (unit * lgain[...] + lshift[...]).astype(BF16)
        return carry

    lax.fori_loop(0, S * L // ROWS, lat_norm, 0)
    own_w = wq_b[0].reshape(D, 3 * I)
    own_qkv = nn(latn[...], own_w).astype(BF16)
    qall[0] = own_qkv[:, :I]
    for s in range(S):
        kvown[s, pl.ds(M, L), :] = own_qkv[s * L : (s + 1) * L, I:]
        ctx[pl.ds(s * Kt + Mt, Lt), :] = latn[pl.ds(pl.multiple_of(s * L + t * Lt, Lt), Lt), :]

    def media_tile(i, carry):
        slot = lax.rem(i, SLOTS_IN_FLIGHT)
        s, r = lax.div(i, T), lax.rem(i, T)
        tile_copy(i).wait()

        def rows_norm(b, inner):
            rows = pl.ds(pl.multiple_of(b * ROWS, ROWS), ROWS)
            unit, _ = unit_rows(mbuf[slot, rows, :].astype(F32))
            xn[rows, :] = (unit * mgain[...] + mshift[...]).astype(BF16)
            return inner

        lax.fori_loop(0, Mt // ROWS, rows_norm, 0)

        @pl.when(i + SLOTS_IN_FLIGHT < n_tiles)
        def _():
            tile_copy(i + SLOTS_IN_FLIGHT).start()

        pair = nn(xn[...], wq_b[0].reshape(D, 3 * I)[:, I:])
        kvown[s, pl.ds(pl.multiple_of(r * Mt, Mt), Mt), :] = pair.astype(BF16)

        @pl.when(r == t)
        def _():
            ctx[pl.ds(pl.multiple_of(s * Kt, 16), Mt), :] = xn[...]

        @pl.when(i == n_tiles // 4)
        def _():
            for copy in wo_z:
                copy.wait_recv()
            over_chips(lambda j: wo_x(j).start())

        @pl.when(i == n_tiles // 2)
        def _():
            for copy in wq_z:
                copy.wait_recv()
            over_chips(lambda j: wq_x(j).start())

        return carry

    lax.fori_loop(0, n_tiles, media_tile, 0)

    lane_head = lax.broadcasted_iota(jnp.int32, (1, I), 1) // HEAD_DIM

    def spread(x):
        zero = jnp.zeros_like(x)
        return jnp.concatenate([jnp.where(lane_head == h, x, zero) for h in range(H)], axis=0)

    def gather_heads(x):
        out = x[:L]
        for h in range(1, H):
            out = jnp.where(lane_head == h, x[h * L : (h + 1) * L], out)
        return out

    def attend(s, carry):
        keys = kvown[s, :, pl.ds(0, I)]
        values = kvown[s, :, pl.ds(I, I)]
        queries = qall[0, pl.ds(pl.multiple_of(s * L, L), L), :]
        scores = nt(keys, spread(queries)) * scale_factor
        slot = lax.broadcasted_iota(jnp.int32, (z.K, 1), 0)
        valid = (slot < counts[s] * PATCH) | (slot >= M)
        scores = jnp.where(valid, scores, NEGATIVE)
        largest = jnp.max(scores, axis=0, keepdims=True)
        total = largest + jnp.log(jnp.sum(jnp.exp(scores - largest), axis=0, keepdims=True))
        probs = jnp.exp(scores - total).astype(BF16)
        att[0, s] = gather_heads(tn(probs, values)).astype(BF16)
        lse[0, pl.ds(s, 1), :] = total
        return carry

    lax.fori_loop(0, S, attend, 0)

    att_z = [remote(att.at[0], att.at[k], zs.at[2, k - 1], zr.at[2, k - 1], z_dev(k)) for k in range(1, T)]
    lse_z = [remote(lse.at[0], lse.at[k], zs.at[3, k - 1], zr.at[3, k - 1], z_dev(k)) for k in range(1, T)]
    for copy in att_z + lse_z:
        copy.start()

    over_chips(lambda j: wo_x(j).wait_recv())
    wo_c.start()
    over_chips(lambda j: up_x(j).wait_recv())
    up_c.start()
    over_chips(lambda j: dn_x(j).wait_recv())
    dn_c.start()

    wo_c.wait_recv()
    for copy in att_z:
        copy.wait_recv()

    def mat(ref, k, width):
        return ref[k].reshape(D, width)

    part = lat[...].astype(F32)
    for k in range(T):
        part = part + nt(att[k].reshape(S * L, I), mat(wo_b, k, I))
    res[...] = part

    def feed_norm(b, carry):
        rows = pl.ds(pl.multiple_of(b * ROWS, ROWS), ROWS)
        unit, _ = unit_rows(res[rows, :])
        hin[rows, :] = (unit * fgain[...] + fshift[...]).astype(BF16)
        return carry

    lax.fori_loop(0, S * L // ROWS, feed_norm, 0)

    up_c.wait_recv()
    dn_c.wait_recv()

    def feed(b, carry):
        cols = pl.ds(pl.multiple_of(b * BLOCK, BLOCK), BLOCK)
        before = nn(hin[...], up_b[:, :, :, cols].reshape(D, BLOCK))
        cdf = 0.5 * (1.0 + lax.erf(before * SQRT_HALF))
        act[:, cols] = (before * cdf).astype(BF16)
        slope = cdf + before * INV_ROOT_TWO_PI * jnp.exp(-0.5 * before * before)
        act_grad = nn(cot[...], dn_b[:, :, :, cols].reshape(D, BLOCK)).astype(BF16)
        bgr[:, cols] = (act_grad.astype(F32) * slope).astype(BF16)
        return carry

    lax.fori_loop(0, F // BLOCK, feed, 0)

    def back_to_width(left, weight, out):
        def one(b, carry):
            cols = pl.ds(pl.multiple_of(b * BLOCK, BLOCK), BLOCK)
            block = nt(left[...], weight[pl.ds(b * n, n)].reshape(BLOCK, F))
            out[:, :, cols] = block.astype(BF16).reshape(S, L, BLOCK)
            return carry

        lax.fori_loop(0, D // BLOCK, one, 0)

    back_to_width(bgr, up_b, hg)
    hg_z = [
        remote(hg.at[:, my_rows(k)], hgr.at[k - 1], zs.at[4, k - 1], zr.at[4, k - 1], z_dev(k)) for k in range(1, T)
    ]
    for copy in hg_z:
        copy.start()
    back_to_width(act, dn_b, fp)
    fp_z = [
        remote(fp.at[:, my_rows(k)], fpr.at[k - 1], zs.at[5, k - 1], zr.at[5, k - 1], z_dev(k)) for k in range(1, T)
    ]
    for copy in fp_z:
        copy.start()

    def feed_weights(left, right, out):
        def one(b, carry):
            cols = pl.ds(pl.multiple_of(b * BLOCK, BLOCK), BLOCK)
            block = tn(left[:, cols], right[...]).astype(BF16)
            out[pl.ds(b * n, n)] = block.reshape(n, 2, R, F)
            return carry

        lax.fori_loop(0, D // BLOCK, one, 0)

    def to_core(i, src, dst):
        return remote(src, dst, cs.at[i], cr.at[i], core_dev)

    feed_weights(hin, bgr, st_up)
    st_up_c = to_core(4, st_up.at[:, other], cr_up)
    st_up_c.start()
    feed_weights(cot, act, st_dn)
    st_dn_c = to_core(5, st_dn.at[:, other], cr_dn)
    st_dn_c.start()

    over_chips(lambda j: wq_x(j).wait_recv())
    wq_c.start()

    own_copy.wait()
    wq_c.wait_recv()

    def all_queries(k, carry):
        qall[k] = nn(latn[...], wq_b[k, :, :, :, pl.ds(0, I)].reshape(D, I)).astype(BF16)
        return carry

    lax.fori_loop(1, T, all_queries, 0)

    def all_pairs(i, carry):
        k, s = lax.div(i, S), lax.rem(i, S)
        rows = pl.ds(pl.multiple_of(s * Kt, 16), Kt)
        pair = nn(ctx[rows, :], wq_b[k, :, :, :, pl.ds(I, 2 * I)].reshape(D, 2 * I))
        kvall[k, rows, :] = pair.astype(BF16)
        return carry

    lax.fori_loop(0, T * S, all_pairs, 0)
    for copy in lse_z:
        copy.wait_recv()
    slot_of = lax.broadcasted_iota(jnp.int32, (Kt, 1), 0)

    def probabilities(i, carry):
        k, s = lax.div(i, S), lax.rem(i, S)
        rows = pl.ds(pl.multiple_of(s * Kt, 16), Kt)
        queries = qall[k, pl.ds(pl.multiple_of(s * L, L), L), :]
        scores = nt(kvall[k, rows, pl.ds(0, I)], spread(queries)) * scale_factor
        valid = (slot_of + t * Mt < counts[s] * PATCH) | (slot_of >= Mt)
        scores = jnp.where(valid, scores, NEGATIVE)
        pall[i] = jnp.exp(scores - lse[k, pl.ds(s, 1), :])
        return carry

    lax.fori_loop(0, T * S, probabilities, 0)

    for copy in hg_z:
        copy.wait_recv()
    feed_gain_part = jnp.zeros((1, D), F32)
    feed_shift_part = jnp.zeros((1, D), F32)
    for s in range(S):
        own = pl.ds(pl.multiple_of(s * L + t * Lt, Lt), Lt)
        unit, scale_inv = unit_rows(res[own, :])
        upstream = hg[s, my_rows(), :].astype(F32)
        for k in range(1, T):
            upstream = upstream + hgr[k - 1, s].astype(F32)
        back = cot[own, :].astype(F32) + norm_back(unit, scale_inv, fgain[...], upstream)
        feed_gain_part = feed_gain_part + jnp.sum(upstream * unit, axis=0, keepdims=True)
        feed_shift_part = feed_shift_part + jnp.sum(upstream, axis=0, keepdims=True)
        rgr[pl.ds(s * Lt, Lt), :] = back
        og[pl.ds(s * Lt, Lt), :] = back.astype(BF16)
    for k in range(T):
        grads = nn(og[...], mat(wo_b, k, I)).astype(BF16)
        dob[head(k), :, my_rows(), :] = grads.reshape(S, Lt, I)
    do_z = [
        remote(
            dob.at[:, :, my_rows(), :], dob.at[:, :, my_rows(), :], zs.at[6, k - 1], zr.at[6, k - 1], z_dev(k)
        )
        for k in range(1, T)
    ]
    do_in = [
        remote(
            dob.at[:, :, my_rows(T - k), :],
            dob.at[:, :, my_rows(T - k), :],
            zs.at[6, k - 1],
            zr.at[6, k - 1],
            z_dev(k),
        )
        for k in range(1, T)
    ]
    for copy in do_z:
        copy.start()

    for k in range(T):
        mine = att[k, :, my_rows(), :].reshape(S * Lt, I)

        def out_weights(b, carry, k=k, mine=mine):
            cols = pl.ds(pl.multiple_of(b * BLOCK, BLOCK), BLOCK)
            block = tn(og[:, cols], mine).astype(BF16)
            st_o[k, pl.ds(b * n, n)] = block.reshape(n, 2, R, I)
            return carry

        lax.fori_loop(0, D // BLOCK, out_weights, 0)
    st_o_c = to_core(6, st_o.at[:, :, other], cr_o)
    st_o_c.start()

    def plane_feed(i, arrive, st, came, land):
        arrive.wait_recv()

        def add(chip):
            st[chip, core] = (st[chip, core].astype(F32) + came[chip].astype(F32)).astype(BF16)

        def copy(j):
            return remote(st.at[x_chip(j), core], land.at[j - 1], xs.at[i, j - 1], xr.at[i, j - 1], x_dev(j))

        def one(j):
            add(x_chip(j))
            copy(j).start()

        over_chips(one)
        add(c)
        return copy

    def plane_heads(i, arrive, st, came, land):
        arrive.wait_recv()

        def add(chip):
            for k in range(T):
                st[k, chip, core] = (st[k, chip, core].astype(F32) + came[k, chip].astype(F32)).astype(BF16)

        def copy(j):
            return remote(st.at[:, x_chip(j), core], land.at[j - 1], xs.at[i, j - 1], xr.at[i, j - 1], x_dev(j))

        def one(j):
            add(x_chip(j))
            copy(j).start()

        over_chips(one)
        add(c)
        return copy

    x_up = plane_feed(4, st_up_c, st_up, cr_up, xr_up)
    x_dn = plane_feed(5, st_dn_c, st_dn, cr_dn, xr_dn)

    for copy in do_in:
        copy.wait_recv()

    def attend_back(i, carry):
        k, s = lax.div(i, S), lax.rem(i, S)
        rows = pl.ds(pl.multiple_of(s * Kt, 16), Kt)
        lanes = pl.multiple_of(k * 2 * I, 2 * I)
        keys = kvall[k, rows, pl.ds(0, I)]
        values = kvall[k, rows, pl.ds(I, I)]
        queries = spread(qall[k, pl.ds(pl.multiple_of(s * L, L), L), :])
        grads = spread(dob[head(k), s])
        outs = spread(att[k, s])
        product = grads.astype(F32) * outs.astype(F32)
        inner = lax.dot_general(
            jnp.ones((8, I), F32),
            product,
            (((1,), (1,)), ((), ())),
            preferred_element_type=F32,
            precision=lax.Precision.HIGHEST,
        )[:1]
        probs = pall[i]
        score_grad = (probs * (nt(values, grads) - inner)).astype(BF16)
        dkv[rows, pl.ds(lanes, I)] = (nn(score_grad, queries) * scale_factor).astype(BF16)
        dkv[rows, pl.ds(lanes + I, I)] = nn(probs.astype(BF16), grads).astype(BF16)
        dqb[head(k), s] = (gather_heads(tn(score_grad, keys)) * scale_factor).astype(BF16)
        return carry

    lax.fori_loop(0, T * S, attend_back, 0)
    dq_z = [
        remote(
            dqb.at[:, :, my_rows(k), :], dqr.at[k - 1], zs.at[7, k - 1], zr.at[7, k - 1], z_dev(k)
        )
        for k in range(1, T)
    ]
    for copy in dq_z:
        copy.start()

    def pair_weights(b, carry):
        cols = pl.ds(pl.multiple_of(b * BLOCK, BLOCK), BLOCK)
        block = tn(ctx[:, cols], dkv[...]).astype(BF16)
        for k in range(T):
            st_qkv[k, pl.ds(b * n, n), :, :, pl.ds(I, 2 * I)] = block[:, k * 2 * I : (k + 1) * 2 * I].reshape(
                n, 2, R, 2 * I
            )
        return carry

    lax.fori_loop(0, D // BLOCK, pair_weights, 0)
    for k in range(T):
        mine = dqb[head(k)].reshape(S * L, I)

        def query_weights(b, carry, k=k, mine=mine):
            cols = pl.ds(pl.multiple_of(b * BLOCK, BLOCK), BLOCK)
            block = tn(latn[:, cols], mine).astype(BF16)
            st_qkv[k, pl.ds(b * n, n), :, :, pl.ds(0, I)] = block.reshape(n, 2, R, I)
            return carry

        lax.fori_loop(0, D // BLOCK, query_weights, 0)
    st_qkv_c = to_core(7, st_qkv.at[:, :, other], cr_qkv)
    st_qkv_c.start()
    x_o = plane_heads(6, st_o_c, st_o, cr_o, xr_o)
    x_qkv = plane_heads(7, st_qkv_c, st_qkv, cr_qkv, xr_qkv)

    for copy in fp_z:
        copy.wait_recv()
    for s in range(S):
        own = pl.ds(pl.multiple_of(s * L + t * Lt, Lt), Lt)
        total = fp[s, my_rows(), :].astype(F32)
        for k in range(1, T):
            total = total + fpr[k - 1, s].astype(F32)
        new_lat[s, my_rows(), :] = (res[own, :] + total).astype(BF16)

    def share_rows(i, ref):
        out = [
            remote(ref.at[:, my_rows(), :], ref.at[:, my_rows(), :], zs.at[i, k - 1], zr.at[i, k - 1], z_dev(k))
            for k in range(1, T)
        ]
        came = [
            remote(
                ref.at[:, my_rows(T - k), :],
                ref.at[:, my_rows(T - k), :],
                zs.at[i, k - 1],
                zr.at[i, k - 1],
                z_dev(k),
            )
            for k in range(1, T)
        ]
        return out, came

    nl_z, nl_in = share_rows(8, new_lat)
    for copy in nl_z:
        copy.start()

    acc[...] = jnp.zeros_like(acc)

    def media_back(s, carry):
        base = pl.multiple_of(s * Kt, 16)

        def width_block(b, inner):
            cols = pl.ds(pl.multiple_of(b * BLOCK, BLOCK), BLOCK)
            weights = jnp.concatenate(
                [wq_b[k, pl.ds(b * n, n), :, :, pl.ds(I, 2 * I)].reshape(BLOCK, 2 * I) for k in range(T)], axis=1
            )
            mg[:, cols] = nt(dkv[pl.ds(base, Kt), :], weights)
            return inner

        lax.fori_loop(0, D // BLOCK, width_block, 0)

        def rows_back(b, inner):
            rows = pl.ds(pl.multiple_of(b * ROWS, ROWS), ROWS)
            unit, scale_inv = unit_rows(mown[s, rows, :].astype(F32))
            upstream = mg[rows, :]
            mown[s, rows, :] = norm_back(unit, scale_inv, mgain[...], upstream).astype(BF16)
            acc[0] += fold(upstream * unit)
            acc[1] += fold(upstream)
            return inner

        lax.fori_loop(0, Mt // ROWS, rows_back, 0)
        mgl[pl.ds(pl.multiple_of(s * Lt, Lt), Lt), :] = mg[pl.ds(Mt, Lt), :]
        pltpu.make_async_copy(mown.at[s], media_grad.at[s], osem.at[s]).start()
        return carry

    lax.fori_loop(0, S, media_back, 0)

    for copy in dq_z:
        copy.wait_recv()
    upstream_all = mgl[...]
    for k in range(T):
        total = dqb[head(k), :, my_rows(), :].astype(F32)
        for m in range(1, T):
            total = total + dqr[m - 1, head(k)].astype(F32)
        weights = wq_b[k, :, :, :, pl.ds(0, I)].reshape(D, I)
        upstream_all = upstream_all + nt(total.astype(BF16).reshape(S * Lt, I), weights)
    mgl[...] = upstream_all
    lat_gain_part = jnp.zeros((1, D), F32)
    lat_shift_part = jnp.zeros((1, D), F32)
    for s in range(S):
        own = pl.ds(pl.multiple_of(s * L + t * Lt, Lt), Lt)
        unit, scale_inv = unit_rows(lat[own, :].astype(F32))
        upstream = mgl[pl.ds(s * Lt, Lt), :]
        back = rgr[pl.ds(s * Lt, Lt), :] + norm_back(unit, scale_inv, lgain[...], upstream)
        lat_grad[s, my_rows(), :] = back.astype(BF16)
        lat_gain_part = lat_gain_part + jnp.sum(upstream * unit, axis=0, keepdims=True)
        lat_shift_part = lat_shift_part + jnp.sum(upstream, axis=0, keepdims=True)
    lg_z, lg_in = share_rows(9, lat_grad)
    for copy in lg_z:
        copy.start()

    vst[...] = jnp.concatenate(
        [
            jnp.sum(acc[0], axis=0, keepdims=True),
            jnp.sum(acc[1], axis=0, keepdims=True),
            lat_gain_part,
            lat_shift_part,
            feed_gain_part,
            feed_shift_part,
            jnp.zeros((2, D), F32),
        ],
        axis=0,
    )
    v_c = to_core(8, vst, vcr)
    v_c.start()
    v_c.wait_recv()
    vx[c] = vst[...] + vcr[...]

    def v_x(j):
        return remote(vx.at[c], vx.at[c], xs.at[8, j - 1], xr.at[8, j - 1], x_dev(j))

    def v_x_in(j):
        chip = lax.rem(c - j + C, C)
        return remote(vx.at[chip], vx.at[chip], xs.at[8, j - 1], xr.at[8, j - 1], x_dev(j))

    over_chips(lambda j: v_x(j).start())

    def sum_heads(x_copy, st, land):
        over_chips(lambda j: x_copy(j).wait_recv())
        for k in range(T):
            total = lax.fori_loop(
                1, C, lambda j, value, k=k: value + land[j - 1, k].astype(F32), st[k, c, core].astype(F32)
            )
            land[0, k] = total.astype(BF16)

    def z_sum(i, land, came):
        return [
            remote(land.at[0, k], came.at[T - k - 1], zs.at[i, k - 1], zr.at[i, T - k - 1], (d, head(k)))
            for k in range(1, T)
        ]

    sum_heads(x_o, st_o, xr_o)
    o_z = z_sum(10, xr_o, zr_o)
    for copy in o_z:
        copy.start()
    sum_heads(x_qkv, st_qkv, xr_qkv)
    q_z = z_sum(11, xr_qkv, zr_qkv)
    for copy in q_z:
        copy.start()

    over_chips(lambda j: v_x_in(j).wait_recv())
    vz[t] = lax.fori_loop(1, C, lambda j, value: value + vx[j], vx[0])
    v_z = [remote(vz.at[t], vz.at[t], zs.at[12, k - 1], zr.at[12, k - 1], z_dev(k)) for k in range(1, T)]
    v_z_in = [
        remote(vz.at[head(k)], vz.at[head(k)], zs.at[12, k - 1], zr.at[12, k - 1], z_dev(k)) for k in range(1, T)
    ]
    for copy in v_z:
        copy.start()

    def sum_feed(x_copy, st, land, out):
        over_chips(lambda j: x_copy(j).wait_recv())
        out[...] = lax.fori_loop(
            1, C, lambda j, value: value + land[j - 1].astype(F32), st[c, core].astype(F32)
        )

    sum_feed(x_up, st_up, xr_up, g_up)
    sum_feed(x_dn, st_dn, xr_dn, g_dn)

    for copy in v_z_in:
        copy.wait_recv()
    g_vec[...] = lax.fori_loop(1, T, lambda k, value: value + vz[k], vz[0])
    for copy in o_z:
        copy.wait_recv()
    total = xr_o[0, 0].astype(F32)
    for k in range(1, T):
        total = total + zr_o[k - 1].astype(F32)
    g_o[...] = total
    for copy in q_z:
        copy.wait_recv()
    total = xr_qkv[0, 0].astype(F32)
    for k in range(1, T):
        total = total + zr_qkv[k - 1].astype(F32)
    g_qkv[...] = total

    for copy in nl_in + lg_in:
        copy.wait_recv()
    for copy in wo_z + wq_z + att_z + lse_z + hg_z + fp_z + do_z + dq_z + nl_z + lg_z + o_z + q_z + v_z:
        copy.wait_send()
    for one in (wo_x, wq_x, up_x, dn_x, x_up, x_dn, x_o, x_qkv, v_x):
        over_chips(lambda j, one=one: one(j).wait_send())
    for copy in (wo_c, wq_c, up_c, dn_c, st_up_c, st_dn_c, st_o_c, st_qkv_c, v_c):
        copy.wait_send()
    for s in range(S):
        pltpu.make_async_copy(mown.at[s], media_grad.at[s], osem.at[s]).wait()


def solution(mesh):
    T, N = mesh.shape["tensor"], mesh.shape["dp"]

    def on_device(
        media_tokens,
        latents,
        image_counts,
        media_gain,
        media_shift,
        latent_gain,
        latent_shift,
        feed_gain,
        feed_shift,
        query_weight,
        key_weight,
        value_weight,
        output_weight,
        up_weight,
        down_weight,
        cotangent,
    ):
        samples, slots, width = media_tokens.shape
        z = Sizes(T, N, samples, latents.shape[1], slots, width, up_weight.shape[1], query_weight.shape[1])
        S, L, D, F, I, R, C = z.S, z.L, z.D, z.F, z.I, z.R, z.C
        row = lambda v: v.reshape(1, D)
        wqkv = jnp.concatenate([query_weight, key_weight, value_weight], axis=1).reshape(C, 2, R, 3 * I)
        wo = output_weight.T.reshape(C, 2, R, I)
        vmem = pl.BlockSpec(memory_space=pltpu.VMEM)
        hbm = pl.BlockSpec(memory_space=pl.ANY)
        V = pltpu.VMEM
        heads_rows = max(z.K, 1)
        scratch = [
            V((T, C, 2, R, 3 * I), BF16),
            V((T, C, 2, R, I), BF16),
            V((C, 2, R, F), BF16),
            V((C, 2, R, F), BF16),
            V((SLOTS_IN_FLIGHT, z.Mt, D), BF16),
            V((S, z.Mt, D), BF16),
            V((z.Mt, D), BF16),
            V((S, heads_rows, 2 * I), BF16),
            V((S * z.Kt, D), BF16),
            V((S * L, D), BF16),
            V((T, S, L, I), BF16),
            V((T, max(S, 8), z.q), F32),
            V((T, S * L, I), BF16),
            V((T, S * z.Kt, 2 * I), BF16),
            V((T * S, z.Kt, z.q), F32),
            V((S * z.Kt, T * 2 * I), BF16),
            V((S * L, D), F32),
            V((S * L, D), BF16),
            V((S * L, F), BF16),
            V((S * L, F), BF16),
            V((S, L, D), BF16),
            V((T - 1, S, z.Lt, D), BF16),
            V((S, L, D), BF16),
            V((T - 1, S, z.Lt, D), BF16),
            V((S * z.Lt, D), BF16),
            V((S * z.Lt, D), F32),
            V((T, S, L, I), BF16),
            V((T, S, L, I), BF16),
            V((T - 1, T, S, z.Lt, I), BF16),
            V((C, 2, R, F), BF16),
            V((C, 2, R, F), BF16),
            V((T, C, 2, R, I), BF16),
            V((T, C, 2, R, 3 * I), BF16),
            V((C, R, F), BF16),
            V((C, R, F), BF16),
            V((T, C, R, I), BF16),
            V((T, C, R, 3 * I), BF16),
            V((max(C - 1, 1), R, F), BF16),
            V((max(C - 1, 1), R, F), BF16),
            V((max(C - 1, 1), T, R, I), BF16),
            V((max(C - 1, 1), T, R, 3 * I), BF16),
            V((T - 1, R, I), BF16),
            V((T - 1, R, 3 * I), BF16),
            V((z.Kt, D), F32),
            V((S * z.Lt, D), F32),
            V((2, 8, D), F32),
            V((8, D), F32),
            V((8, D), F32),
            V((C, 8, D), F32),
            V((T, 8, D), F32),
            pltpu.SemaphoreType.DMA((SLOTS_IN_FLIGHT + 1,)),
            pltpu.SemaphoreType.DMA((S,)),
            pltpu.SemaphoreType.DMA((13, T - 1)),
            pltpu.SemaphoreType.DMA((13, T - 1)),
            pltpu.SemaphoreType.DMA((9, max(C - 1, 1))),
            pltpu.SemaphoreType.DMA((9, max(C - 1, 1))),
            pltpu.SemaphoreType.DMA((9,)),
            pltpu.SemaphoreType.DMA((9,)),
        ]
        shape = jax.ShapeDtypeStruct
        outs = pl.pallas_call(
            functools.partial(layer_kernel, z),
            out_shape=[
                shape((S, L, D), BF16),
                shape((S, z.Mt, D), BF16),
                shape((S, L, D), BF16),
                shape((R, 3 * I), F32),
                shape((R, I), F32),
                shape((R, F), F32),
                shape((R, F), F32),
                shape((8, D), F32),
            ],
            in_specs=[pl.BlockSpec(memory_space=pltpu.SMEM), hbm] + [vmem] * 12,
            out_specs=[vmem, hbm] + [vmem] * 6,
            scratch_shapes=scratch,
            compiler_params=pltpu.CompilerParams(
                collective_id=0, has_side_effects=True, vmem_limit_bytes=60 * 1024 * 1024
            ),
            name="resampler_layer",
        )(
            image_counts,
            media_tokens,
            latents.reshape(S * L, D),
            cotangent.reshape(S * L, D),
            row(media_gain),
            row(media_shift),
            row(latent_gain),
            row(latent_shift),
            row(feed_gain),
            row(feed_shift),
            wqkv,
            wo,
            up_weight,
            down_weight.T,
        )
        new_latents, media_grad, latent_grad, g_qkv, g_o, g_up, g_dn, g_vec = outs
        own = lax.dynamic_slice_in_dim(g_vec, lax.axis_index("dp") * R, R, 1)
        return (
            new_latents,
            media_grad,
            latent_grad,
            g_qkv[:, :I],
            g_qkv[:, I : 2 * I],
            g_qkv[:, 2 * I :],
            g_o.T,
            g_up,
            g_dn.T,
            g_vec[0],
            g_vec[1],
            own[2],
            own[3],
            own[4],
            own[5],
        )

    placed = (
        P("dp", None, None),
        P("dp", None, None),
        P("dp"),
        P(),
        P(),
        P(),
        P(),
        P(),
        P(),
        P(None, "tensor"),
        P(None, "tensor"),
        P(None, "tensor"),
        P("tensor", None),
        P("dp", "tensor"),
        P("tensor", "dp"),
        P("dp", None, None),
    )
    return jax.shard_map(
        on_device,
        mesh=mesh,
        in_specs=placed,
        out_specs=(
            P("dp", None, None),
            P("dp", "tensor", None),
            P("dp", None, None),
            P("dp", "tensor"),
            P("dp", "tensor"),
            P("dp", "tensor"),
            P("tensor", "dp"),
            P("dp", "tensor"),
            P("tensor", "dp"),
            P(),
            P(),
            P("dp"),
            P("dp"),
            P("dp"),
            P("dp"),
        ),
        check_vma=False,
    )
```

```python
import functools

import jax
import jax.numpy as jnp
from jax import lax
from jax.experimental import pallas as pl
from jax.experimental.pallas import tpu as pltpu
from jax.sharding import PartitionSpec as P

HEAD_DIM = 64
PATCH = 256
EPSILON = 1e-05
NEGATIVE = -1e30
SQRT_HALF = 0.7071067811865476
INV_ROOT_TWO_PI = 0.3989422804014327
F32 = jnp.float32
BF16 = jnp.bfloat16
MESH = pl.DeviceIdType.MESH
BLOCK = 256
ROWS = 32
SLOTS_IN_FLIGHT = 3


def nn(left, right):
    return lax.dot_general(left, right, (((1,), (0,)), ((), ())), preferred_element_type=F32)


def nt(left, right):
    return lax.dot_general(left, right, (((1,), (1,)), ((), ())), preferred_element_type=F32)


def tn(left, right):
    return lax.dot_general(left, right, (((0,), (0,)), ((), ())), preferred_element_type=F32)


def unit_rows(x):
    centre = x - jnp.mean(x, axis=-1, keepdims=True)
    scale_inv = lax.rsqrt(jnp.mean(centre * centre, axis=-1, keepdims=True) + EPSILON)
    return centre * scale_inv, scale_inv


def norm_back(unit, scale_inv, gain, upstream):
    scaled = upstream * gain
    inner = scaled - jnp.mean(scaled, axis=-1, keepdims=True)
    inner = inner - unit * jnp.mean(scaled * unit, axis=-1, keepdims=True)
    return inner * scale_inv


def fold(x):
    return jnp.sum(x.reshape(x.shape[0] // 8, 8, x.shape[1]), axis=0)


class Sizes:
    def __init__(self, tensor, dp, samples, lat, slots, width, hidden, inner):
        self.T, self.N, self.C = tensor, dp, dp // 2
        self.S, self.L, self.M, self.D = samples, lat, slots, width
        self.F, self.I = hidden, inner
        self.R = width // dp
        self.Lt, self.Mt = lat // tensor, slots // tensor
        self.Kt = self.Lt + self.Mt
        self.K = lat + slots
        self.H = inner // HEAD_DIM
        self.q = self.H * lat
        self.G = min(2, tensor)


def layer_kernel(
    z,
    counts,
    media,
    lat,
    cot,
    mgain,
    mshift,
    lgain,
    lshift,
    fgain,
    fshift,
    wq,
    wk,
    wv,
    wo,
    up,
    dn,
    new_lat,
    media_grad,
    lat_grad,
    g_qkv,
    g_o,
    g_up,
    g_dn,
    g_vec,
    wq_b,
    wo_b,
    up_b,
    dn_b,
    mbuf,
    mown,
    xn,
    ctx,
    latn,
    att,
    lse,
    qall,
    kall,
    vall,
    pall,
    pairs,
    res,
    hin,
    act,
    bgr,
    hg,
    hgr,
    fp,
    fpr,
    og,
    rgr,
    dob,
    dqb,
    dqr,
    st_up,
    st_dn,
    st_o,
    st_qkv,
    cr_up,
    cr_dn,
    cr_o,
    cr_qkv,
    xr_up,
    xr_dn,
    xr_o,
    xr_qkv,
    zr_o,
    zr_qkv,
    mgl,
    acc,
    vst,
    vcr,
    vx,
    vz,
    msem,
    osem,
    zs,
    zr,
    xs,
    xr,
    cs,
    cr,
):
    T, N, C, S, L, M, D = z.T, z.N, z.C, z.S, z.L, z.M, z.D
    F, I, R, Lt, Mt, Kt, G = z.F, z.I, z.R, z.Lt, z.Mt, z.Kt, z.G
    GI = G * I
    scale_factor = HEAD_DIM ** (-0.5)
    t = lax.axis_index("tensor")
    d = lax.axis_index("dp")
    c = lax.div(d, 2)
    core = lax.rem(d, 2)
    other = 1 - core
    sib = d + 1 - 2 * core
    n = BLOCK // (2 * R)

    def z_dev(k):
        return (d, lax.rem(t + k, T))

    def x_chip(j):
        return lax.rem(c + j, C)

    def x_dev(j):
        return (2 * x_chip(j) + core, t)

    core_dev = (sib, t)

    def head(k):
        return lax.rem(t - k + T, T)

    def my_rows(k=0):
        return pl.ds(pl.multiple_of(lax.rem(t + k, T) * Lt, Lt), Lt)

    def remote(src, dst, send, recv, dev):
        return pltpu.make_async_remote_copy(
            src_ref=src, dst_ref=dst, send_sem=send, recv_sem=recv, device_id=dev, device_id_type=MESH
        )

    def over_chips(body):
        lax.fori_loop(1, C, lambda j, carry: (body(j), carry)[1], 0)

    def gather_z(i, buf):
        return [
            remote(buf.at[0, c, core], buf.at[k, c, core], zs.at[i, k - 1], zr.at[i, k - 1], z_dev(k))
            for k in range(1, T)
        ]

    def gather_x(i, src, dst):
        def one(j):
            return remote(src, dst, xs.at[i, j - 1], xr.at[i, j - 1], x_dev(j))

        return one

    wo_z = gather_z(0, wo_b)
    wq_z = gather_z(1, wq_b)
    wo_x = gather_x(0, wo_b.at[pl.ds(1, T - 1), c, core], wo_b.at[pl.ds(1, T - 1), c, core])
    wq_x = gather_x(1, wq_b.at[pl.ds(1, T - 1), c, core], wq_b.at[pl.ds(1, T - 1), c, core])
    up_x = gather_x(2, up, up_b.at[c, core])
    dn_x = gather_x(3, dn_b.at[c, core], dn_b.at[c, core])

    def relay(i, ref):
        return remote(ref, ref, cs.at[i], cr.at[i], core_dev)

    wo_c = relay(0, wo_b.at[pl.ds(1, T - 1), :, core])
    wq_c = relay(1, wq_b.at[pl.ds(1, T - 1), :, core])
    up_c = relay(2, up_b.at[:, core])
    dn_c = relay(3, dn_b.at[:, core])

    n_tiles = S * T

    def tile_copy(i):
        slot = lax.rem(i, SLOTS_IN_FLIGHT)
        s, r = lax.div(i, T), lax.rem(i, T)
        return pltpu.make_async_copy(
            media.at[s, pl.ds(pl.multiple_of(r * Mt, Mt), Mt)], mbuf.at[slot], msem.at[slot]
        )

    own_copy = pltpu.make_async_copy(
        media.at[:, pl.ds(pl.multiple_of(t * Mt, Mt), Mt)], mown, msem.at[SLOTS_IN_FLIGHT]
    )
    for i in range(min(SLOTS_IN_FLIGHT, n_tiles)):
        tile_copy(i).start()
    own_copy.start()

    wo_b[0] = wo[...].T.reshape(C, 2, R, I)
    for m, weight in enumerate((wq, wk, wv)):
        wq_b[0, :, :, :, pl.ds(m * I, I)] = weight[...].reshape(C, 2, R, I)
    up_b[c, core] = up[...]
    dn_b[c, core] = dn[...].T
    barrier = pltpu.get_barrier_semaphore()

    def greet(dev):
        pl.semaphore_signal(barrier, inc=1, device_id=dev, device_id_type=MESH)

    for k in range(1, T):
        greet(z_dev(k))
    over_chips(lambda j: greet(x_dev(j)))
    greet(core_dev)
    pl.semaphore_wait(barrier, T + C - 1)

    for copy in wo_z + wq_z:
        copy.start()
    over_chips(lambda j: up_x(j).start())
    over_chips(lambda j: dn_x(j).start())

    for b in range(S * L // ROWS):
        rows = pl.ds(b * ROWS, ROWS)
        unit, _ = unit_rows(lat[rows, :].astype(F32))
        latn[rows, :] = (unit * lgain[...] + lshift[...]).astype(BF16)
    own_qkv = nn(latn[...], wq_b[0].reshape(D, 3 * I)).astype(BF16)
    qall[:, pl.ds(0, I)] = own_qkv[:, :I]
    for s in range(S):
        pairs[pl.ds(M, L), pl.ds(s * 2 * I, 2 * I)] = own_qkv[s * L : (s + 1) * L, I:]
        ctx[pl.ds(s * Kt + Mt, Lt), :] = latn[pl.ds(pl.multiple_of(s * L + t * Lt, Lt), Lt), :]

    def tile_norm(i, half):
        slot = lax.rem(i, SLOTS_IN_FLIGHT)
        for b in range(Mt // ROWS):
            rows = pl.ds(b * ROWS, ROWS)
            unit, _ = unit_rows(mbuf[slot, rows, :].astype(F32))
            xn[half, rows, :] = (unit * mgain[...] + mshift[...]).astype(BF16)

    def tile_pair(i, half):
        s, r = lax.div(i, T), lax.rem(i, T)
        pair = nn(xn[half], wq_b[0, :, :, :, pl.ds(I, 2 * I)].reshape(D, 2 * I))
        lanes = pl.ds(pl.multiple_of(s * 2 * I, 2 * I), 2 * I)
        pairs[pl.ds(pl.multiple_of(r * Mt, Mt), Mt), lanes] = pair.astype(BF16)

    def tile_keep(i, half):
        s, r = lax.div(i, T), lax.rem(i, T)

        @pl.when(r == t)
        def _():
            ctx[pl.ds(pl.multiple_of(s * Kt, 16), Mt), :] = xn[half]

    def tile_next(i):
        @pl.when(i + SLOTS_IN_FLIGHT < n_tiles)
        def _():
            tile_copy(i + SLOTS_IN_FLIGHT).start()

    tile_copy(0).wait()
    tile_norm(0, 0)
    tile_next(0)

    def two_tiles(j, carry):
        i = 2 * j
        tile_copy(i + 1).wait()

        @pl.when(i + 2 < n_tiles)
        def _():
            tile_copy(i + 2).wait()

        tile_keep(i, 0)
        tile_pair(i, 0)
        tile_norm(i + 1, 1)
        tile_keep(i + 1, 1)
        tile_pair(i + 1, 1)
        tile_norm(lax.rem(i + 2, n_tiles), 0)
        tile_next(i + 1)
        tile_next(i + 2)

        @pl.when(j == n_tiles // 8)
        def _():
            for copy in wo_z:
                copy.wait_recv()
            over_chips(lambda j: wo_x(j).start())

        @pl.when(j == n_tiles // 4)
        def _():
            for copy in wq_z:
                copy.wait_recv()
            over_chips(lambda j: wq_x(j).start())

        return carry

    lax.fori_loop(0, n_tiles // 2, two_tiles, 0)

    def spread(x):
        lane_head = lax.broadcasted_iota(jnp.int32, (1, x.shape[1]), 1) // HEAD_DIM
        zero = jnp.zeros_like(x)
        return jnp.concatenate(
            [jnp.where(lane_head == h, x, zero) for h in range(x.shape[1] // HEAD_DIM)], axis=0
        )

    def gather_heads(x):
        lane_head = lax.broadcasted_iota(jnp.int32, (1, x.shape[1]), 1) // HEAD_DIM
        out = x[:L]
        for h in range(1, x.shape[1] // HEAD_DIM):
            out = jnp.where(lane_head == h, x[h * L : (h + 1) * L], out)
        return out

    for s in range(S):
        keys = pairs[pl.ds(0, z.K), pl.ds(s * 2 * I, I)]
        values = pairs[pl.ds(0, z.K), pl.ds(s * 2 * I + I, I)]
        scores = nt(keys, spread(qall[pl.ds(s * L, L), pl.ds(0, I)])) * scale_factor
        slot = lax.broadcasted_iota(jnp.int32, (z.K, 1), 0)
        valid = (slot < counts[s] * PATCH) | (slot >= M)
        scores = jnp.where(valid, scores, NEGATIVE)
        largest = jnp.max(scores, axis=0, keepdims=True)
        total = largest + jnp.log(jnp.sum(jnp.exp(scores - largest), axis=0, keepdims=True))
        probs = jnp.exp(scores - total).astype(BF16)
        att[0, s] = gather_heads(tn(probs, values)).astype(BF16)
        lse[0, pl.ds(s, 1), :] = total

    att_z = [remote(att.at[0], att.at[k], zs.at[2, k - 1], zr.at[2, k - 1], z_dev(k)) for k in range(1, T)]
    lse_z = [remote(lse.at[0], lse.at[k], zs.at[3, k - 1], zr.at[3, k - 1], z_dev(k)) for k in range(1, T)]
    for copy in att_z + lse_z:
        copy.start()

    over_chips(lambda j: wo_x(j).wait_recv())
    wo_c.start()
    over_chips(lambda j: up_x(j).wait_recv())
    up_c.start()
    over_chips(lambda j: dn_x(j).wait_recv())
    dn_c.start()

    wo_c.wait_recv()
    for copy in att_z:
        copy.wait_recv()

    def heads_wo():
        return jnp.concatenate([wo_b[k].reshape(D, I) for k in range(T)], axis=1)

    att_all = jnp.concatenate([att[k].reshape(S * L, I) for k in range(T)], axis=1)
    res[...] = lat[...].astype(F32) + nt(att_all, heads_wo())
    for b in range(S * L // ROWS):
        rows = pl.ds(b * ROWS, ROWS)
        unit, _ = unit_rows(res[rows, :])
        hin[rows, :] = (unit * fgain[...] + fshift[...]).astype(BF16)

    up_c.wait_recv()
    dn_c.wait_recv()

    def feed(b, carry):
        cols = pl.ds(pl.multiple_of(b * BLOCK, BLOCK), BLOCK)
        before = nn(hin[...], up_b[:, :, :, cols].reshape(D, BLOCK))
        cdf = 0.5 * (1.0 + lax.erf(before * SQRT_HALF))
        act[:, cols] = (before * cdf).astype(BF16)
        slope = cdf + before * INV_ROOT_TWO_PI * jnp.exp(-0.5 * before * before)
        act_grad = nn(cot[...], dn_b[:, :, :, cols].reshape(D, BLOCK)).astype(BF16)
        bgr[:, cols] = (act_grad.astype(F32) * slope).astype(BF16)
        return carry

    lax.fori_loop(0, F // BLOCK, feed, 0)

    def back_to_width(left, weight, out):
        def one(b, carry):
            cols = pl.ds(pl.multiple_of(b * BLOCK, BLOCK), BLOCK)
            block = nt(left[...], weight[pl.ds(b * n, n)].reshape(BLOCK, F))
            out[:, :, cols] = block.astype(BF16).reshape(S, L, BLOCK)
            return carry

        lax.fori_loop(0, D // BLOCK, one, 0)

    back_to_width(bgr, up_b, hg)
    hg_z = [
        remote(hg.at[:, my_rows(k)], hgr.at[k - 1], zs.at[4, k - 1], zr.at[4, k - 1], z_dev(k)) for k in range(1, T)
    ]
    for copy in hg_z:
        copy.start()
    back_to_width(act, dn_b, fp)
    fp_z = [
        remote(fp.at[:, my_rows(k)], fpr.at[k - 1], zs.at[5, k - 1], zr.at[5, k - 1], z_dev(k)) for k in range(1, T)
    ]
    for copy in fp_z:
        copy.start()

    def feed_weights(left, right, out):
        def one(b, carry):
            cols = pl.ds(pl.multiple_of(b * BLOCK, BLOCK), BLOCK)
            block = tn(left[:, cols], right[...]).astype(BF16)
            out[pl.ds(b * n, n)] = block.reshape(n, 2, R, F)
            return carry

        lax.fori_loop(0, D // BLOCK, one, 0)

    def to_core(i, src, dst):
        return remote(src, dst, cs.at[i], cr.at[i], core_dev)

    feed_weights(hin, bgr, st_up)
    st_up_c = to_core(4, st_up.at[:, other], cr_up)
    st_up_c.start()
    feed_weights(cot, act, st_dn)
    st_dn_c = to_core(5, st_dn.at[:, other], cr_dn)
    st_dn_c.start()

    over_chips(lambda j: wq_x(j).wait_recv())
    wq_c.start()

    own_copy.wait()
    wq_c.wait_recv()

    for k in range(1, T):
        qall[:, pl.ds(k * I, I)] = nn(latn[...], wq_b[k, :, :, :, pl.ds(0, I)].reshape(D, I)).astype(BF16)
    half_rows = S * Kt // 2

    def all_pairs(i, carry):
        k = lax.div(i, 2)
        rows = pl.ds(pl.multiple_of(lax.rem(i, 2) * half_rows, 16), half_rows)
        lanes = pl.ds(pl.multiple_of(k * I, I), I)
        pair = nn(ctx[rows, :], wq_b[k, :, :, :, pl.ds(I, 2 * I)].reshape(D, 2 * I)).astype(BF16)
        kall[rows, lanes] = pair[:, :I]
        vall[rows, lanes] = pair[:, I:]
        return carry

    lax.fori_loop(0, 2 * T, all_pairs, 0)
    for copy in lse_z:
        copy.wait_recv()
    slot_of = lax.broadcasted_iota(jnp.int32, (Kt, 1), 0)

    def group(i):
        g, s = lax.div(i, S), lax.rem(i, S)
        rows = pl.ds(pl.multiple_of(s * Kt, 16), Kt)
        lanes = pl.ds(pl.multiple_of(g * GI, GI), GI)
        lat_rows = pl.ds(pl.multiple_of(s * L, L), L)
        return g, s, rows, lanes, lat_rows

    def joined(g, pick):
        return jnp.concatenate([pick(g * G + j) for j in range(G)], axis=1)

    def probabilities(i, carry):
        g, s, rows, lanes, lat_rows = group(i)
        scores = nt(kall[rows, lanes], spread(qall[lat_rows, lanes])) * scale_factor
        valid = (slot_of + t * Mt < counts[s] * PATCH) | (slot_of >= Mt)
        scores = jnp.where(valid, scores, NEGATIVE)
        pall[i] = jnp.exp(scores - joined(g, lambda k: lse[k, pl.ds(s, 1), :]))
        return carry

    lax.fori_loop(0, T // G * S, probabilities, 0, unroll=2)

    for copy in hg_z:
        copy.wait_recv()
    feed_gain_part = jnp.zeros((1, D), F32)
    feed_shift_part = jnp.zeros((1, D), F32)
    for s in range(S):
        own = pl.ds(pl.multiple_of(s * L + t * Lt, Lt), Lt)
        unit, scale_inv = unit_rows(res[own, :])
        upstream = hg[s, my_rows(), :].astype(F32)
        for k in range(1, T):
            upstream = upstream + hgr[k - 1, s].astype(F32)
        back = cot[own, :].astype(F32) + norm_back(unit, scale_inv, fgain[...], upstream)
        feed_gain_part = feed_gain_part + jnp.sum(upstream * unit, axis=0, keepdims=True)
        feed_shift_part = feed_shift_part + jnp.sum(upstream, axis=0, keepdims=True)
        rgr[pl.ds(s * Lt, Lt), :] = back
        og[pl.ds(s * Lt, Lt), :] = back.astype(BF16)
    grads_all = nn(og[...], heads_wo()).astype(BF16)
    for k in range(T):
        dob[head(k), :, my_rows(), :] = grads_all[:, k * I : (k + 1) * I].reshape(S, Lt, I)
    do_z = [
        remote(
            dob.at[:, :, my_rows(), :], dob.at[:, :, my_rows(), :], zs.at[6, k - 1], zr.at[6, k - 1], z_dev(k)
        )
        for k in range(1, T)
    ]
    do_in = [
        remote(
            dob.at[:, :, my_rows(T - k), :],
            dob.at[:, :, my_rows(T - k), :],
            zs.at[6, k - 1],
            zr.at[6, k - 1],
            z_dev(k),
        )
        for k in range(1, T)
    ]
    for copy in do_z:
        copy.start()

    att_own = jnp.concatenate([att[k, :, my_rows(), :].reshape(S * Lt, I) for k in range(T)], axis=1)
    for b in range(D // BLOCK):
        block = tn(og[:, pl.ds(b * BLOCK, BLOCK)], att_own).astype(BF16)
        for k in range(T):
            st_o[k, pl.ds(b * n, n)] = block[:, k * I : (k + 1) * I].reshape(n, 2, R, I)
    st_o_c = to_core(6, st_o.at[:, :, other], cr_o)
    st_o_c.start()

    def plane_feed(i, arrive, st, came, land):
        arrive.wait_recv()

        def add(chip):
            st[chip, core] = (st[chip, core].astype(F32) + came[chip].astype(F32)).astype(BF16)

        def copy(j):
            return remote(st.at[x_chip(j), core], land.at[j - 1], xs.at[i, j - 1], xr.at[i, j - 1], x_dev(j))

        def one(j):
            add(x_chip(j))
            copy(j).start()

        over_chips(one)
        add(c)
        return copy

    def plane_heads(i, arrive, st, came, land):
        arrive.wait_recv()

        def add(chip):
            for k in range(T):
                st[k, chip, core] = (st[k, chip, core].astype(F32) + came[k, chip].astype(F32)).astype(BF16)

        def copy(j):
            return remote(st.at[:, x_chip(j), core], land.at[j - 1], xs.at[i, j - 1], xr.at[i, j - 1], x_dev(j))

        def one(j):
            add(x_chip(j))
            copy(j).start()

        over_chips(one)
        add(c)
        return copy

    x_up = plane_feed(4, st_up_c, st_up, cr_up, xr_up)
    x_dn = plane_feed(5, st_dn_c, st_dn, cr_dn, xr_dn)

    for copy in do_in:
        copy.wait_recv()

    def attend_back(i, carry):
        g, s, rows, lanes, lat_rows = group(i)
        values_at = pl.ds(pl.multiple_of(T * I + g * GI, GI), GI)
        keys = kall[rows, lanes]
        queries = spread(qall[lat_rows, lanes])
        grads = spread(joined(g, lambda k: dob[head(k), s]))
        outs = spread(joined(g, lambda k: att[k, s]))
        product = grads.astype(F32) * outs.astype(F32)
        inner = lax.dot_general(
            jnp.ones((8, GI), F32),
            product,
            (((1,), (1,)), ((), ())),
            preferred_element_type=F32,
            precision=lax.Precision.HIGHEST,
        )[:1]
        probs = pall[i]
        score_grad = (probs * (nt(vall[rows, lanes], grads) - inner)).astype(BF16)
        pairs[rows, lanes] = (nn(score_grad, queries) * scale_factor).astype(BF16)
        pairs[rows, values_at] = nn(probs.astype(BF16), grads).astype(BF16)
        query_grad = (gather_heads(tn(score_grad, keys)) * scale_factor).astype(BF16)
        for j in range(G):
            dqb[head(g * G + j), s] = query_grad[:, j * I : (j + 1) * I]
        return carry

    lax.fori_loop(0, T // G * S, attend_back, 0, unroll=2)
    dq_z = [
        remote(
            dqb.at[:, :, my_rows(k), :], dqr.at[k - 1], zs.at[7, k - 1], zr.at[7, k - 1], z_dev(k)
        )
        for k in range(1, T)
    ]
    for copy in dq_z:
        copy.start()

    dq_all = jnp.concatenate([dqb[head(k)].reshape(S * L, I) for k in range(T)], axis=1)
    for b in range(D // BLOCK):
        cols = pl.ds(b * BLOCK, BLOCK)
        block = tn(ctx[:, cols], pairs[pl.ds(0, S * Kt), pl.ds(0, 2 * T * I)]).astype(BF16)
        query_block = tn(latn[:, cols], dq_all).astype(BF16)
        for k in range(T):
            lanes = slice(k * I, (k + 1) * I)
            parts = (query_block[:, lanes], block[:, lanes], block[:, T * I :][:, lanes])
            for m, part in enumerate(parts):
                st_qkv[k, pl.ds(b * n, n), :, :, pl.ds(m * I, I)] = part.reshape(n, 2, R, I)
    st_qkv_c = to_core(7, st_qkv.at[:, :, other], cr_qkv)
    st_qkv_c.start()
    x_o = plane_heads(6, st_o_c, st_o, cr_o, xr_o)
    x_qkv = plane_heads(7, st_qkv_c, st_qkv, cr_qkv, xr_qkv)

    for copy in fp_z:
        copy.wait_recv()
    for s in range(S):
        own = pl.ds(pl.multiple_of(s * L + t * Lt, Lt), Lt)
        total = fp[s, my_rows(), :].astype(F32)
        for k in range(1, T):
            total = total + fpr[k - 1, s].astype(F32)
        new_lat[s, my_rows(), :] = (res[own, :] + total).astype(BF16)

    def share_rows(i, ref):
        out = [
            remote(ref.at[:, my_rows(), :], ref.at[:, my_rows(), :], zs.at[i, k - 1], zr.at[i, k - 1], z_dev(k))
            for k in range(1, T)
        ]
        came = [
            remote(
                ref.at[:, my_rows(T - k), :],
                ref.at[:, my_rows(T - k), :],
                zs.at[i, k - 1],
                zr.at[i, k - 1],
                z_dev(k),
            )
            for k in range(1, T)
        ]
        return out, came

    nl_z, nl_in = share_rows(8, new_lat)
    for copy in nl_z:
        copy.start()

    acc[...] = jnp.zeros_like(acc)

    blocks = D // BLOCK

    def width(s, rows):
        return jnp.concatenate([pall[s % 2 * blocks + b, rows, :] for b in range(blocks)], axis=1)

    def media_width(s):
        for b in range(blocks):
            weights = jnp.concatenate(
                [
                    wq_b[k, pl.ds(b * n, n), :, :, pl.ds(m * I, I)].reshape(BLOCK, I)
                    for m in (1, 2)
                    for k in range(T)
                ],
                axis=1,
            )
            pall[s % 2 * blocks + b] = nt(pairs[pl.ds(s * Kt, Kt), pl.ds(0, 2 * T * I)], weights)

    def media_rows(s):
        for b in range(Mt // ROWS):
            rows = pl.ds(b * ROWS, ROWS)
            unit, scale_inv = unit_rows(mown[s, rows, :].astype(F32))
            upstream = width(s, rows)
            mown[s, rows, :] = norm_back(unit, scale_inv, mgain[...], upstream).astype(BF16)
            acc[0] += fold(upstream * unit)
            acc[1] += fold(upstream)
        mgl[pl.ds(s * Lt, Lt), :] = width(s, pl.ds(Mt, Lt))
        pltpu.make_async_copy(mown.at[s], media_grad.at[s], osem.at[s]).start()

    media_width(0)
    for s in range(S):
        if s + 1 < S:
            media_width(s + 1)
        media_rows(s)

    for copy in dq_z:
        copy.wait_recv()
    upstream_all = mgl[...]
    for k in range(T):
        total = dqb[head(k), :, my_rows(), :].astype(F32)
        for m in range(1, T):
            total = total + dqr[m - 1, head(k)].astype(F32)
        weights = wq_b[k, :, :, :, pl.ds(0, I)].reshape(D, I)
        upstream_all = upstream_all + nt(total.astype(BF16).reshape(S * Lt, I), weights)
    mgl[...] = upstream_all
    lat_gain_part = jnp.zeros((1, D), F32)
    lat_shift_part = jnp.zeros((1, D), F32)
    for s in range(S):
        own = pl.ds(pl.multiple_of(s * L + t * Lt, Lt), Lt)
        unit, scale_inv = unit_rows(lat[own, :].astype(F32))
        upstream = mgl[pl.ds(s * Lt, Lt), :]
        back = rgr[pl.ds(s * Lt, Lt), :] + norm_back(unit, scale_inv, lgain[...], upstream)
        lat_grad[s, my_rows(), :] = back.astype(BF16)
        lat_gain_part = lat_gain_part + jnp.sum(upstream * unit, axis=0, keepdims=True)
        lat_shift_part = lat_shift_part + jnp.sum(upstream, axis=0, keepdims=True)
    lg_z, lg_in = share_rows(9, lat_grad)
    for copy in lg_z:
        copy.start()

    vst[...] = jnp.concatenate(
        [
            jnp.sum(acc[0], axis=0, keepdims=True),
            jnp.sum(acc[1], axis=0, keepdims=True),
            lat_gain_part,
            lat_shift_part,
            feed_gain_part,
            feed_shift_part,
            jnp.zeros((2, D), F32),
        ],
        axis=0,
    )
    v_c = to_core(8, vst, vcr)
    v_c.start()
    v_c.wait_recv()
    vx[c] = vst[...] + vcr[...]

    def v_x(j):
        return remote(vx.at[c], vx.at[c], xs.at[8, j - 1], xr.at[8, j - 1], x_dev(j))

    def v_x_in(j):
        chip = lax.rem(c - j + C, C)
        return remote(vx.at[chip], vx.at[chip], xs.at[8, j - 1], xr.at[8, j - 1], x_dev(j))

    over_chips(lambda j: v_x(j).start())

    def sum_heads(x_copy, st, land):
        over_chips(lambda j: x_copy(j).wait_recv())
        for k in range(T):
            total = lax.fori_loop(
                1, C, lambda j, value, k=k: value + land[j - 1, k].astype(F32), st[k, c, core].astype(F32)
            )
            land[0, k] = total.astype(BF16)

    def z_sum(i, land, came):
        return [
            remote(land.at[0, k], came.at[T - k - 1], zs.at[i, k - 1], zr.at[i, T - k - 1], (d, head(k)))
            for k in range(1, T)
        ]

    sum_heads(x_o, st_o, xr_o)
    o_z = z_sum(10, xr_o, zr_o)
    for copy in o_z:
        copy.start()
    sum_heads(x_qkv, st_qkv, xr_qkv)
    q_z = z_sum(11, xr_qkv, zr_qkv)
    for copy in q_z:
        copy.start()

    over_chips(lambda j: v_x_in(j).wait_recv())
    vz[t] = lax.fori_loop(1, C, lambda j, value: value + vx[j], vx[0])
    v_z = [remote(vz.at[t], vz.at[t], zs.at[12, k - 1], zr.at[12, k - 1], z_dev(k)) for k in range(1, T)]
    v_z_in = [
        remote(vz.at[head(k)], vz.at[head(k)], zs.at[12, k - 1], zr.at[12, k - 1], z_dev(k)) for k in range(1, T)
    ]
    for copy in v_z:
        copy.start()

    def sum_feed(x_copy, st, land, out):
        over_chips(lambda j: x_copy(j).wait_recv())
        out[...] = lax.fori_loop(
            1, C, lambda j, value: value + land[j - 1].astype(F32), st[c, core].astype(F32)
        )

    sum_feed(x_up, st_up, xr_up, g_up)
    sum_feed(x_dn, st_dn, xr_dn, g_dn)

    for copy in v_z_in:
        copy.wait_recv()
    g_vec[...] = lax.fori_loop(1, T, lambda k, value: value + vz[k], vz[0])
    for copy in o_z:
        copy.wait_recv()
    total = xr_o[0, 0].astype(F32)
    for k in range(1, T):
        total = total + zr_o[k - 1].astype(F32)
    g_o[...] = total
    for copy in q_z:
        copy.wait_recv()
    total = xr_qkv[0, 0].astype(F32)
    for k in range(1, T):
        total = total + zr_qkv[k - 1].astype(F32)
    g_qkv[...] = total

    for copy in nl_in + lg_in:
        copy.wait_recv()
    for copy in wo_z + wq_z + att_z + lse_z + hg_z + fp_z + do_z + dq_z + nl_z + lg_z + o_z + q_z + v_z:
        copy.wait_send()
    for one in (wo_x, wq_x, up_x, dn_x, x_up, x_dn, x_o, x_qkv, v_x):
        over_chips(lambda j, one=one: one(j).wait_send())
    for copy in (wo_c, wq_c, up_c, dn_c, st_up_c, st_dn_c, st_o_c, st_qkv_c, v_c):
        copy.wait_send()
    for s in range(S):
        pltpu.make_async_copy(mown.at[s], media_grad.at[s], osem.at[s]).wait()


def hand_out(z, new_lat, media_grad, lat_grad, g_qkv, g_o, g_up, g_dn, g_vec, *refs):
    outs, held, sem_in, sem_out = refs[:15], refs[15], refs[16], refs[17]
    loads = [pltpu.make_async_copy(media_grad.at[s], held.at[s], sem_in.at[s]) for s in range(z.S)]
    stores = [pltpu.make_async_copy(held.at[s], outs[1].at[s], sem_out.at[s]) for s in range(z.S)]
    for copy in loads:
        copy.start()
    for load, store in zip(loads, stores):
        load.wait()
        store.start()
    outs[0][...] = new_lat[...]
    outs[2][...] = lat_grad[...]
    for m in range(3):
        outs[3 + m][...] = g_qkv[:, pl.ds(m * z.I, z.I)]
    outs[6][...] = g_o[...].T
    outs[7][...] = g_up[...]
    outs[8][...] = g_dn[...].T
    outs[9][...] = g_vec[pl.ds(0, 1), :]
    outs[10][...] = g_vec[pl.ds(1, 1), :]
    first = lax.axis_index("dp") * z.R
    row = lax.broadcasted_iota(jnp.int32, (z.D, z.R), 0)
    col = lax.broadcasted_iota(jnp.int32, (z.D, z.R), 1)
    pick = jnp.where(row == col + first, 1.0, 0.0).astype(F32)
    own = lax.dot_general(
        g_vec[...], pick, (((1,), (0,)), ((), ())), preferred_element_type=F32, precision=lax.Precision.HIGHEST
    )
    for m in range(4):
        outs[11 + m][...] = own[2 + m : 3 + m]
    for store in stores:
        store.wait()


def solution(mesh):
    T, N = mesh.shape["tensor"], mesh.shape["dp"]

    def on_device(
        media_tokens,
        latents,
        image_counts,
        media_gain,
        media_shift,
        latent_gain,
        latent_shift,
        feed_gain,
        feed_shift,
        query_weight,
        key_weight,
        value_weight,
        output_weight,
        up_weight,
        down_weight,
        cotangent,
    ):
        samples, slots, width = media_tokens.shape
        z = Sizes(T, N, samples, latents.shape[1], slots, width, up_weight.shape[1], query_weight.shape[1])
        S, L, D, F, I, R, C = z.S, z.L, z.D, z.F, z.I, z.R, z.C
        row = lambda v: v.reshape(1, D)
        vmem = pl.BlockSpec(memory_space=pltpu.VMEM)
        hbm = pl.BlockSpec(memory_space=pl.ANY)
        V = pltpu.VMEM
        scratch = [
            V((T, C, 2, R, 3 * I), BF16),
            V((T, C, 2, R, I), BF16),
            V((C, 2, R, F), BF16),
            V((C, 2, R, F), BF16),
            V((SLOTS_IN_FLIGHT, z.Mt, D), BF16),
            V((S, z.Mt, D), BF16),
            V((2, z.Mt, D), BF16),
            V((S * z.Kt, D), BF16),
            V((S * L, D), BF16),
            V((T, S, L, I), BF16),
            V((T, max(S, 8), z.q), F32),
            V((S * L, T * I), BF16),
            V((S * z.Kt, T * I), BF16),
            V((S * z.Kt, T * I), BF16),
            V((max(T // z.G * S, 2 * D // BLOCK), z.Kt, z.G * z.q), F32),
            V((max(z.K, S * z.Kt), max(S, T) * 2 * I), BF16),
            V((S * L, D), F32),
            V((S * L, D), BF16),
            V((S * L, F), BF16),
            V((S * L, F), BF16),
            V((S, L, D), BF16),
            V((T - 1, S, z.Lt, D), BF16),
            V((S, L, D), BF16),
            V((T - 1, S, z.Lt, D), BF16),
            V((S * z.Lt, D), BF16),
            V((S * z.Lt, D), F32),
            V((T, S, L, I), BF16),
            V((T, S, L, I), BF16),
            V((T - 1, T, S, z.Lt, I), BF16),
            V((C, 2, R, F), BF16),
            V((C, 2, R, F), BF16),
            V((T, C, 2, R, I), BF16),
            V((T, C, 2, R, 3 * I), BF16),
            V((C, R, F), BF16),
            V((C, R, F), BF16),
            V((T, C, R, I), BF16),
            V((T, C, R, 3 * I), BF16),
            V((max(C - 1, 1), R, F), BF16),
            V((max(C - 1, 1), R, F), BF16),
            V((max(C - 1, 1), T, R, I), BF16),
            V((max(C - 1, 1), T, R, 3 * I), BF16),
            V((T - 1, R, I), BF16),
            V((T - 1, R, 3 * I), BF16),
            V((S * z.Lt, D), F32),
            V((2, 8, D), F32),
            V((8, D), F32),
            V((8, D), F32),
            V((C, 8, D), F32),
            V((T, 8, D), F32),
            pltpu.SemaphoreType.DMA((SLOTS_IN_FLIGHT + 1,)),
            pltpu.SemaphoreType.DMA((S,)),
            pltpu.SemaphoreType.DMA((13, T - 1)),
            pltpu.SemaphoreType.DMA((13, T - 1)),
            pltpu.SemaphoreType.DMA((9, max(C - 1, 1))),
            pltpu.SemaphoreType.DMA((9, max(C - 1, 1))),
            pltpu.SemaphoreType.DMA((9,)),
            pltpu.SemaphoreType.DMA((9,)),
        ]
        shape = jax.ShapeDtypeStruct
        outs = pl.pallas_call(
            functools.partial(layer_kernel, z),
            out_shape=[
                shape((S, L, D), BF16),
                shape((S, z.Mt, D), BF16),
                shape((S, L, D), BF16),
                shape((R, 3 * I), F32),
                shape((R, I), F32),
                shape((R, F), F32),
                shape((R, F), F32),
                shape((8, D), F32),
            ],
            in_specs=[pl.BlockSpec(memory_space=pltpu.SMEM), hbm] + [vmem] * 14,
            out_specs=[vmem, hbm] + [vmem] * 6,
            scratch_shapes=scratch,
            compiler_params=pltpu.CompilerParams(
                collective_id=0, has_side_effects=True, vmem_limit_bytes=63 * 1024 * 1024
            ),
            name="resampler_layer",
        )(
            image_counts,
            media_tokens,
            latents.reshape(S * L, D),
            cotangent.reshape(S * L, D),
            row(media_gain),
            row(media_shift),
            row(latent_gain),
            row(latent_shift),
            row(feed_gain),
            row(feed_shift),
            query_weight,
            key_weight,
            value_weight,
            output_weight,
            up_weight,
            down_weight,
        )
        final = pl.pallas_call(
            functools.partial(hand_out, z),
            out_shape=[
                shape((S, L, D), BF16),
                shape((S, z.Mt, D), BF16),
                shape((S, L, D), BF16),
                shape((R, I), F32),
                shape((R, I), F32),
                shape((R, I), F32),
                shape((I, R), F32),
                shape((R, F), F32),
                shape((F, R), F32),
                shape((1, D), F32),
                shape((1, D), F32),
            ]
            + [shape((1, R), F32)] * 4,
            in_specs=[vmem, hbm] + [vmem] * 6,
            out_specs=[vmem, hbm] + [vmem] * 13,
            scratch_shapes=[V((S, z.Mt, D), BF16), pltpu.SemaphoreType.DMA((S,)), pltpu.SemaphoreType.DMA((S,))],
            name="hand_out",
        )(*outs)
        return tuple(final[:9]) + tuple(v.reshape(-1) for v in final[9:])

    placed = (
        P("dp", None, None),
        P("dp", None, None),
        P("dp"),
        P(),
        P(),
        P(),
        P(),
        P(),
        P(),
        P(None, "tensor"),
        P(None, "tensor"),
        P(None, "tensor"),
        P("tensor", None),
        P("dp", "tensor"),
        P("tensor", "dp"),
        P("dp", None, None),
    )
    return jax.shard_map(
        on_device,
        mesh=mesh,
        in_specs=placed,
        out_specs=(
            P("dp", None, None),
            P("dp", "tensor", None),
            P("dp", None, None),
            P("dp", "tensor"),
            P("dp", "tensor"),
            P("dp", "tensor"),
            P("tensor", "dp"),
            P("dp", "tensor"),
            P("tensor", "dp"),
            P(),
            P(),
            P("dp"),
            P("dp"),
            P("dp"),
            P("dp"),
        ),
        check_vma=False,
    )
```

```python
import functools

import jax
import jax.numpy as jnp
from jax import lax
from jax.experimental import pallas as pl
from jax.experimental.pallas import tpu as pltpu
from jax.sharding import PartitionSpec as P

HEAD_DIM = 64
PATCH = 256
EPSILON = 1e-05
NEGATIVE = -1e30
SQRT_HALF = 0.7071067811865476
INV_ROOT_TWO_PI = 0.3989422804014327
F32 = jnp.float32
BF16 = jnp.bfloat16
MESH = pl.DeviceIdType.MESH
BLOCK = 256
ROWS = 32
SLOTS_IN_FLIGHT = 3


def nn(left, right):
    return lax.dot_general(left, right, (((1,), (0,)), ((), ())), preferred_element_type=F32)


def nt(left, right):
    return lax.dot_general(left, right, (((1,), (1,)), ((), ())), preferred_element_type=F32)


def tn(left, right):
    return lax.dot_general(left, right, (((0,), (0,)), ((), ())), preferred_element_type=F32)


def unit_rows(x):
    centre = x - jnp.mean(x, axis=-1, keepdims=True)
    scale_inv = lax.rsqrt(jnp.mean(centre * centre, axis=-1, keepdims=True) + EPSILON)
    return centre * scale_inv, scale_inv


def norm_back(unit, scale_inv, gain, upstream):
    scaled = upstream * gain
    inner = scaled - jnp.mean(scaled, axis=-1, keepdims=True)
    inner = inner - unit * jnp.mean(scaled * unit, axis=-1, keepdims=True)
    return inner * scale_inv


def fold(x):
    return jnp.sum(x.reshape(x.shape[0] // 8, 8, x.shape[1]), axis=0)


class Sizes:
    def __init__(self, tensor, dp, samples, lat, slots, width, hidden, inner):
        self.T, self.N, self.C = tensor, dp, dp // 2
        self.S, self.L, self.M, self.D = samples, lat, slots, width
        self.F, self.I = hidden, inner
        self.R = width // dp
        self.Lt, self.Mt = lat // tensor, slots // tensor
        self.Kt = self.Lt + self.Mt
        self.K = lat + slots
        self.H = inner // HEAD_DIM
        self.q = self.H * lat
        self.G = min(2, tensor)


def layer_kernel(
    z,
    counts,
    media,
    lat,
    cot,
    mgain,
    mshift,
    lgain,
    lshift,
    fgain,
    fshift,
    wq,
    wk,
    wv,
    wo,
    up,
    dn,
    new_lat,
    media_grad,
    lat_grad,
    g_qkv,
    g_o,
    g_up,
    g_dn,
    g_vec,
    wq_b,
    wo_b,
    up_b,
    dn_b,
    mbuf,
    mown,
    xn,
    ctx,
    latn,
    att,
    lse,
    qall,
    kall,
    vall,
    pall,
    pairs,
    res,
    hin,
    act,
    bgr,
    hg,
    hgr,
    fp,
    fpr,
    og,
    rgr,
    dob,
    dqb,
    dqr,
    st_up,
    st_dn,
    st_o,
    st_qkv,
    cr_up,
    cr_dn,
    cr_o,
    cr_qkv,
    xr_up,
    xr_dn,
    xr_o,
    xr_qkv,
    zb_o,
    zb_qkv,
    zr_o,
    zr_qkv,
    mgl,
    acc,
    vst,
    vcr,
    vx,
    vz,
    msem,
    osem,
    zs,
    zr,
    xs,
    xr,
    cs,
    cr,
):
    T, N, C, S, L, M, D = z.T, z.N, z.C, z.S, z.L, z.M, z.D
    F, I, R, Lt, Mt, Kt, G = z.F, z.I, z.R, z.Lt, z.Mt, z.Kt, z.G
    GI = G * I
    groups = T // G
    scale_factor = HEAD_DIM ** (-0.5)
    t = lax.axis_index("tensor")
    d = lax.axis_index("dp")
    c = lax.div(d, 2)
    core = lax.rem(d, 2)
    other = 1 - core
    n = BLOCK // (2 * R)
    blocks = D // BLOCK
    count = {"z": 0, "x": 0, "c": 0}
    started = []

    def row(kind):
        count[kind] += 1
        return count[kind] - 1

    def start(copies):
        for copy in copies:
            copy.start()
        started.extend(copies)

    def arrive(copies):
        for copy in copies:
            copy.wait_recv()

    def z_dev(k):
        return (d, lax.rem(t + k, T))

    def x_dev(j):
        return (2 * lax.rem(c + j, C) + core, t)

    core_dev = (d + 1 - 2 * core, t)

    def head(k):
        return lax.rem(t - k + T, T)

    def my_rows(k=0):
        return pl.ds(pl.multiple_of(lax.rem(t + k, T) * Lt, Lt), Lt)

    def remote(src, dst, send, recv, dev):
        return pltpu.make_async_remote_copy(
            src_ref=src, dst_ref=dst, send_sem=send, recv_sem=recv, device_id=dev, device_id_type=MESH
        )

    def over_z(pick):
        i = row("z")
        return [remote(*pick(k), zs.at[i, k - 1], zr.at[i, k - 1], z_dev(k)) for k in range(1, T)]

    def share_rows(pick):
        out = over_z(lambda k: (pick(my_rows()), pick(my_rows())))
        i = count["z"] - 1
        came = [
            remote(pick(my_rows(T - k)), pick(my_rows(T - k)), zs.at[i, k - 1], zr.at[i, k - 1], z_dev(k))
            for k in range(1, T)
        ]
        return out, came

    def line_share(pick):
        ways = []
        for step in (1, -1):
            i = row("z")
            hops = []
            for h in range(1, T):
                owner, fresh = t - step * (h - 1), t - step * h
                beyond = t + step
                sends = (owner >= 0) & (owner < T) & (beyond >= 0) & (beyond < T)
                comes = (fresh >= 0) & (fresh < T)
                mine, theirs = pick(my_rows(T - step * (h - 1))), pick(my_rows(T - step * h))
                dev = (d, lax.rem(t + step + T, T))
                sems = (zs.at[i, h - 1], zr.at[i, h - 1])
                hops.append((sends, remote(mine, mine, *sems, dev), comes, remote(theirs, theirs, *sems, dev)))
            ways.append(hops)

        def hop(h, last=False):
            if h >= T and not last:
                return
            for hops in ways:
                if h > 1:
                    pl.when(hops[h - 2][2])(hops[h - 2][3].wait_recv)
                if h < T:
                    pl.when(hops[h - 1][0])(hops[h - 1][1].start)

        def end():
            hop(T, last=True)
            for hops in ways:
                for sends, copy, _, _ in hops:
                    pl.when(sends)(copy.wait_send)

        return hop, end

    def over_core(src, dst):
        i = row("c")
        return [remote(src, dst, cs.at[i], cr.at[i], core_dev)]

    bits = C.bit_length() - 1
    x_first = list(range(bits))
    y_first = x_first[::-1]

    def flip(chip, mask):
        for bit in range(bits):
            if mask >> bit & 1:
                chip = chip + (1 - 2 * lax.rem(lax.div(chip, 1 << bit), 2)) * (1 << bit)
        return chip

    def subsets(order):
        masks = [0]
        for bit in order:
            masks = masks + [m | 1 << bit for m in masks]
        return masks

    def gather_steps(view, order):
        i, at, steps = row("x"), 0, []
        for step, bit in enumerate(order):
            peer = flip(c, 1 << bit)
            dev = (2 * peer + core, t)
            out, came = [], []
            for m in subsets(order[:step]):
                sems = (xs.at[i, at], xr.at[i, at])
                mine, theirs = view(flip(c, m)), view(flip(peer, m))
                out.append(remote(mine, mine, *sems, dev))
                came.append(remote(theirs, theirs, *sems, dev))
                at += 1
            steps.append((out, came))
        return steps

    def scatter_steps(view, land, order):
        i, at, steps = row("x"), 0, []
        for step, bit in enumerate(order):
            peer = flip(c, 1 << bit)
            dev = (2 * peer + core, t)
            out, keep = [], []
            for m in subsets(order[step + 1 :]):
                out.append(remote(view(flip(peer, m)), land(at), xs.at[i, at], xr.at[i, at], dev))
                keep.append((flip(c, m), at))
                at += 1
            steps.append((out, keep))
        return steps

    n_tiles = S * T

    def tile_copy(i):
        slot = lax.rem(i, SLOTS_IN_FLIGHT)
        s, r = lax.div(i, T), lax.rem(i, T)
        return pltpu.make_async_copy(
            media.at[s, pl.ds(pl.multiple_of(r * Mt, Mt), Mt)], mbuf.at[slot], msem.at[slot]
        )

    own_copy = pltpu.make_async_copy(
        media.at[:, pl.ds(pl.multiple_of(t * Mt, Mt), Mt)], mown, msem.at[SLOTS_IN_FLIGHT]
    )
    for i in range(min(SLOTS_IN_FLIGHT, n_tiles)):
        tile_copy(i).start()
    barrier = pltpu.get_barrier_semaphore()

    def greet(dev):
        pl.semaphore_signal(barrier, inc=1, device_id=dev, device_id_type=MESH)

    for k in range(1, T):
        greet(z_dev(k))
    lax.fori_loop(1, C, lambda j, carry: (greet(x_dev(j)), carry)[1], 0)
    greet(core_dev)
    up_b[c, core] = up[...]
    dn_b[c, core] = dn[...].T
    wo_b[0] = wo[...].T.reshape(C, 2, R, I)
    for m, weight in enumerate((wq, wk, wv)):
        wq_b[0, :, :, :, pl.ds(m * I, I)] = weight[...].reshape(C, 2, R, I)
    pl.semaphore_wait(barrier, T + C - 1)

    foreign = pl.ds(1, T - 1)
    up_x = gather_steps(lambda chip: up_b.at[chip, core], x_first)
    dn_x = gather_steps(lambda chip: dn_b.at[chip, core], y_first)
    wo_x = gather_steps(lambda chip: wo_b.at[foreign, chip, core], x_first)
    qk_x = gather_steps(lambda chip: wq_b.at[foreign, chip, core, :, pl.ds(0, 2 * I)], x_first)
    v_x = gather_steps(lambda chip: wq_b.at[foreign, chip, core, :, pl.ds(2 * I, I)], y_first)
    wo_z = over_z(lambda k: (wo_b.at[0, c, core], wo_b.at[k, c, core]))
    wq_z = over_z(lambda k: (wq_b.at[0, c, core], wq_b.at[k, c, core]))
    up_c = over_core(up_b.at[:, core], up_b.at[:, core])
    dn_c = over_core(dn_b.at[:, core], dn_b.at[:, core])
    wo_c = over_core(wo_b.at[foreign, :, core], wo_b.at[foreign, :, core])
    wq_c = over_core(wq_b.at[foreign, :, core], wq_b.at[foreign, :, core])

    def gather_rest(steps):
        for step in range(1, len(steps)):
            arrive(steps[step - 1][1])
            start(steps[step][0])

    start(up_x[0][0])
    start(dn_x[0][0])
    start(wo_z)
    start(wq_z)
    own_copy.start()

    for b in range(S * L // ROWS):
        rows = pl.ds(b * ROWS, ROWS)
        unit, _ = unit_rows(lat[rows, :].astype(F32))
        latn[rows, :] = (unit * lgain[...] + lshift[...]).astype(BF16)
    own_qkv = nn(latn[...], wq_b[0].reshape(D, 3 * I)).astype(BF16)
    qall[:, pl.ds(0, I)] = own_qkv[:, :I]
    for s in range(S):
        pairs[pl.ds(M, L), pl.ds(s * 2 * I, 2 * I)] = own_qkv[s * L : (s + 1) * L, I:]
        ctx[pl.ds(s * Kt + Mt, Lt), :] = latn[pl.ds(pl.multiple_of(s * L + t * Lt, Lt), Lt), :]

    def tile_norm(i, half):
        slot = lax.rem(i, SLOTS_IN_FLIGHT)
        for b in range(Mt // ROWS):
            rows = pl.ds(b * ROWS, ROWS)
            unit, _ = unit_rows(mbuf[slot, rows, :].astype(F32))
            xn[half, rows, :] = (unit * mgain[...] + mshift[...]).astype(BF16)

    def tile_pair(i, half):
        s, r = lax.div(i, T), lax.rem(i, T)
        pair = nn(xn[half], wq_b[0, :, :, :, pl.ds(I, 2 * I)].reshape(D, 2 * I))
        lanes = pl.ds(pl.multiple_of(s * 2 * I, 2 * I), 2 * I)
        pairs[pl.ds(pl.multiple_of(r * Mt, Mt), Mt), lanes] = pair.astype(BF16)

    def tile_keep(i, half):
        s, r = lax.div(i, T), lax.rem(i, T)

        @pl.when(r == t)
        def _():
            ctx[pl.ds(pl.multiple_of(s * Kt, 16), Mt), :] = xn[half]

    def tile_next(i):
        @pl.when(i + SLOTS_IN_FLIGHT < n_tiles)
        def _():
            tile_copy(i + SLOTS_IN_FLIGHT).start()

    tile_copy(0).wait()
    tile_norm(0, 0)
    tile_next(0)

    def two_tiles(j, carry):
        i = 2 * j
        tile_copy(i + 1).wait()

        @pl.when(i + 2 < n_tiles)
        def _():
            tile_copy(i + 2).wait()

        tile_keep(i, 0)
        tile_pair(i, 0)
        tile_norm(i + 1, 1)
        tile_keep(i + 1, 1)
        tile_pair(i + 1, 1)
        tile_norm(lax.rem(i + 2, n_tiles), 0)
        tile_next(i + 1)
        tile_next(i + 2)
        return carry

    first, second = n_tiles // 8, 3 * n_tiles // 8
    lax.fori_loop(0, first, two_tiles, 0)
    arrive(wo_z)
    start(wo_x[0][0])
    lax.fori_loop(first, second, two_tiles, 0)
    gather_rest(up_x)
    gather_rest(dn_x)
    lax.fori_loop(second, n_tiles // 2, two_tiles, 0)
    gather_rest(wo_x)

    def spread(x):
        lane_head = lax.broadcasted_iota(jnp.int32, (1, x.shape[1]), 1) // HEAD_DIM
        zero = jnp.zeros_like(x)
        return jnp.concatenate(
            [jnp.where(lane_head == h, x, zero) for h in range(x.shape[1] // HEAD_DIM)], axis=0
        )

    def gather_heads(x):
        lane_head = lax.broadcasted_iota(jnp.int32, (1, x.shape[1]), 1) // HEAD_DIM
        out = x[:L]
        for h in range(1, x.shape[1] // HEAD_DIM):
            out = jnp.where(lane_head == h, x[h * L : (h + 1) * L], out)
        return out

    att_z = []
    for s in range(S):
        keys = pairs[pl.ds(0, z.K), pl.ds(s * 2 * I, I)]
        values = pairs[pl.ds(0, z.K), pl.ds(s * 2 * I + I, I)]
        scores = nt(keys, spread(qall[pl.ds(s * L, L), pl.ds(0, I)])) * scale_factor
        slot = lax.broadcasted_iota(jnp.int32, (z.K, 1), 0)
        valid = (slot < counts[s] * PATCH) | (slot >= M)
        scores = jnp.where(valid, scores, NEGATIVE)
        largest = jnp.max(scores, axis=0, keepdims=True)
        total = largest + jnp.log(jnp.sum(jnp.exp(scores - largest), axis=0, keepdims=True))
        probs = jnp.exp(scores - total).astype(BF16)
        att[0, s] = gather_heads(tn(probs, values)).astype(BF16)
        lse[0, pl.ds(s, 1), :] = total
        if s % 2 == 1:
            now = over_z(lambda k, s=s: (att.at[0, pl.ds(s - 1, 2)], att.at[k, pl.ds(s - 1, 2)]))
            start(now)
            att_z += now
    lse_z = over_z(lambda k: (lse.at[0], lse.at[k]))
    start(lse_z)

    for s in range(S):
        lanes = s * 2 * I
        own_slots = pl.ds(pl.multiple_of(t * Mt, Mt), Mt)
        own_lat = pl.ds(pl.multiple_of(M + t * Lt, Lt), Lt)
        for m, ref in enumerate((kall, vall)):
            ref[pl.ds(s * Kt, Mt), pl.ds(0, I)] = pairs[own_slots, pl.ds(lanes + m * I, I)]
            ref[pl.ds(s * Kt + Mt, Lt), pl.ds(0, I)] = pairs[own_lat, pl.ds(lanes + m * I, I)]
    arrive(wo_x[-1][1])
    start(wo_c)
    arrive(up_x[-1][1])
    start(up_c)
    arrive(dn_x[-1][1])
    start(dn_c)
    arrive(wq_z)
    start(qk_x[0][0])
    start(v_x[0][0])

    def heads_wo():
        return jnp.concatenate([wo_b[k].reshape(D, I) for k in range(T)], axis=1)

    arrive(wo_c)
    arrive(att_z)
    att_all = jnp.concatenate([att[k].reshape(S * L, I) for k in range(T)], axis=1)
    res[...] = lat[...].astype(F32) + nt(att_all, heads_wo())
    for b in range(S * L // ROWS):
        rows = pl.ds(b * ROWS, ROWS)
        unit, _ = unit_rows(res[rows, :])
        hin[rows, :] = (unit * fgain[...] + fshift[...]).astype(BF16)

    arrive(up_c)
    arrive(dn_c)

    def feed(b, carry):
        cols = pl.ds(pl.multiple_of(b * BLOCK, BLOCK), BLOCK)
        before = nn(hin[...], up_b[:, :, :, cols].reshape(D, BLOCK))
        cdf = 0.5 * (1.0 + lax.erf(before * SQRT_HALF))
        act[:, cols] = (before * cdf).astype(BF16)
        slope = cdf + before * INV_ROOT_TWO_PI * jnp.exp(-0.5 * before * before)
        act_grad = nn(cot[...], dn_b[:, :, :, cols].reshape(D, BLOCK)).astype(BF16)
        bgr[:, cols] = (act_grad.astype(F32) * slope).astype(BF16)
        return carry

    lax.fori_loop(0, F // BLOCK, feed, 0, unroll=2)

    def back_to_width(left, weight, out, b):
        block = nt(left[...], weight[pl.ds(b * n, n)].reshape(BLOCK, F))
        out[:, :, pl.ds(b * BLOCK, BLOCK)] = block.astype(BF16).reshape(S, L, BLOCK)

    hg_z = []
    for b in range(blocks):
        cols = pl.ds(b * BLOCK, BLOCK)
        back_to_width(bgr, up_b, hg, b)
        now = over_z(lambda k, cols=cols: (hg.at[:, my_rows(k), cols], hgr.at[k - 1, :, :, cols]))
        start(now)
        hg_z += now
    gather_rest(qk_x)
    gather_rest(v_x)

    def feed_weights(left, right, out, b):
        block = tn(left[:, pl.ds(b * BLOCK, BLOCK)], right[...]).astype(BF16)
        out[pl.ds(b * n, n)] = block.reshape(n, 2, R, F)

    for b in range(blocks):
        feed_weights(hin, bgr, st_up, b)
    st_up_c = over_core(st_up.at[:, other], cr_up)
    start(st_up_c)
    for b in range(blocks):
        feed_weights(cot, act, st_dn, b)
    st_dn_c = over_core(st_dn.at[:, other], cr_dn)
    start(st_dn_c)
    for b in range(blocks):
        back_to_width(act, dn_b, fp, b)

    up_g = scatter_steps(lambda chip: st_up.at[chip, core], lambda at: xr_up.at[at], y_first)
    dn_g = scatter_steps(lambda chip: st_dn.at[chip, core], lambda at: xr_dn.at[at], x_first)

    def feed_core(copy, st, came, steps):
        arrive(copy)
        sent = steps[0][0]
        for m in subsets(range(bits)):
            chip = flip(c, m)
            st[chip, core] = (st[chip, core].astype(F32) + came[chip].astype(F32)).astype(BF16)
        start(sent)

    def feed_step(st, land, steps):
        for step in range(1, len(steps)):
            arrive(steps[step - 1][0])
            for chip, at in steps[step - 1][1]:
                st[chip, core] = (st[chip, core].astype(F32) + land[at].astype(F32)).astype(BF16)
            start(steps[step][0])

    def feed_last(st, land, steps, out):
        arrive(steps[-1][0])
        out[...] = st[c, core].astype(F32) + land[steps[-1][1][0][1]].astype(F32)

    feed_core(st_up_c, st_up, cr_up, up_g)
    feed_core(st_dn_c, st_dn, cr_dn, dn_g)

    arrive(hg_z)
    feed_gain_part = jnp.zeros((1, D), F32)
    feed_shift_part = jnp.zeros((1, D), F32)
    for s in range(S):
        own = pl.ds(pl.multiple_of(s * L + t * Lt, Lt), Lt)
        unit, scale_inv = unit_rows(res[own, :])
        upstream = hg[s, my_rows(), :].astype(F32)
        for k in range(1, T):
            upstream = upstream + hgr[k - 1, s].astype(F32)
        back = cot[own, :].astype(F32) + norm_back(unit, scale_inv, fgain[...], upstream)
        feed_gain_part = feed_gain_part + jnp.sum(upstream * unit, axis=0, keepdims=True)
        feed_shift_part = feed_shift_part + jnp.sum(upstream, axis=0, keepdims=True)
        rgr[pl.ds(s * Lt, Lt), :] = back
        og[pl.ds(s * Lt, Lt), :] = back.astype(BF16)
    vst[...] = jnp.concatenate(
        [jnp.zeros((4, D), F32), feed_gain_part, feed_shift_part, jnp.zeros((2, D), F32)], axis=0
    )
    grads_all = nn(og[...], heads_wo()).astype(BF16)
    for k in range(T):
        dob[head(k), :, my_rows(), :] = grads_all[:, k * I : (k + 1) * I].reshape(S, Lt, I)
    do_z, do_in = share_rows(lambda rows: dob.at[:, :, rows, :])
    start(do_z)

    att_own = jnp.concatenate([att[k, :, my_rows(), :].reshape(S * Lt, I) for k in range(T)], axis=1)
    for b in range(blocks):
        block = tn(og[:, pl.ds(b * BLOCK, BLOCK)], att_own).astype(BF16)
        for k in range(T):
            st_o[k, pl.ds(b * n, n)] = block[:, k * I : (k + 1) * I].reshape(n, 2, R, I)
    st_o_c = over_core(st_o.at[:, :, other], cr_o)
    start(st_o_c)

    arrive(qk_x[-1][1])
    arrive(v_x[-1][1])
    start(wq_c)
    own_copy.wait()
    arrive(wq_c)
    for k in range(1, T):
        qall[:, pl.ds(k * I, I)] = nn(latn[...], wq_b[k, :, :, :, pl.ds(0, I)].reshape(D, I)).astype(BF16)
    half_rows = S * Kt // 2

    def all_pairs(i, carry):
        k = lax.div(i, 2)
        rows = pl.ds(pl.multiple_of(lax.rem(i, 2) * half_rows, 16), half_rows)
        lanes = pl.ds(pl.multiple_of(k * I, I), I)
        pair = nn(ctx[rows, :], wq_b[k, :, :, :, pl.ds(I, 2 * I)].reshape(D, 2 * I)).astype(BF16)
        kall[rows, lanes] = pair[:, :I]
        vall[rows, lanes] = pair[:, I:]
        return carry

    lax.fori_loop(2, 2 * T, all_pairs, 0)
    arrive(lse_z)
    slot_of = lax.broadcasted_iota(jnp.int32, (Kt, 1), 0)

    def group(g, s):
        rows = pl.ds(pl.multiple_of(s * Kt, 16), Kt)
        lat_rows = pl.ds(pl.multiple_of(s * L, L), L)
        return rows, pl.ds(g * GI, GI), lat_rows

    def joined(g, pick):
        return jnp.concatenate([pick(g * G + j) for j in range(G)], axis=1)

    for g in range(groups):

        def probabilities(s, carry, g=g):
            rows, lanes, lat_rows = group(g, s)
            scores = nt(kall[rows, lanes], spread(qall[lat_rows, lanes])) * scale_factor
            valid = (slot_of + t * Mt < counts[s] * PATCH) | (slot_of >= Mt)
            scores = jnp.where(valid, scores, NEGATIVE)
            pall[g * S + s] = jnp.exp(scores - joined(g, lambda k: lse[k, pl.ds(s, 1), :]))
            return carry

        lax.fori_loop(0, S, probabilities, 0, unroll=2)

    def heads_core(st, came, ks, steps):
        for m in subsets(range(bits)):
            chip = flip(c, m)
            for k in ks:
                st[k, chip, core] = (st[k, chip, core].astype(F32) + came[k, chip].astype(F32)).astype(BF16)
        start(steps[0][0])

    def heads_step(st, land, ks, steps):
        for step in range(1, len(steps)):
            arrive(steps[step - 1][0])
            for chip, at in steps[step - 1][1]:
                for j, k in enumerate(ks):
                    st[k, chip, core] = (st[k, chip, core].astype(F32) + land[at, j].astype(F32)).astype(BF16)
            start(steps[step][0])

    def heads_last(st, land, ks, steps, held, came):
        arrive(steps[-1][0])
        at = steps[-1][1][0][1]
        for j, k in enumerate(ks):
            held[k] = (st[k, c, core].astype(F32) + land[at, j].astype(F32)).astype(BF16)
        i = row("z")
        copies = [
            remote(held.at[k], came.at[T - k - 1], zs.at[i, k - 1], zr.at[i, T - k - 1], (d, head(k)))
            for k in ks
            if k
        ]
        start(copies)
        return copies

    orders = (x_first, y_first)
    o_heads = [range(g * T // 2, (g + 1) * T // 2) for g in range(2)]
    o_steps = [
        scatter_steps(
            lambda chip, g=g: st_o.at[pl.ds(g * T // 2, T // 2), chip, core], lambda at, g=g: xr_o.at[g, at], orders[g]
        )
        for g in range(2)
    ]
    arrive(st_o_c)
    for g in range(2):
        heads_core(st_o, cr_o, o_heads[g], o_steps[g])

    arrive(do_in)
    fp_z = over_z(lambda k: (fp.at[:, my_rows(k)], fpr.at[k - 1]))
    start(fp_z)
    feed_step(st_up, xr_up, up_g)
    feed_step(st_dn, xr_dn, dn_g)

    def attend_back(s, carry, g):
        rows, lanes, lat_rows = group(g, s)
        keys = kall[rows, lanes]
        queries = spread(qall[lat_rows, lanes])
        grads = spread(joined(g, lambda k: dob[head(k), s]))
        outs = spread(joined(g, lambda k: att[k, s]))
        product = grads.astype(F32) * outs.astype(F32)
        inner = lax.dot_general(
            jnp.ones((8, GI), F32),
            product,
            (((1,), (1,)), ((), ())),
            preferred_element_type=F32,
            precision=lax.Precision.HIGHEST,
        )[:1]
        probs = pall[g * S + s]
        score_grad = (probs * (nt(vall[rows, lanes], grads) - inner)).astype(BF16)
        pairs[rows, lanes] = (nn(score_grad, queries) * scale_factor).astype(BF16)
        pairs[rows, pl.ds(T * I + g * GI, GI)] = nn(probs.astype(BF16), grads).astype(BF16)
        query_grad = (gather_heads(tn(score_grad, keys)) * scale_factor).astype(BF16)
        for j in range(G):
            dqb[g * G + j, s] = query_grad[:, j * I : (j + 1) * I]
        return carry

    def group_weights(g):
        query_part = jnp.concatenate([dqb[g * G + j].reshape(S * L, I) for j in range(G)], axis=1)
        all_rows = pl.ds(0, S * Kt)
        part = jnp.concatenate(
            [pairs[all_rows, pl.ds(g * GI, GI)], pairs[all_rows, pl.ds(T * I + g * GI, GI)]], axis=1
        )
        for b in range(blocks):
            cols = pl.ds(b * BLOCK, BLOCK)
            block = tn(ctx[:, cols], part).astype(BF16)
            query_block = tn(latn[:, cols], query_part).astype(BF16)
            for j in range(G):
                lanes = slice(j * I, (j + 1) * I)
                pieces = (query_block[:, lanes], block[:, lanes], block[:, GI:][:, lanes])
                for m, piece in enumerate(pieces):
                    st_qkv[g * G + j, pl.ds(b * n, n), :, :, pl.ds(m * I, I)] = piece.reshape(n, 2, R, I)
        ks = pl.ds(g * G, G)
        copy = over_core(st_qkv.at[ks, :, other], cr_qkv.at[ks])
        start(copy)
        return copy

    q_steps = [
        scatter_steps(lambda chip, k=k: st_qkv.at[pl.ds(k, 1), chip, core], lambda at, k=k: xr_qkv.at[k, at], orders[k % 2])
        for k in range(T)
    ]
    group_heads = [range(g * G, (g + 1) * G) for g in range(groups)]
    q_c, dq_z = [], []

    def group_core(g):
        arrive(q_c[g])
        for k in group_heads[g]:
            heads_core(st_qkv, cr_qkv, (k,), q_steps[k])

    def group_step(g):
        for k in group_heads[g]:
            heads_step(st_qkv, xr_qkv.at[k], (k,), q_steps[k])

    def group_last(g):
        out = []
        for k in group_heads[g]:
            out += heads_last(st_qkv, xr_qkv.at[k], (k,), q_steps[k], zb_qkv, zr_qkv)
        return out

    for g in range(groups):
        lax.fori_loop(0, S, functools.partial(attend_back, g=g), 0, unroll=2)
        for j in range(G):
            k = g * G + j
            now = over_z(lambda m, k=k: (dqb.at[k, :, my_rows(m), :], dqr.at[m - 1, (m + k) % T]))
            start(now)
            dq_z += now
        if g:
            group_core(g - 1)
        q_c.append(group_weights(g))
    for g in range(2):
        heads_step(st_o, xr_o.at[g], o_heads[g], o_steps[g])

    acc[...] = jnp.zeros_like(acc)

    def width(s, rows):
        return jnp.concatenate([pall[s % 2 * blocks + b, rows, :] for b in range(blocks)], axis=1)

    def media_width(s):
        for b in range(blocks):
            weights = jnp.concatenate(
                [
                    wq_b[k, pl.ds(b * n, n), :, :, pl.ds(m * I, I)].reshape(BLOCK, I)
                    for m in (1, 2)
                    for k in range(T)
                ],
                axis=1,
            )
            pall[s % 2 * blocks + b] = nt(pairs[pl.ds(s * Kt, Kt), pl.ds(0, 2 * T * I)], weights)

    def media_rows(s):
        for b in range(Mt // ROWS):
            rows = pl.ds(b * ROWS, ROWS)
            unit, scale_inv = unit_rows(mown[s, rows, :].astype(F32))
            upstream = width(s, rows)
            mown[s, rows, :] = norm_back(unit, scale_inv, mgain[...], upstream).astype(BF16)
            acc[0] += fold(upstream * unit)
            acc[1] += fold(upstream)
        mgl[pl.ds(s * Lt, Lt), :] = width(s, pl.ds(Mt, Lt))
        pltpu.make_async_copy(mown.at[s], media_grad.at[s], osem.at[s]).start()

    media_width(0)
    for s in range(S):
        if s + 1 < S:
            media_width(s + 1)
        media_rows(s)
        if s == 0:
            group_core(groups - 1)
        if s == S // 2:
            for g in range(groups - 1):
                group_step(g)

    arrive(fp_z)
    for s in range(S):
        own = pl.ds(pl.multiple_of(s * L + t * Lt, Lt), Lt)
        total = fp[s, my_rows(), :].astype(F32)
        for k in range(1, T):
            total = total + fpr[k - 1, s].astype(F32)
        new_lat[s, my_rows(), :] = (res[own, :] + total).astype(BF16)
    nl_hop, nl_end = line_share(lambda rows: new_lat.at[:, rows, :])
    nl_hop(1)
    o_z = []
    for g in range(2):
        o_z += heads_last(st_o, xr_o.at[g], o_heads[g], o_steps[g], zb_o, zr_o)

    arrive(dq_z)
    upstream_all = mgl[...]
    for k in range(T):
        total = dqb[k, :, my_rows(), :].astype(F32)
        for m in range(1, T):
            total = total + dqr[m - 1, k].astype(F32)
        weights = wq_b[k, :, :, :, pl.ds(0, I)].reshape(D, I)
        upstream_all = upstream_all + nt(total.astype(BF16).reshape(S * Lt, I), weights)
    mgl[...] = upstream_all
    lat_gain_part = jnp.zeros((1, D), F32)
    lat_shift_part = jnp.zeros((1, D), F32)
    for s in range(S):
        own = pl.ds(pl.multiple_of(s * L + t * Lt, Lt), Lt)
        unit, scale_inv = unit_rows(lat[own, :].astype(F32))
        upstream = mgl[pl.ds(s * Lt, Lt), :]
        back = rgr[pl.ds(s * Lt, Lt), :] + norm_back(unit, scale_inv, lgain[...], upstream)
        lat_grad[s, my_rows(), :] = back.astype(BF16)
        lat_gain_part = lat_gain_part + jnp.sum(upstream * unit, axis=0, keepdims=True)
        lat_shift_part = lat_shift_part + jnp.sum(upstream, axis=0, keepdims=True)
    lg_hop, lg_end = line_share(lambda rows: lat_grad.at[:, rows, :])
    lg_hop(1)

    vst[...] += jnp.concatenate(
        [
            jnp.sum(acc[0], axis=0, keepdims=True),
            jnp.sum(acc[1], axis=0, keepdims=True),
            lat_gain_part,
            lat_shift_part,
            jnp.zeros((4, D), F32),
        ],
        axis=0,
    )
    vec_c = over_core(vst, vcr)
    start(vec_c)
    arrive(vec_c)
    vx[c] = vst[...] + vcr[...]
    vec_row = row("x")

    def vec_x(j, chip):
        return remote(vx.at[chip], vx.at[chip], xs.at[vec_row, j - 1], xr.at[vec_row, j - 1], x_dev(j))

    lax.fori_loop(1, C, lambda j, carry: (vec_x(j, c).start(), carry)[1], 0)

    group_step(groups - 1)
    nl_hop(2)
    q_z = []
    for g in range(groups - 1):
        q_z += group_last(g)
    feed_last(st_up, xr_up, up_g, g_up)
    feed_last(st_dn, xr_dn, dn_g, g_dn)
    lax.fori_loop(1, C, lambda j, carry: (vec_x(j, lax.rem(c - j + C, C)).wait_recv(), carry)[1], 0)
    vz[t] = lax.fori_loop(1, C, lambda j, value: value + vx[j], vx[0])
    v_z = over_z(lambda k: (vz.at[t], vz.at[t]))
    i = count["z"] - 1
    v_in = [remote(vz.at[head(k)], vz.at[head(k)], zs.at[i, k - 1], zr.at[i, k - 1], z_dev(k)) for k in range(1, T)]
    start(v_z)
    lg_hop(2)
    q_z += group_last(groups - 1)
    for h in range(3, T):
        nl_hop(h)
        lg_hop(h)
    arrive(v_in)
    g_vec[...] = lax.fori_loop(1, T, lambda k, value: value + vz[k], vz[0])
    arrive(o_z)
    total = zb_o[0].astype(F32)
    for k in range(1, T):
        total = total + zr_o[k - 1].astype(F32)
    g_o[...] = total
    arrive(q_z)
    total = zb_qkv[0].astype(F32)
    for k in range(1, T):
        total = total + zr_qkv[k - 1].astype(F32)
    g_qkv[...] = total

    nl_end()
    lg_end()
    for copy in started:
        copy.wait_send()
    lax.fori_loop(1, C, lambda j, carry: (vec_x(j, c).wait_send(), carry)[1], 0)
    for s in range(S):
        pltpu.make_async_copy(mown.at[s], media_grad.at[s], osem.at[s]).wait()


def hand_out(z, new_lat, media_grad, lat_grad, g_qkv, g_o, g_up, g_dn, g_vec, *refs):
    outs, held, sem_in, sem_out = refs[:15], refs[15], refs[16], refs[17]
    loads = [pltpu.make_async_copy(media_grad.at[s], held.at[s], sem_in.at[s]) for s in range(z.S)]
    stores = [pltpu.make_async_copy(held.at[s], outs[1].at[s], sem_out.at[s]) for s in range(z.S)]
    for copy in loads:
        copy.start()
    for load, store in zip(loads, stores):
        load.wait()
        store.start()
    outs[0][...] = new_lat[...]
    outs[2][...] = lat_grad[...]
    for m in range(3):
        outs[3 + m][...] = g_qkv[:, pl.ds(m * z.I, z.I)]
    outs[6][...] = g_o[...].T
    outs[7][...] = g_up[...]
    outs[8][...] = g_dn[...].T
    outs[9][...] = g_vec[pl.ds(0, 1), :]
    outs[10][...] = g_vec[pl.ds(1, 1), :]
    first = lax.axis_index("dp") * z.R
    row = lax.broadcasted_iota(jnp.int32, (z.D, z.R), 0)
    col = lax.broadcasted_iota(jnp.int32, (z.D, z.R), 1)
    pick = jnp.where(row == col + first, 1.0, 0.0).astype(F32)
    own = lax.dot_general(
        g_vec[...], pick, (((1,), (0,)), ((), ())), preferred_element_type=F32, precision=lax.Precision.HIGHEST
    )
    for m in range(4):
        outs[11 + m][...] = own[2 + m : 3 + m]
    for store in stores:
        store.wait()


def solution(mesh):
    T, N = mesh.shape["tensor"], mesh.shape["dp"]

    def on_device(
        media_tokens,
        latents,
        image_counts,
        media_gain,
        media_shift,
        latent_gain,
        latent_shift,
        feed_gain,
        feed_shift,
        query_weight,
        key_weight,
        value_weight,
        output_weight,
        up_weight,
        down_weight,
        cotangent,
    ):
        samples, slots, width = media_tokens.shape
        z = Sizes(T, N, samples, latents.shape[1], slots, width, up_weight.shape[1], query_weight.shape[1])
        S, L, D, F, I, R, C = z.S, z.L, z.D, z.F, z.I, z.R, z.C
        row = lambda v: v.reshape(1, D)
        vmem = pl.BlockSpec(memory_space=pltpu.VMEM)
        hbm = pl.BlockSpec(memory_space=pl.ANY)
        V = pltpu.VMEM
        scratch = [
            V((T, C, 2, R, 3 * I), BF16),
            V((T, C, 2, R, I), BF16),
            V((C, 2, R, F), BF16),
            V((C, 2, R, F), BF16),
            V((SLOTS_IN_FLIGHT, z.Mt, D), BF16),
            V((S, z.Mt, D), BF16),
            V((2, z.Mt, D), BF16),
            V((S * z.Kt, D), BF16),
            V((S * L, D), BF16),
            V((T, S, L, I), BF16),
            V((T, max(S, 8), z.q), F32),
            V((S * L, T * I), BF16),
            V((S * z.Kt, T * I), BF16),
            V((S * z.Kt, T * I), BF16),
            V((max(T // z.G * S, 2 * D // BLOCK), z.Kt, z.G * z.q), F32),
            V((max(z.K, S * z.Kt), max(S, T) * 2 * I), BF16),
            V((S * L, D), F32),
            V((S * L, D), BF16),
            V((S * L, F), BF16),
            V((S * L, F), BF16),
            V((S, L, D), BF16),
            V((T - 1, S, z.Lt, D), BF16),
            V((S, L, D), BF16),
            V((T - 1, S, z.Lt, D), BF16),
            V((S * z.Lt, D), BF16),
            V((S * z.Lt, D), F32),
            V((T, S, L, I), BF16),
            V((T, S, L, I), BF16),
            V((T - 1, T, S, z.Lt, I), BF16),
            V((C, 2, R, F), BF16),
            V((C, 2, R, F), BF16),
            V((T, C, 2, R, I), BF16),
            V((T, C, 2, R, 3 * I), BF16),
            V((C, R, F), BF16),
            V((C, R, F), BF16),
            V((T, C, R, I), BF16),
            V((T, C, R, 3 * I), BF16),
            V((max(C - 1, 1), R, F), BF16),
            V((max(C - 1, 1), R, F), BF16),
            V((2, max(C - 1, 1), T // 2, R, I), BF16),
            V((T, max(C - 1, 1), 1, R, 3 * I), BF16),
            V((T, R, I), BF16),
            V((T, R, 3 * I), BF16),
            V((T - 1, R, I), BF16),
            V((T - 1, R, 3 * I), BF16),
            V((S * z.Lt, D), F32),
            V((2, 8, D), F32),
            V((8, D), F32),
            V((8, D), F32),
            V((C, 8, D), F32),
            V((T, 8, D), F32),
            pltpu.SemaphoreType.DMA((SLOTS_IN_FLIGHT + 1,)),
            pltpu.SemaphoreType.DMA((S,)),
            pltpu.SemaphoreType.DMA((26, T - 1)),
            pltpu.SemaphoreType.DMA((26, T - 1)),
            pltpu.SemaphoreType.DMA((14, max(C - 1, 1))),
            pltpu.SemaphoreType.DMA((14, max(C - 1, 1))),
            pltpu.SemaphoreType.DMA((10,)),
            pltpu.SemaphoreType.DMA((10,)),
        ]
        shape = jax.ShapeDtypeStruct
        outs = pl.pallas_call(
            functools.partial(layer_kernel, z),
            out_shape=[
                shape((S, L, D), BF16),
                shape((S, z.Mt, D), BF16),
                shape((S, L, D), BF16),
                shape((R, 3 * I), F32),
                shape((R, I), F32),
                shape((R, F), F32),
                shape((R, F), F32),
                shape((8, D), F32),
            ],
            in_specs=[pl.BlockSpec(memory_space=pltpu.SMEM), hbm] + [vmem] * 14,
            out_specs=[vmem, hbm] + [vmem] * 6,
            scratch_shapes=scratch,
            compiler_params=pltpu.CompilerParams(
                collective_id=0, has_side_effects=True, vmem_limit_bytes=63 * 1024 * 1024
            ),
            name="resampler_layer",
        )(
            image_counts,
            media_tokens,
            latents.reshape(S * L, D),
            cotangent.reshape(S * L, D),
            row(media_gain),
            row(media_shift),
            row(latent_gain),
            row(latent_shift),
            row(feed_gain),
            row(feed_shift),
            query_weight,
            key_weight,
            value_weight,
            output_weight,
            up_weight,
            down_weight,
        )
        final = pl.pallas_call(
            functools.partial(hand_out, z),
            out_shape=[
                shape((S, L, D), BF16),
                shape((S, z.Mt, D), BF16),
                shape((S, L, D), BF16),
                shape((R, I), F32),
                shape((R, I), F32),
                shape((R, I), F32),
                shape((I, R), F32),
                shape((R, F), F32),
                shape((F, R), F32),
                shape((1, D), F32),
                shape((1, D), F32),
            ]
            + [shape((1, R), F32)] * 4,
            in_specs=[vmem, hbm] + [vmem] * 6,
            out_specs=[vmem, hbm] + [vmem] * 13,
            scratch_shapes=[V((S, z.Mt, D), BF16), pltpu.SemaphoreType.DMA((S,)), pltpu.SemaphoreType.DMA((S,))],
            name="hand_out",
        )(*outs)
        return tuple(final[:9]) + tuple(v.reshape(-1) for v in final[9:])

    placed = (
        P("dp", None, None),
        P("dp", None, None),
        P("dp"),
        P(),
        P(),
        P(),
        P(),
        P(),
        P(),
        P(None, "tensor"),
        P(None, "tensor"),
        P(None, "tensor"),
        P("tensor", None),
        P("dp", "tensor"),
        P("tensor", "dp"),
        P("dp", None, None),
    )
    return jax.shard_map(
        on_device,
        mesh=mesh,
        in_specs=placed,
        out_specs=(
            P("dp", None, None),
            P("dp", "tensor", None),
            P("dp", None, None),
            P("dp", "tensor"),
            P("dp", "tensor"),
            P("dp", "tensor"),
            P("tensor", "dp"),
            P("dp", "tensor"),
            P("tensor", "dp"),
            P(),
            P(),
            P("dp"),
            P("dp"),
            P("dp"),
            P("dp"),
        ),
        check_vma=False,
    )
```

```python
import functools

import jax
import jax.numpy as jnp
from jax import lax
from jax.experimental import pallas as pl
from jax.experimental.pallas import tpu as pltpu
from jax.sharding import PartitionSpec as P

HEAD_DIM = 64
PATCH = 256
EPSILON = 1e-05
NEGATIVE = -1e30
SQRT_HALF = 0.7071067811865476
INV_ROOT_TWO_PI = 0.3989422804014327
F32 = jnp.float32
BF16 = jnp.bfloat16
MESH = pl.DeviceIdType.MESH
BLOCK = 256
ROWS = 32
SLOTS_IN_FLIGHT = 3


def nn(left, right):
    return lax.dot_general(left, right, (((1,), (0,)), ((), ())), preferred_element_type=F32)


def nt(left, right):
    return lax.dot_general(left, right, (((1,), (1,)), ((), ())), preferred_element_type=F32)


def tn(left, right):
    return lax.dot_general(left, right, (((0,), (0,)), ((), ())), preferred_element_type=F32)


def unit_rows(x):
    centre = x - jnp.mean(x, axis=-1, keepdims=True)
    scale_inv = lax.rsqrt(jnp.mean(centre * centre, axis=-1, keepdims=True) + EPSILON)
    return centre * scale_inv, scale_inv


def norm_back(unit, scale_inv, gain, upstream):
    scaled = upstream * gain
    inner = scaled - jnp.mean(scaled, axis=-1, keepdims=True)
    inner = inner - unit * jnp.mean(scaled * unit, axis=-1, keepdims=True)
    return inner * scale_inv


def fold(x):
    return jnp.sum(x.reshape(x.shape[0] // 8, 8, x.shape[1]), axis=0)


class Sizes:
    def __init__(self, tensor, dp, samples, lat, slots, width, hidden, inner):
        self.T, self.N, self.C = tensor, dp, dp // 2
        self.S, self.L, self.M, self.D = samples, lat, slots, width
        self.F, self.I = hidden, inner
        self.R = width // dp
        self.Lt, self.Mt = lat // tensor, slots // tensor
        self.Kt = self.Lt + self.Mt
        self.K = lat + slots
        self.H = inner // HEAD_DIM
        self.q = self.H * lat
        self.G = min(2, tensor)


def layer_kernel(
    z,
    counts,
    media,
    lat_h,
    cot_h,
    mgain,
    mshift,
    lgain,
    lshift,
    fgain,
    fshift,
    wq,
    wk,
    wv,
    wo,
    up,
    dn,
    new_lat,
    media_grad,
    lat_grad,
    g_qkv,
    g_o,
    g_up,
    g_dn,
    g_vec,
    lat,
    cot,
    dn_v,
    wo_v,
    wq_b,
    wo_b,
    up_b,
    dn_b,
    mbuf,
    mown,
    xn,
    ctx,
    latn,
    att,
    lse,
    qall,
    kall,
    vall,
    pall,
    pairs,
    res,
    hin,
    act,
    bgr,
    hg,
    hgr,
    fp,
    fpr,
    og,
    rgr,
    dob,
    dqb,
    dqr,
    st_up,
    st_dn,
    st_o,
    st_qkv,
    cr_up,
    cr_dn,
    cr_o,
    cr_qkv,
    xr_up,
    xr_dn,
    xr_o,
    xr_qkv,
    zb_o,
    zb_qkv,
    zr_o,
    zr_qkv,
    mgl,
    acc,
    vst,
    vcr,
    vx,
    vz,
    lsem,
    msem,
    osem,
    zs,
    zr,
    xs,
    xr,
    cs,
    cr,
):
    T, N, C, S, L, M, D = z.T, z.N, z.C, z.S, z.L, z.M, z.D
    F, I, R, Lt, Mt, Kt, G = z.F, z.I, z.R, z.Lt, z.Mt, z.Kt, z.G
    GI = G * I
    groups = T // G
    scale_factor = HEAD_DIM ** (-0.5)
    t = lax.axis_index("tensor")
    d = lax.axis_index("dp")
    c = lax.div(d, 2)
    core = lax.rem(d, 2)
    other = 1 - core
    n = BLOCK // (2 * R)
    blocks = D // BLOCK
    count = {"z": 0, "x": 0, "c": 0}
    started = []

    def row(kind):
        count[kind] += 1
        return count[kind] - 1

    def start(copies):
        for copy in copies:
            copy.start()
        started.extend(copies)

    def arrive(copies):
        for copy in copies:
            copy.wait_recv()

    def z_dev(k):
        return (d, lax.rem(t + k, T))

    def x_dev(j):
        return (2 * lax.rem(c + j, C) + core, t)

    core_dev = (d + 1 - 2 * core, t)

    def head(k):
        return lax.rem(t - k + T, T)

    def my_rows(k=0):
        return pl.ds(pl.multiple_of(lax.rem(t + k, T) * Lt, Lt), Lt)

    def remote(src, dst, send, recv, dev):
        return pltpu.make_async_remote_copy(
            src_ref=src, dst_ref=dst, send_sem=send, recv_sem=recv, device_id=dev, device_id_type=MESH
        )

    def over_z(pick):
        i = row("z")
        return [remote(*pick(k), zs.at[i, k - 1], zr.at[i, k - 1], z_dev(k)) for k in range(1, T)]

    def share_rows(pick):
        out = over_z(lambda k: (pick(my_rows()), pick(my_rows())))
        i = count["z"] - 1
        came = [
            remote(pick(my_rows(T - k)), pick(my_rows(T - k)), zs.at[i, k - 1], zr.at[i, k - 1], z_dev(k))
            for k in range(1, T)
        ]
        return out, came

    def line_share(pick):
        ways = []
        for step in (1, -1):
            i = row("z")
            hops = []
            for h in range(1, T):
                owner, fresh = t - step * (h - 1), t - step * h
                beyond = t + step
                sends = (owner >= 0) & (owner < T) & (beyond >= 0) & (beyond < T)
                comes = (fresh >= 0) & (fresh < T)
                mine, theirs = pick(my_rows(T - step * (h - 1))), pick(my_rows(T - step * h))
                dev = (d, lax.rem(t + step + T, T))
                sems = (zs.at[i, h - 1], zr.at[i, h - 1])
                hops.append((sends, remote(mine, mine, *sems, dev), comes, remote(theirs, theirs, *sems, dev)))
            ways.append(hops)

        def hop(h, last=False):
            if h >= T and not last:
                return
            for hops in ways:
                if h > 1:
                    pl.when(hops[h - 2][2])(hops[h - 2][3].wait_recv)
                if h < T:
                    pl.when(hops[h - 1][0])(hops[h - 1][1].start)

        def end():
            hop(T, last=True)
            for hops in ways:
                for sends, copy, _, _ in hops:
                    pl.when(sends)(copy.wait_send)

        return hop, end

    def over_core(src, dst):
        i = row("c")
        return [remote(src, dst, cs.at[i], cr.at[i], core_dev)]

    bits = C.bit_length() - 1
    x_first = list(range(bits))
    y_first = x_first[::-1]

    def flip(chip, mask):
        for bit in range(bits):
            if mask >> bit & 1:
                chip = chip + (1 - 2 * lax.rem(lax.div(chip, 1 << bit), 2)) * (1 << bit)
        return chip

    def subsets(order):
        masks = [0]
        for bit in order:
            masks = masks + [m | 1 << bit for m in masks]
        return masks

    def gather_steps(view, order):
        i, at, rests = row("x"), 0, []
        firsts = ([], [])
        for step, bit in enumerate(order):
            peer = flip(c, 1 << bit)
            dev = (2 * peer + core, t)
            rest = ([], [])
            for m in subsets(order[:step]):
                sems = (xs.at[i, at], xr.at[i, at])
                mine, theirs = view(flip(c, m)), view(flip(peer, m))
                out, came = rest if m else firsts
                out.append(remote(mine, mine, *sems, dev))
                came.append(remote(theirs, theirs, *sems, dev))
                at += 1
            if step:
                rests.append(rest)
        return firsts, rests

    def gather_rest(gather):
        firsts, rests = gather
        for step, rest in enumerate(rests):
            arrive([firsts[1][step]])
            if step:
                arrive(rests[step - 1][1])
            start(rest[0])

    def gather_near(gather):
        arrive([gather[0][1][-1]])

    def gather_done(gather):
        if gather[1]:
            arrive(gather[1][-1][1])

    def scatter_steps(view, land, order):
        i, at, steps = row("x"), 0, []
        for step, bit in enumerate(order):
            peer = flip(c, 1 << bit)
            dev = (2 * peer + core, t)
            out, keep = [], []
            for m in subsets(order[step + 1 :]):
                out.append(remote(view(flip(peer, m)), land(at), xs.at[i, at], xr.at[i, at], dev))
                keep.append((flip(c, m), at))
                at += 1
            steps.append((out, keep))
        return steps

    n_tiles = S * T

    def tile_copy(i):
        slot = lax.rem(i, SLOTS_IN_FLIGHT)
        s, r = lax.div(i, T), lax.rem(i, T)
        return pltpu.make_async_copy(
            media.at[s, pl.ds(pl.multiple_of(r * Mt, Mt), Mt)], mbuf.at[slot], msem.at[slot]
        )

    own_copy = pltpu.make_async_copy(
        media.at[:, pl.ds(pl.multiple_of(t * Mt, Mt), Mt)], mown, msem.at[SLOTS_IN_FLIGHT]
    )
    barrier = pltpu.get_barrier_semaphore()

    def greet(dev):
        pl.semaphore_signal(barrier, inc=1, device_id=dev, device_id_type=MESH)

    for k in range(1, T):
        greet(z_dev(k))
    lax.fori_loop(1, C, lambda j, carry: (greet(x_dev(j)), carry)[1], 0)
    greet(core_dev)
    loads = [
        pltpu.make_async_copy(src, dst, lsem.at[i])
        for i, (src, dst) in enumerate(
            [(up, up_b.at[c, core]), (dn, dn_v), (wo, wo_v)]
            + [(w, wq_b.at[0, :, :, :, pl.ds(m * I, I)]) for m, w in enumerate((wq, wk, wv))]
            + [(lat_h, lat), (cot_h, cot)]
        )
    ]
    for copy in loads:
        copy.start()
    for i in range(min(SLOTS_IN_FLIGHT, n_tiles)):
        tile_copy(i).start()
    for copy in loads[:3]:
        copy.wait()
    dn_b[c, core] = dn_v[...].T
    wo_b[0] = wo_v[...].T.reshape(C, 2, R, I)
    pl.semaphore_wait(barrier, T + C - 1)

    foreign = pl.ds(1, T - 1)
    up_x = gather_steps(lambda chip: up_b.at[chip, core], x_first)
    dn_x = gather_steps(lambda chip: dn_b.at[chip, core], y_first)
    wo_x = gather_steps(lambda chip: wo_b.at[foreign, chip, core], x_first)
    qk_x = gather_steps(lambda chip: wq_b.at[foreign, chip, core, :, pl.ds(0, 2 * I)], x_first)
    v_x = gather_steps(lambda chip: wq_b.at[foreign, chip, core, :, pl.ds(2 * I, I)], y_first)
    wo_z = over_z(lambda k: (wo_b.at[0, c, core], wo_b.at[k, c, core]))
    wq_z = over_z(lambda k: (wq_b.at[0, c, core], wq_b.at[k, c, core]))
    near = [0] + [1 << bit for bit in range(bits)]
    far = [m for m in range(C) if m not in near]

    def relay(ref, masks):
        return [copy for m in masks for copy in over_core(ref.at[flip(c, m), core], ref.at[flip(c, m), core])]

    feed_near = relay(up_b, near) + relay(dn_b, near)
    feed_far = relay(up_b, far) + relay(dn_b, far)
    wo_c = over_core(wo_b.at[foreign, :, core], wo_b.at[foreign, :, core])
    wq_c = over_core(wq_b.at[foreign, :, core], wq_b.at[foreign, :, core])

    for way in range(bits):
        start([up_x[0][0][way], dn_x[0][0][way]])
    start(wo_z)
    for copy in loads[3:]:
        copy.wait()
    start(wq_z)
    own_copy.start()

    for b in range(S * L // ROWS):
        rows = pl.ds(b * ROWS, ROWS)
        unit, _ = unit_rows(lat[rows, :].astype(F32))
        latn[rows, :] = (unit * lgain[...] + lshift[...]).astype(BF16)
    own_qkv = nn(latn[...], wq_b[0].reshape(D, 3 * I)).astype(BF16)
    qall[:, pl.ds(0, I)] = own_qkv[:, :I]
    for s in range(S):
        pairs[pl.ds(M, L), pl.ds(s * 2 * I, 2 * I)] = own_qkv[s * L : (s + 1) * L, I:]
        ctx[pl.ds(s * Kt + Mt, Lt), :] = latn[pl.ds(pl.multiple_of(s * L + t * Lt, Lt), Lt), :]

    def tile_norm(i, half):
        slot = lax.rem(i, SLOTS_IN_FLIGHT)
        for b in range(Mt // ROWS):
            rows = pl.ds(b * ROWS, ROWS)
            unit, _ = unit_rows(mbuf[slot, rows, :].astype(F32))
            xn[half, rows, :] = (unit * mgain[...] + mshift[...]).astype(BF16)

    def tile_pair(i, half):
        s, r = lax.div(i, T), lax.rem(i, T)
        pair = nn(xn[half], wq_b[0, :, :, :, pl.ds(I, 2 * I)].reshape(D, 2 * I))
        lanes = pl.ds(pl.multiple_of(s * 2 * I, 2 * I), 2 * I)
        pairs[pl.ds(pl.multiple_of(r * Mt, Mt), Mt), lanes] = pair.astype(BF16)

    def tile_keep(i, half):
        s, r = lax.div(i, T), lax.rem(i, T)

        @pl.when(r == t)
        def _():
            ctx[pl.ds(pl.multiple_of(s * Kt, 16), Mt), :] = xn[half]

    def tile_next(i):
        @pl.when(i + SLOTS_IN_FLIGHT < n_tiles)
        def _():
            tile_copy(i + SLOTS_IN_FLIGHT).start()

    tile_copy(0).wait()
    tile_norm(0, 0)
    tile_next(0)

    def two_tiles(j, carry):
        i = 2 * j
        tile_copy(i + 1).wait()

        @pl.when(i + 2 < n_tiles)
        def _():
            tile_copy(i + 2).wait()

        tile_keep(i, 0)
        tile_pair(i, 0)
        tile_norm(i + 1, 1)
        tile_keep(i + 1, 1)
        tile_pair(i + 1, 1)
        tile_norm(lax.rem(i + 2, n_tiles), 0)
        tile_next(i + 1)
        tile_next(i + 2)
        return carry

    first = n_tiles // 8
    lax.fori_loop(0, first, two_tiles, 0)
    arrive(wo_z)
    start(wo_x[0][0])
    lax.fori_loop(first, n_tiles // 2, two_tiles, 0)
    gather_rest(up_x)
    gather_rest(dn_x)
    gather_rest(wo_x)

    def spread(x):
        lane_head = lax.broadcasted_iota(jnp.int32, (1, x.shape[1]), 1) // HEAD_DIM
        zero = jnp.zeros_like(x)
        return jnp.concatenate(
            [jnp.where(lane_head == h, x, zero) for h in range(x.shape[1] // HEAD_DIM)], axis=0
        )

    def gather_heads(x):
        lane_head = lax.broadcasted_iota(jnp.int32, (1, x.shape[1]), 1) // HEAD_DIM
        out = x[:L]
        for h in range(1, x.shape[1] // HEAD_DIM):
            out = jnp.where(lane_head == h, x[h * L : (h + 1) * L], out)
        return out

    att_z = []
    for s in range(S):
        keys = pairs[pl.ds(0, z.K), pl.ds(s * 2 * I, I)]
        values = pairs[pl.ds(0, z.K), pl.ds(s * 2 * I + I, I)]
        scores = nt(keys, spread(qall[pl.ds(s * L, L), pl.ds(0, I)])) * scale_factor
        slot = lax.broadcasted_iota(jnp.int32, (z.K, 1), 0)
        valid = (slot < counts[s] * PATCH) | (slot >= M)
        scores = jnp.where(valid, scores, NEGATIVE)
        largest = jnp.max(scores, axis=0, keepdims=True)
        total = largest + jnp.log(jnp.sum(jnp.exp(scores - largest), axis=0, keepdims=True))
        probs = jnp.exp(scores - total).astype(BF16)
        att[0, s] = gather_heads(tn(probs, values)).astype(BF16)
        lse[0, pl.ds(s, 1), :] = total
        if s % 2 == 1:
            now = over_z(lambda k, s=s: (att.at[0, pl.ds(s - 1, 2)], att.at[k, pl.ds(s - 1, 2)]))
            start(now)
            att_z += now
    lse_z = over_z(lambda k: (lse.at[0], lse.at[k]))
    start(lse_z)

    for s in range(S):
        lanes = s * 2 * I
        own_slots = pl.ds(pl.multiple_of(t * Mt, Mt), Mt)
        own_lat = pl.ds(pl.multiple_of(M + t * Lt, Lt), Lt)
        for m, ref in enumerate((kall, vall)):
            ref[pl.ds(s * Kt, Mt), pl.ds(0, I)] = pairs[own_slots, pl.ds(lanes + m * I, I)]
            ref[pl.ds(s * Kt + Mt, Lt), pl.ds(0, I)] = pairs[own_lat, pl.ds(lanes + m * I, I)]
    gather_near(wo_x)
    gather_near(up_x)
    gather_near(dn_x)
    start(feed_near)
    gather_done(wo_x)
    start(wo_c)
    arrive(wq_z)
    gather_done(up_x)
    gather_done(dn_x)
    start(feed_far)
    start(qk_x[0][0])
    start(v_x[0][0])

    def heads_wo():
        return jnp.concatenate([wo_b[k].reshape(D, I) for k in range(T)], axis=1)

    arrive(wo_c)
    arrive(att_z)
    att_all = jnp.concatenate([att[k].reshape(S * L, I) for k in range(T)], axis=1)
    res[...] = lat[...].astype(F32) + nt(att_all, heads_wo())
    for b in range(S * L // ROWS):
        rows = pl.ds(b * ROWS, ROWS)
        unit, _ = unit_rows(res[rows, :])
        hin[rows, :] = (unit * fgain[...] + fshift[...]).astype(BF16)

    arrive(feed_near)
    arrive(feed_far)

    def feed(b, carry):
        cols = pl.ds(pl.multiple_of(b * BLOCK, BLOCK), BLOCK)
        before = nn(hin[...], up_b[:, :, :, cols].reshape(D, BLOCK))
        cdf = 0.5 * (1.0 + lax.erf(before * SQRT_HALF))
        act[:, cols] = (before * cdf).astype(BF16)
        slope = cdf + before * INV_ROOT_TWO_PI * jnp.exp(-0.5 * before * before)
        act_grad = nn(cot[...], dn_b[:, :, :, cols].reshape(D, BLOCK)).astype(BF16)
        bgr[:, cols] = (act_grad.astype(F32) * slope).astype(BF16)
        return carry

    lax.fori_loop(0, F // BLOCK, feed, 0, unroll=2)
    gather_rest(qk_x)
    gather_rest(v_x)

    def back_to_width(left, weight, out, b):
        block = nt(left[...], weight[pl.ds(b * n, n)].reshape(BLOCK, F))
        out[:, :, pl.ds(b * BLOCK, BLOCK)] = block.astype(BF16).reshape(S, L, BLOCK)

    hg_z = []
    for b in range(blocks):
        cols = pl.ds(b * BLOCK, BLOCK)
        back_to_width(bgr, up_b, hg, b)
        now = over_z(lambda k, cols=cols: (hg.at[:, my_rows(k), cols], hgr.at[k - 1, :, :, cols]))
        start(now)
        hg_z += now

    def feed_weights(left, right, out, b):
        block = tn(left[:, pl.ds(b * BLOCK, BLOCK)], right[...]).astype(BF16)
        out[pl.ds(b * n, n)] = block.reshape(n, 2, R, F)

    for b in range(blocks):
        feed_weights(hin, bgr, st_up, b)
    st_up_c = over_core(st_up.at[:, other], cr_up)
    start(st_up_c)
    for b in range(blocks):
        feed_weights(cot, act, st_dn, b)
    st_dn_c = over_core(st_dn.at[:, other], cr_dn)
    start(st_dn_c)
    for b in range(blocks):
        back_to_width(act, dn_b, fp, b)

    up_g = scatter_steps(lambda chip: st_up.at[chip, core], lambda at: xr_up.at[at], y_first)
    dn_g = scatter_steps(lambda chip: st_dn.at[chip, core], lambda at: xr_dn.at[at], x_first)

    def feed_core(copy, st, came, steps):
        arrive(copy)
        sent = steps[0][0]
        for m in subsets(range(bits)):
            chip = flip(c, m)
            st[chip, core] = (st[chip, core].astype(F32) + came[chip].astype(F32)).astype(BF16)
        start(sent)

    def feed_step(st, land, steps):
        for step in range(1, len(steps)):
            arrive(steps[step - 1][0])
            for chip, at in steps[step - 1][1]:
                st[chip, core] = (st[chip, core].astype(F32) + land[at].astype(F32)).astype(BF16)
            start(steps[step][0])

    def feed_last(st, land, steps, out):
        arrive(steps[-1][0])
        out[...] = st[c, core].astype(F32) + land[steps[-1][1][0][1]].astype(F32)

    feed_core(st_up_c, st_up, cr_up, up_g)
    feed_core(st_dn_c, st_dn, cr_dn, dn_g)

    for gather in (qk_x, v_x):
        gather_near(gather)
        gather_done(gather)
    start(wq_c)
    own_copy.wait()
    arrive(wq_c)
    for k in range(1, T):
        qall[:, pl.ds(k * I, I)] = nn(latn[...], wq_b[k, :, :, :, pl.ds(0, I)].reshape(D, I)).astype(BF16)
    half_rows = S * Kt // 2

    def all_pairs(i, carry):
        k = lax.div(i, 2)
        rows = pl.ds(pl.multiple_of(lax.rem(i, 2) * half_rows, 16), half_rows)
        lanes = pl.ds(pl.multiple_of(k * I, I), I)
        pair = nn(ctx[rows, :], wq_b[k, :, :, :, pl.ds(I, 2 * I)].reshape(D, 2 * I)).astype(BF16)
        kall[rows, lanes] = pair[:, :I]
        vall[rows, lanes] = pair[:, I:]
        return carry

    lax.fori_loop(2, 2 * T, all_pairs, 0)
    arrive(lse_z)
    slot_of = lax.broadcasted_iota(jnp.int32, (Kt, 1), 0)

    def group(g, s):
        rows = pl.ds(pl.multiple_of(s * Kt, 16), Kt)
        lat_rows = pl.ds(pl.multiple_of(s * L, L), L)
        return rows, pl.ds(g * GI, GI), lat_rows

    def joined(g, pick):
        return jnp.concatenate([pick(g * G + j) for j in range(G)], axis=1)

    for g in range(groups):

        def probabilities(s, carry, g=g):
            rows, lanes, lat_rows = group(g, s)
            scores = nt(kall[rows, lanes], spread(qall[lat_rows, lanes])) * scale_factor
            valid = (slot_of + t * Mt < counts[s] * PATCH) | (slot_of >= Mt)
            scores = jnp.where(valid, scores, NEGATIVE)
            pall[g * S + s] = jnp.exp(scores - joined(g, lambda k: lse[k, pl.ds(s, 1), :]))
            return carry

        lax.fori_loop(0, S, probabilities, 0, unroll=2)

    arrive(hg_z)
    feed_gain_part = jnp.zeros((1, D), F32)
    feed_shift_part = jnp.zeros((1, D), F32)
    for s in range(S):
        own = pl.ds(pl.multiple_of(s * L + t * Lt, Lt), Lt)
        unit, scale_inv = unit_rows(res[own, :])
        upstream = hg[s, my_rows(), :].astype(F32)
        for k in range(1, T):
            upstream = upstream + hgr[k - 1, s].astype(F32)
        back = cot[own, :].astype(F32) + norm_back(unit, scale_inv, fgain[...], upstream)
        feed_gain_part = feed_gain_part + jnp.sum(upstream * unit, axis=0, keepdims=True)
        feed_shift_part = feed_shift_part + jnp.sum(upstream, axis=0, keepdims=True)
        rgr[pl.ds(s * Lt, Lt), :] = back
        og[pl.ds(s * Lt, Lt), :] = back.astype(BF16)
    vst[...] = jnp.concatenate(
        [jnp.zeros((4, D), F32), feed_gain_part, feed_shift_part, jnp.zeros((2, D), F32)], axis=0
    )
    grads_all = nn(og[...], heads_wo()).astype(BF16)
    for k in range(T):
        dob[head(k), :, my_rows(), :] = grads_all[:, k * I : (k + 1) * I].reshape(S, Lt, I)
    do_z, do_in = share_rows(lambda rows: dob.at[:, :, rows, :])
    start(do_z)

    att_own = jnp.concatenate([att[k, :, my_rows(), :].reshape(S * Lt, I) for k in range(T)], axis=1)
    for b in range(blocks):
        block = tn(og[:, pl.ds(b * BLOCK, BLOCK)], att_own).astype(BF16)
        for k in range(T):
            st_o[k, pl.ds(b * n, n)] = block[:, k * I : (k + 1) * I].reshape(n, 2, R, I)
    st_o_c = over_core(st_o.at[:, :, other], cr_o)
    start(st_o_c)

    def heads_core(st, came, ks, steps):
        for m in subsets(range(bits)):
            chip = flip(c, m)
            for k in ks:
                st[k, chip, core] = (st[k, chip, core].astype(F32) + came[k, chip].astype(F32)).astype(BF16)
        start(steps[0][0])

    def heads_step(st, land, ks, steps):
        for step in range(1, len(steps)):
            arrive(steps[step - 1][0])
            for chip, at in steps[step - 1][1]:
                for j, k in enumerate(ks):
                    st[k, chip, core] = (st[k, chip, core].astype(F32) + land[at, j].astype(F32)).astype(BF16)
            start(steps[step][0])

    def heads_last(st, land, ks, steps, held, came):
        arrive(steps[-1][0])
        at = steps[-1][1][0][1]
        for j, k in enumerate(ks):
            held[k] = (st[k, c, core].astype(F32) + land[at, j].astype(F32)).astype(BF16)
        i = row("z")
        copies = [
            remote(held.at[k], came.at[T - k - 1], zs.at[i, k - 1], zr.at[i, T - k - 1], (d, head(k)))
            for k in ks
            if k
        ]
        start(copies)
        return copies

    orders = (x_first, y_first)
    o_heads = [range(g * T // 2, (g + 1) * T // 2) for g in range(2)]
    o_steps = [
        scatter_steps(
            lambda chip, g=g: st_o.at[pl.ds(g * T // 2, T // 2), chip, core], lambda at, g=g: xr_o.at[g, at], orders[g]
        )
        for g in range(2)
    ]
    arrive(st_o_c)
    for g in range(2):
        heads_core(st_o, cr_o, o_heads[g], o_steps[g])

    arrive(do_in)
    fp_z = over_z(lambda k: (fp.at[:, my_rows(k)], fpr.at[k - 1]))
    start(fp_z)
    feed_step(st_up, xr_up, up_g)
    feed_step(st_dn, xr_dn, dn_g)

    def attend_back(s, carry, g):
        rows, lanes, lat_rows = group(g, s)
        keys = kall[rows, lanes]
        queries = spread(qall[lat_rows, lanes])
        grads = spread(joined(g, lambda k: dob[head(k), s]))
        outs = spread(joined(g, lambda k: att[k, s]))
        product = grads.astype(F32) * outs.astype(F32)
        inner = lax.dot_general(
            jnp.ones((8, GI), F32),
            product,
            (((1,), (1,)), ((), ())),
            preferred_element_type=F32,
            precision=lax.Precision.HIGHEST,
        )[:1]
        probs = pall[g * S + s]
        score_grad = (probs * (nt(vall[rows, lanes], grads) - inner)).astype(BF16)
        pairs[rows, lanes] = (nn(score_grad, queries) * scale_factor).astype(BF16)
        pairs[rows, pl.ds(T * I + g * GI, GI)] = nn(probs.astype(BF16), grads).astype(BF16)
        query_grad = (gather_heads(tn(score_grad, keys)) * scale_factor).astype(BF16)
        for j in range(G):
            dqb[g * G + j, s] = query_grad[:, j * I : (j + 1) * I]
        return carry

    def group_weights(g):
        query_part = jnp.concatenate([dqb[g * G + j].reshape(S * L, I) for j in range(G)], axis=1)
        all_rows = pl.ds(0, S * Kt)
        part = jnp.concatenate(
            [pairs[all_rows, pl.ds(g * GI, GI)], pairs[all_rows, pl.ds(T * I + g * GI, GI)]], axis=1
        )
        for b in range(blocks):
            cols = pl.ds(b * BLOCK, BLOCK)
            block = tn(ctx[:, cols], part).astype(BF16)
            query_block = tn(latn[:, cols], query_part).astype(BF16)
            for j in range(G):
                lanes = slice(j * I, (j + 1) * I)
                pieces = (query_block[:, lanes], block[:, lanes], block[:, GI:][:, lanes])
                for m, piece in enumerate(pieces):
                    st_qkv[g * G + j, pl.ds(b * n, n), :, :, pl.ds(m * I, I)] = piece.reshape(n, 2, R, I)
        ks = pl.ds(g * G, G)
        copy = over_core(st_qkv.at[ks, :, other], cr_qkv.at[ks])
        start(copy)
        return copy

    q_steps = [
        scatter_steps(lambda chip, k=k: st_qkv.at[pl.ds(k, 1), chip, core], lambda at, k=k: xr_qkv.at[k, at], orders[k % 2])
        for k in range(T)
    ]
    group_heads = [range(g * G, (g + 1) * G) for g in range(groups)]
    q_c, dq_z = [], []

    def group_core(g):
        arrive(q_c[g])
        for k in group_heads[g]:
            heads_core(st_qkv, cr_qkv, (k,), q_steps[k])

    def group_step(g):
        for k in group_heads[g]:
            heads_step(st_qkv, xr_qkv.at[k], (k,), q_steps[k])

    def group_last(g):
        out = []
        for k in group_heads[g]:
            out += heads_last(st_qkv, xr_qkv.at[k], (k,), q_steps[k], zb_qkv, zr_qkv)
        return out

    for g in range(groups):
        lax.fori_loop(0, S, functools.partial(attend_back, g=g), 0, unroll=2)
        for j in range(G):
            k = g * G + j
            now = over_z(lambda m, k=k: (dqb.at[k, :, my_rows(m), :], dqr.at[m - 1, (m + k) % T]))
            start(now)
            dq_z += now
        if g:
            group_core(g - 1)
        q_c.append(group_weights(g))
    for g in range(2):
        heads_step(st_o, xr_o.at[g], o_heads[g], o_steps[g])

    acc[...] = jnp.zeros_like(acc)

    def width(s, rows):
        return jnp.concatenate([pall[s % 2 * blocks + b, rows, :] for b in range(blocks)], axis=1)

    def media_width(s):
        for b in range(blocks):
            weights = jnp.concatenate(
                [
                    wq_b[k, pl.ds(b * n, n), :, :, pl.ds(m * I, I)].reshape(BLOCK, I)
                    for m in (1, 2)
                    for k in range(T)
                ],
                axis=1,
            )
            pall[s % 2 * blocks + b] = nt(pairs[pl.ds(s * Kt, Kt), pl.ds(0, 2 * T * I)], weights)

    def media_rows(s):
        for b in range(Mt // ROWS):
            rows = pl.ds(b * ROWS, ROWS)
            unit, scale_inv = unit_rows(mown[s, rows, :].astype(F32))
            upstream = width(s, rows)
            mown[s, rows, :] = norm_back(unit, scale_inv, mgain[...], upstream).astype(BF16)
            acc[0] += fold(upstream * unit)
            acc[1] += fold(upstream)
        mgl[pl.ds(s * Lt, Lt), :] = width(s, pl.ds(Mt, Lt))
        pltpu.make_async_copy(mown.at[s], media_grad.at[s], osem.at[s]).start()

    media_width(0)
    for s in range(S):
        if s + 1 < S:
            media_width(s + 1)
        media_rows(s)
        if s == 0:
            group_core(groups - 1)
        if s == S // 2:
            for g in range(groups - 1):
                group_step(g)

    arrive(fp_z)
    for s in range(S):
        own = pl.ds(pl.multiple_of(s * L + t * Lt, Lt), Lt)
        total = fp[s, my_rows(), :].astype(F32)
        for k in range(1, T):
            total = total + fpr[k - 1, s].astype(F32)
        new_lat[s, my_rows(), :] = (res[own, :] + total).astype(BF16)
    nl_hop, nl_end = line_share(lambda rows: new_lat.at[:, rows, :])
    nl_hop(1)
    o_z = []
    for g in range(2):
        o_z += heads_last(st_o, xr_o.at[g], o_heads[g], o_steps[g], zb_o, zr_o)

    arrive(dq_z)
    upstream_all = mgl[...]
    for k in range(T):
        total = dqb[k, :, my_rows(), :].astype(F32)
        for m in range(1, T):
            total = total + dqr[m - 1, k].astype(F32)
        weights = wq_b[k, :, :, :, pl.ds(0, I)].reshape(D, I)
        upstream_all = upstream_all + nt(total.astype(BF16).reshape(S * Lt, I), weights)
    mgl[...] = upstream_all
    lat_gain_part = jnp.zeros((1, D), F32)
    lat_shift_part = jnp.zeros((1, D), F32)
    for s in range(S):
        own = pl.ds(pl.multiple_of(s * L + t * Lt, Lt), Lt)
        unit, scale_inv = unit_rows(lat[own, :].astype(F32))
        upstream = mgl[pl.ds(s * Lt, Lt), :]
        back = rgr[pl.ds(s * Lt, Lt), :] + norm_back(unit, scale_inv, lgain[...], upstream)
        lat_grad[s, my_rows(), :] = back.astype(BF16)
        lat_gain_part = lat_gain_part + jnp.sum(upstream * unit, axis=0, keepdims=True)
        lat_shift_part = lat_shift_part + jnp.sum(upstream, axis=0, keepdims=True)
    lg_hop, lg_end = line_share(lambda rows: lat_grad.at[:, rows, :])
    lg_hop(1)

    vst[...] += jnp.concatenate(
        [
            jnp.sum(acc[0], axis=0, keepdims=True),
            jnp.sum(acc[1], axis=0, keepdims=True),
            lat_gain_part,
            lat_shift_part,
            jnp.zeros((4, D), F32),
        ],
        axis=0,
    )
    vec_c = over_core(vst, vcr)
    start(vec_c)
    arrive(vec_c)
    vx[c] = vst[...] + vcr[...]
    vec_row = row("x")

    def vec_x(j, chip):
        return remote(vx.at[chip], vx.at[chip], xs.at[vec_row, j - 1], xr.at[vec_row, j - 1], x_dev(j))

    lax.fori_loop(1, C, lambda j, carry: (vec_x(j, c).start(), carry)[1], 0)

    group_step(groups - 1)
    nl_hop(2)
    q_z = []
    for g in range(groups - 1):
        q_z += group_last(g)
    feed_last(st_up, xr_up, up_g, g_up)
    feed_last(st_dn, xr_dn, dn_g, g_dn)
    lax.fori_loop(1, C, lambda j, carry: (vec_x(j, lax.rem(c - j + C, C)).wait_recv(), carry)[1], 0)
    vz[t] = lax.fori_loop(1, C, lambda j, value: value + vx[j], vx[0])
    v_z = over_z(lambda k: (vz.at[t], vz.at[t]))
    i = count["z"] - 1
    v_in = [remote(vz.at[head(k)], vz.at[head(k)], zs.at[i, k - 1], zr.at[i, k - 1], z_dev(k)) for k in range(1, T)]
    start(v_z)
    lg_hop(2)
    q_z += group_last(groups - 1)
    for h in range(3, T):
        nl_hop(h)
        lg_hop(h)
    arrive(v_in)
    g_vec[...] = lax.fori_loop(1, T, lambda k, value: value + vz[k], vz[0])
    arrive(o_z)
    total = zb_o[0].astype(F32)
    for k in range(1, T):
        total = total + zr_o[k - 1].astype(F32)
    g_o[...] = total
    arrive(q_z)
    total = zb_qkv[0].astype(F32)
    for k in range(1, T):
        total = total + zr_qkv[k - 1].astype(F32)
    g_qkv[...] = total

    nl_end()
    lg_end()
    for copy in started:
        copy.wait_send()
    lax.fori_loop(1, C, lambda j, carry: (vec_x(j, c).wait_send(), carry)[1], 0)
    for s in range(S):
        pltpu.make_async_copy(mown.at[s], media_grad.at[s], osem.at[s]).wait()


def hand_out(z, *refs):
    ins, outs, held, results, sem_in, sem_out = refs[:8], refs[8:23], refs[23:31], refs[31:38], refs[38], refs[39]
    order = (1, 0, 2, 5, 6, 3, 4, 7)
    loads = {i: pltpu.make_async_copy(ins[i], held[i], sem_in.at[i]) for i in order}
    stores = []

    def store(src, i):
        copy = pltpu.make_async_copy(src, outs[i], sem_out.at[i])
        copy.start()
        stores.append(copy)

    for i in order:
        loads[i].start()
    new_lat, media_grad, lat_grad, g_qkv, g_o, g_up, g_dn, g_vec = held
    loads[5].wait()
    store(g_up, 7)
    loads[6].wait()
    results[0][...] = g_dn[...].T
    store(results[0], 8)
    loads[0].wait()
    store(new_lat, 0)
    loads[2].wait()
    store(lat_grad, 2)
    loads[1].wait()
    store(media_grad, 1)
    loads[3].wait()
    for m in range(3):
        store(g_qkv.at[:, pl.ds(m * z.I, z.I)], 3 + m)
    loads[4].wait()
    results[1][...] = g_o[...].T
    store(results[1], 6)
    loads[7].wait()
    for m in range(2):
        store(g_vec.at[pl.ds(m, 1)], 9 + m)
    first = lax.axis_index("dp") * z.R
    row = lax.broadcasted_iota(jnp.int32, (z.D, z.R), 0)
    col = lax.broadcasted_iota(jnp.int32, (z.D, z.R), 1)
    pick = jnp.where(row == col + first, 1.0, 0.0).astype(F32)
    own = lax.dot_general(
        g_vec[...], pick, (((1,), (0,)), ((), ())), preferred_element_type=F32, precision=lax.Precision.HIGHEST
    )
    for m in range(4):
        results[2 + m][...] = own[2 + m : 3 + m]
        store(results[2 + m], 11 + m)
    for copy in stores:
        copy.wait()


def solution(mesh):
    T, N = mesh.shape["tensor"], mesh.shape["dp"]

    def on_device(
        media_tokens,
        latents,
        image_counts,
        media_gain,
        media_shift,
        latent_gain,
        latent_shift,
        feed_gain,
        feed_shift,
        query_weight,
        key_weight,
        value_weight,
        output_weight,
        up_weight,
        down_weight,
        cotangent,
    ):
        samples, slots, width = media_tokens.shape
        z = Sizes(T, N, samples, latents.shape[1], slots, width, up_weight.shape[1], query_weight.shape[1])
        S, L, D, F, I, R, C = z.S, z.L, z.D, z.F, z.I, z.R, z.C
        row = lambda v: v.reshape(1, D)
        vmem = pl.BlockSpec(memory_space=pltpu.VMEM)
        hbm = pl.BlockSpec(memory_space=pl.ANY)
        V = pltpu.VMEM
        scratch = [
            V((S * L, D), BF16),
            V((S * L, D), BF16),
            V((F, R), BF16),
            V((I, D), BF16),
            V((T, C, 2, R, 3 * I), BF16),
            V((T, C, 2, R, I), BF16),
            V((C, 2, R, F), BF16),
            V((C, 2, R, F), BF16),
            V((SLOTS_IN_FLIGHT, z.Mt, D), BF16),
            V((S, z.Mt, D), BF16),
            V((2, z.Mt, D), BF16),
            V((S * z.Kt, D), BF16),
            V((S * L, D), BF16),
            V((T, S, L, I), BF16),
            V((T, max(S, 8), z.q), F32),
            V((S * L, T * I), BF16),
            V((S * z.Kt, T * I), BF16),
            V((S * z.Kt, T * I), BF16),
            V((max(T // z.G * S, 2 * D // BLOCK), z.Kt, z.G * z.q), F32),
            V((max(z.K, S * z.Kt), max(S, T) * 2 * I), BF16),
            V((S * L, D), F32),
            V((S * L, D), BF16),
            V((S * L, F), BF16),
            V((S * L, F), BF16),
            V((S, L, D), BF16),
            V((T - 1, S, z.Lt, D), BF16),
            V((S, L, D), BF16),
            V((T - 1, S, z.Lt, D), BF16),
            V((S * z.Lt, D), BF16),
            V((S * z.Lt, D), F32),
            V((T, S, L, I), BF16),
            V((T, S, L, I), BF16),
            V((T - 1, T, S, z.Lt, I), BF16),
            V((C, 2, R, F), BF16),
            V((C, 2, R, F), BF16),
            V((T, C, 2, R, I), BF16),
            V((T, C, 2, R, 3 * I), BF16),
            V((C, R, F), BF16),
            V((C, R, F), BF16),
            V((T, C, R, I), BF16),
            V((T, C, R, 3 * I), BF16),
            V((max(C - 1, 1), R, F), BF16),
            V((max(C - 1, 1), R, F), BF16),
            V((2, max(C - 1, 1), T // 2, R, I), BF16),
            V((T, max(C - 1, 1), 1, R, 3 * I), BF16),
            V((T, R, I), BF16),
            V((T, R, 3 * I), BF16),
            V((T - 1, R, I), BF16),
            V((T - 1, R, 3 * I), BF16),
            V((S * z.Lt, D), F32),
            V((2, 8, D), F32),
            V((8, D), F32),
            V((8, D), F32),
            V((C, 8, D), F32),
            V((T, 8, D), F32),
            pltpu.SemaphoreType.DMA((8,)),
            pltpu.SemaphoreType.DMA((SLOTS_IN_FLIGHT + 1,)),
            pltpu.SemaphoreType.DMA((S,)),
            pltpu.SemaphoreType.DMA((26, T - 1)),
            pltpu.SemaphoreType.DMA((26, T - 1)),
            pltpu.SemaphoreType.DMA((14, max(C - 1, 1))),
            pltpu.SemaphoreType.DMA((14, max(C - 1, 1))),
            pltpu.SemaphoreType.DMA((8 + 2 * C,)),
            pltpu.SemaphoreType.DMA((8 + 2 * C,)),
        ]
        shape = jax.ShapeDtypeStruct
        outs = pl.pallas_call(
            functools.partial(layer_kernel, z),
            out_shape=[
                shape((S, L, D), BF16),
                shape((S, z.Mt, D), BF16),
                shape((S, L, D), BF16),
                shape((R, 3 * I), F32),
                shape((R, I), F32),
                shape((R, F), F32),
                shape((R, F), F32),
                shape((8, D), F32),
            ],
            in_specs=[pl.BlockSpec(memory_space=pltpu.SMEM)] + [hbm] * 3 + [vmem] * 6 + [hbm] * 6,
            out_specs=[vmem, hbm] + [vmem] * 6,
            scratch_shapes=scratch,
            compiler_params=pltpu.CompilerParams(
                collective_id=0, has_side_effects=True, vmem_limit_bytes=63 * 1024 * 1024
            ),
            name="resampler_layer",
        )(
            image_counts,
            media_tokens,
            latents.reshape(S * L, D),
            cotangent.reshape(S * L, D),
            row(media_gain),
            row(media_shift),
            row(latent_gain),
            row(latent_shift),
            row(feed_gain),
            row(feed_shift),
            query_weight.reshape(C, 2, R, I),
            key_weight.reshape(C, 2, R, I),
            value_weight.reshape(C, 2, R, I),
            output_weight,
            up_weight,
            down_weight,
        )
        final = pl.pallas_call(
            functools.partial(hand_out, z),
            out_shape=[
                shape((S, L, D), BF16),
                shape((S, z.Mt, D), BF16),
                shape((S, L, D), BF16),
                shape((R, I), F32),
                shape((R, I), F32),
                shape((R, I), F32),
                shape((I, R), F32),
                shape((R, F), F32),
                shape((F, R), F32),
                shape((1, D), F32),
                shape((1, D), F32),
            ]
            + [shape((1, R), F32)] * 4,
            in_specs=[hbm] * 8,
            out_specs=[hbm] * 15,
            scratch_shapes=[V(out.shape, out.dtype) for out in outs]
            + [V((F, R), F32), V((I, R), F32)]
            + [V((1, R), F32)] * 5
            + [pltpu.SemaphoreType.DMA((8,)), pltpu.SemaphoreType.DMA((15,))],
            name="hand_out",
        )(*outs)
        return tuple(final[:9]) + tuple(v.reshape(-1) for v in final[9:])

    placed = (
        P("dp", None, None),
        P("dp", None, None),
        P("dp"),
        P(),
        P(),
        P(),
        P(),
        P(),
        P(),
        P(None, "tensor"),
        P(None, "tensor"),
        P(None, "tensor"),
        P("tensor", None),
        P("dp", "tensor"),
        P("tensor", "dp"),
        P("dp", None, None),
    )
    return jax.shard_map(
        on_device,
        mesh=mesh,
        in_specs=placed,
        out_specs=(
            P("dp", None, None),
            P("dp", "tensor", None),
            P("dp", None, None),
            P("dp", "tensor"),
            P("dp", "tensor"),
            P("dp", "tensor"),
            P("tensor", "dp"),
            P("dp", "tensor"),
            P("tensor", "dp"),
            P(),
            P(),
            P("dp"),
            P("dp"),
            P("dp"),
            P("dp"),
        ),
        check_vma=False,
    )
```

```python
import functools

import jax
import jax.numpy as jnp
from jax import lax
from jax.experimental import pallas as pl
from jax.experimental.pallas import tpu as pltpu
from jax.sharding import PartitionSpec as P

HEAD_DIM = 64
PATCH = 256
EPSILON = 1e-05
NEGATIVE = -1e30
SQRT_HALF = 0.7071067811865476
INV_ROOT_TWO_PI = 0.3989422804014327
F32 = jnp.float32
BF16 = jnp.bfloat16
MESH = pl.DeviceIdType.MESH
BLOCK = 256
ROWS = 32
SLOTS_IN_FLIGHT = 3


def nn(left, right):
    return lax.dot_general(left, right, (((1,), (0,)), ((), ())), preferred_element_type=F32)


def nt(left, right):
    return lax.dot_general(left, right, (((1,), (1,)), ((), ())), preferred_element_type=F32)


def tn(left, right):
    return lax.dot_general(left, right, (((0,), (0,)), ((), ())), preferred_element_type=F32)


def unit_rows(x):
    centre = x - jnp.mean(x, axis=-1, keepdims=True)
    scale_inv = lax.rsqrt(jnp.mean(centre * centre, axis=-1, keepdims=True) + EPSILON)
    return centre * scale_inv, scale_inv


def norm_back(unit, scale_inv, gain, upstream):
    scaled = upstream * gain
    inner = scaled - jnp.mean(scaled, axis=-1, keepdims=True)
    inner = inner - unit * jnp.mean(scaled * unit, axis=-1, keepdims=True)
    return inner * scale_inv


def fold(x):
    return jnp.sum(x.reshape(x.shape[0] // 8, 8, x.shape[1]), axis=0)


class Sizes:
    def __init__(self, tensor, dp, samples, lat, slots, width, hidden, inner):
        self.T, self.N, self.C = tensor, dp, dp // 2
        self.S, self.L, self.M, self.D = samples, lat, slots, width
        self.F, self.I = hidden, inner
        self.R = width // dp
        self.Lt, self.Mt = lat // tensor, slots // tensor
        self.Kt = self.Lt + self.Mt
        self.K = lat + slots
        self.H = inner // HEAD_DIM
        self.q = self.H * lat
        self.G = min(2, tensor)


def layer_kernel(
    z,
    counts,
    media,
    lat_h,
    cot_h,
    mgain,
    mshift,
    lgain,
    lshift,
    fgain,
    fshift,
    wq,
    wk,
    wv,
    wo,
    up,
    dn,
    new_lat,
    media_grad,
    lat_grad,
    g_qkv,
    g_o,
    g_up,
    g_dn,
    g_vec,
    lat,
    cot,
    dn_v,
    wo_v,
    wq_b,
    wo_b,
    up_b,
    dn_b,
    mbuf,
    mown,
    xn,
    ctx,
    latn,
    att,
    lse,
    qall,
    kall,
    vall,
    pall,
    pairs,
    res,
    hin,
    act,
    bgr,
    hg,
    hgr,
    fp,
    fpr,
    og,
    rgr,
    dob,
    dos,
    dqb,
    dqr,
    st_up,
    st_dn,
    st_o,
    st_qkv,
    cr_up,
    cr_dn,
    cr_o,
    cr_qkv,
    xr_up,
    xr_dn,
    xr_o,
    xr_qkv,
    zb_o,
    zb_qkv,
    zr_o,
    zr_qkv,
    mgl,
    acc,
    vst,
    vcr,
    vx,
    vz,
    lsem,
    msem,
    osem,
    zs,
    zr,
    xs,
    xr,
    cs,
    cr,
):
    T, N, C, S, L, M, D = z.T, z.N, z.C, z.S, z.L, z.M, z.D
    F, I, R, Lt, Mt, Kt, G = z.F, z.I, z.R, z.Lt, z.Mt, z.Kt, z.G
    GI = G * I
    groups = T // G
    scale_factor = HEAD_DIM ** (-0.5)
    t = lax.axis_index("tensor")
    d = lax.axis_index("dp")
    c = lax.div(d, 2)
    core = lax.rem(d, 2)
    other = 1 - core
    n = BLOCK // (2 * R)
    blocks = D // BLOCK
    count = {"z": 0, "x": 0, "c": 0}
    started = []

    def row(kind):
        count[kind] += 1
        return count[kind] - 1

    def start(copies):
        for copy in copies:
            copy.start()
        started.extend(copies)

    def arrive(copies):
        for copy in copies:
            copy.wait_recv()

    def z_dev(k):
        return (d, lax.rem(t + k, T))

    def x_dev(j):
        return (2 * lax.rem(c + j, C) + core, t)

    core_dev = (d + 1 - 2 * core, t)

    def head(k):
        return lax.rem(t - k + T, T)

    def my_rows(k=0):
        return pl.ds(pl.multiple_of(lax.rem(t + k, T) * Lt, Lt), Lt)

    def remote(src, dst, send, recv, dev):
        return pltpu.make_async_remote_copy(
            src_ref=src, dst_ref=dst, send_sem=send, recv_sem=recv, device_id=dev, device_id_type=MESH
        )

    def over_z(pick):
        i = row("z")
        return [remote(*pick(k), zs.at[i, k - 1], zr.at[i, k - 1], z_dev(k)) for k in range(1, T)]

    def line_share(pick):
        ways = []
        for step in (1, -1):
            i = row("z")
            hops = []
            for h in range(1, T):
                owner, fresh = t - step * (h - 1), t - step * h
                beyond = t + step
                sends = (owner >= 0) & (owner < T) & (beyond >= 0) & (beyond < T)
                comes = (fresh >= 0) & (fresh < T)
                mine, theirs = pick(my_rows(T - step * (h - 1))), pick(my_rows(T - step * h))
                dev = (d, lax.rem(t + step + T, T))
                sems = (zs.at[i, h - 1], zr.at[i, h - 1])
                hops.append((sends, remote(mine, mine, *sems, dev), comes, remote(theirs, theirs, *sems, dev)))
            ways.append(hops)

        def hop(h, last=False):
            if h >= T and not last:
                return
            for hops in ways:
                if h > 1:
                    pl.when(hops[h - 2][2])(hops[h - 2][3].wait_recv)
                if h < T:
                    pl.when(hops[h - 1][0])(hops[h - 1][1].start)

        def end():
            hop(T, last=True)
            for hops in ways:
                for sends, copy, _, _ in hops:
                    pl.when(sends)(copy.wait_send)

        return hop, end

    def over_core(src, dst):
        i = row("c")
        return [remote(src, dst, cs.at[i], cr.at[i], core_dev)]

    bits = C.bit_length() - 1
    x_first = list(range(bits))
    y_first = x_first[::-1]

    def flip(chip, mask):
        for bit in range(bits):
            if mask >> bit & 1:
                chip = chip + (1 - 2 * lax.rem(lax.div(chip, 1 << bit), 2)) * (1 << bit)
        return chip

    def subsets(order):
        masks = [0]
        for bit in order:
            masks = masks + [m | 1 << bit for m in masks]
        return masks

    def gather_steps(view, order):
        i, at, rests = row("x"), 0, []
        firsts = ([], [])
        for step, bit in enumerate(order):
            peer = flip(c, 1 << bit)
            dev = (2 * peer + core, t)
            rest = ([], [])
            for m in subsets(order[:step]):
                sems = (xs.at[i, at], xr.at[i, at])
                mine, theirs = view(flip(c, m)), view(flip(peer, m))
                out, came = rest if m else firsts
                out.append(remote(mine, mine, *sems, dev))
                came.append(remote(theirs, theirs, *sems, dev))
                at += 1
            if step:
                rests.append(rest)
        return firsts, rests

    def gather_rest(gather):
        firsts, rests = gather
        for step, rest in enumerate(rests):
            arrive([firsts[1][step]])
            if step:
                arrive(rests[step - 1][1])
            start(rest[0])

    def gather_near(gather):
        arrive([gather[0][1][-1]])

    def gather_done(gather):
        if gather[1]:
            arrive(gather[1][-1][1])

    def scatter_steps(view, land, order):
        i, at, steps = row("x"), 0, []
        for step, bit in enumerate(order):
            peer = flip(c, 1 << bit)
            dev = (2 * peer + core, t)
            out, keep = [], []
            for m in subsets(order[step + 1 :]):
                out.append(remote(view(flip(peer, m)), land(at), xs.at[i, at], xr.at[i, at], dev))
                keep.append((flip(c, m), at))
                at += 1
            steps.append((out, keep))
        return steps

    n_tiles = S * T

    def tile_copy(i):
        slot = lax.rem(i, SLOTS_IN_FLIGHT)
        s, r = lax.div(i, T), lax.rem(i, T)
        return pltpu.make_async_copy(
            media.at[s, pl.ds(pl.multiple_of(r * Mt, Mt), Mt)], mbuf.at[slot], msem.at[slot]
        )

    own_copy = pltpu.make_async_copy(
        media.at[:, pl.ds(pl.multiple_of(t * Mt, Mt), Mt)], mown, msem.at[SLOTS_IN_FLIGHT]
    )
    barrier = pltpu.get_barrier_semaphore()

    def greet(dev):
        pl.semaphore_signal(barrier, inc=1, device_id=dev, device_id_type=MESH)

    for k in range(1, T):
        greet(z_dev(k))
    lax.fori_loop(1, C, lambda j, carry: (greet(x_dev(j)), carry)[1], 0)
    greet(core_dev)
    loads = [
        pltpu.make_async_copy(src, dst, lsem.at[i])
        for i, (src, dst) in enumerate(
            [(up, up_b.at[c, core]), (dn, dn_v), (wo, wo_v)]
            + [(w, wq_b.at[0, m]) for m, w in enumerate((wq, wk, wv))]
            + [(lat_h, lat), (cot_h, cot)]
        )
    ]
    for copy in loads:
        copy.start()
    for i in range(min(SLOTS_IN_FLIGHT, n_tiles)):
        tile_copy(i).start()
    for copy in loads[:3]:
        copy.wait()
    dn_b[c, core] = dn_v[...].T
    wo_b[0] = wo_v[...].T.reshape(C, 2, R, I)
    pl.semaphore_wait(barrier, T + C - 1)

    foreign = pl.ds(1, T - 1)
    up_x = gather_steps(lambda chip: up_b.at[chip, core], x_first)
    dn_x = gather_steps(lambda chip: dn_b.at[chip, core], y_first)
    wo_x = gather_steps(lambda chip: wo_b.at[foreign, chip, core], x_first)
    qk_x = gather_steps(lambda chip: wq_b.at[foreign, pl.ds(0, 2), chip, core], x_first)
    v_x = gather_steps(lambda chip: wq_b.at[foreign, 2, chip, core], y_first)
    wo_z = over_z(lambda k: (wo_b.at[0, c, core], wo_b.at[k, c, core]))
    wq_z = over_z(lambda k: (wq_b.at[0, :, c, core], wq_b.at[k, :, c, core]))
    near = [0] + [1 << bit for bit in range(bits)]
    far = [m for m in range(C) if m not in near]

    def relay(ref, masks):
        return [copy for m in masks for copy in over_core(ref.at[flip(c, m), core], ref.at[flip(c, m), core])]

    feed_near = relay(up_b, near) + relay(dn_b, near)
    feed_far = relay(up_b, far) + relay(dn_b, far)
    wo_c = over_core(wo_b.at[foreign, :, core], wo_b.at[foreign, :, core])
    wq_c = over_core(wq_b.at[foreign, :, :, core], wq_b.at[foreign, :, :, core])

    for way in range(bits):
        start([up_x[0][0][way], dn_x[0][0][way]])
    start(wo_z)
    for copy in loads[3:]:
        copy.wait()
    start(wq_z)
    own_copy.start()

    for b in range(S * L // ROWS):
        rows = pl.ds(b * ROWS, ROWS)
        unit, _ = unit_rows(lat[rows, :].astype(F32))
        latn[rows, :] = (unit * lgain[...] + lshift[...]).astype(BF16)
    def head_weights(k, ms):
        return jnp.concatenate([wq_b[k, m].reshape(D, I) for m in ms], axis=1)

    own_qkv = nn(latn[...], head_weights(0, range(3))).astype(BF16)
    qall[:, pl.ds(0, I)] = own_qkv[:, :I]
    for s in range(S):
        pairs[pl.ds(M, L), pl.ds(s * 2 * I, 2 * I)] = own_qkv[s * L : (s + 1) * L, I:]
        ctx[pl.ds(s * Kt + Mt, Lt), :] = latn[pl.ds(pl.multiple_of(s * L + t * Lt, Lt), Lt), :]

    def tile_norm(i, half):
        slot = lax.rem(i, SLOTS_IN_FLIGHT)
        for b in range(Mt // ROWS):
            rows = pl.ds(b * ROWS, ROWS)
            unit, _ = unit_rows(mbuf[slot, rows, :].astype(F32))
            xn[half, rows, :] = (unit * mgain[...] + mshift[...]).astype(BF16)

    def tile_pair(i, half):
        s, r = lax.div(i, T), lax.rem(i, T)
        pair = nn(xn[half], head_weights(0, (1, 2)))
        lanes = pl.ds(pl.multiple_of(s * 2 * I, 2 * I), 2 * I)
        pairs[pl.ds(pl.multiple_of(r * Mt, Mt), Mt), lanes] = pair.astype(BF16)

    def tile_keep(i, half):
        s, r = lax.div(i, T), lax.rem(i, T)

        @pl.when(r == t)
        def _():
            ctx[pl.ds(pl.multiple_of(s * Kt, 16), Mt), :] = xn[half]

    def tile_next(i):
        @pl.when(i + SLOTS_IN_FLIGHT < n_tiles)
        def _():
            tile_copy(i + SLOTS_IN_FLIGHT).start()

    tile_copy(0).wait()
    tile_norm(0, 0)
    tile_next(0)

    def two_tiles(j, carry):
        i = 2 * j
        tile_copy(i + 1).wait()

        @pl.when(i + 2 < n_tiles)
        def _():
            tile_copy(i + 2).wait()

        tile_keep(i, 0)
        tile_pair(i, 0)
        tile_norm(i + 1, 1)
        tile_keep(i + 1, 1)
        tile_pair(i + 1, 1)
        tile_norm(lax.rem(i + 2, n_tiles), 0)
        tile_next(i + 1)
        tile_next(i + 2)
        return carry

    first = n_tiles // 8
    lax.fori_loop(0, first, two_tiles, 0)
    arrive(wo_z)
    start(wo_x[0][0])
    lax.fori_loop(first, n_tiles // 2, two_tiles, 0)
    gather_rest(up_x)
    gather_rest(dn_x)
    gather_rest(wo_x)

    def spread(x):
        lane_head = lax.broadcasted_iota(jnp.int32, (1, x.shape[1]), 1) // HEAD_DIM
        zero = jnp.zeros_like(x)
        return jnp.concatenate(
            [jnp.where(lane_head == h, x, zero) for h in range(x.shape[1] // HEAD_DIM)], axis=0
        )

    def gather_heads(x):
        lane_head = lax.broadcasted_iota(jnp.int32, (1, x.shape[1]), 1) // HEAD_DIM
        out = x[:L]
        for h in range(1, x.shape[1] // HEAD_DIM):
            out = jnp.where(lane_head == h, x[h * L : (h + 1) * L], out)
        return out

    att_z = []
    for s in range(S):
        keys = pairs[pl.ds(0, z.K), pl.ds(s * 2 * I, I)]
        values = pairs[pl.ds(0, z.K), pl.ds(s * 2 * I + I, I)]
        scores = nt(keys, spread(qall[pl.ds(s * L, L), pl.ds(0, I)])) * scale_factor
        slot = lax.broadcasted_iota(jnp.int32, (z.K, 1), 0)
        valid = (slot < counts[s] * PATCH) | (slot >= M)
        scores = jnp.where(valid, scores, NEGATIVE)
        largest = jnp.max(scores, axis=0, keepdims=True)
        total = largest + jnp.log(jnp.sum(jnp.exp(scores - largest), axis=0, keepdims=True))
        probs = jnp.exp(scores - total).astype(BF16)
        att[0, s] = gather_heads(tn(probs, values)).astype(BF16)
        lse[0, pl.ds(s, 1), :] = total
        if s % 2 == 1:
            now = over_z(lambda k, s=s: (att.at[0, pl.ds(s - 1, 2)], att.at[k, pl.ds(s - 1, 2)]))
            start(now)
            att_z += now
    lse_z = over_z(lambda k: (lse.at[0], lse.at[k]))
    start(lse_z)

    for s in range(S):
        lanes = s * 2 * I
        own_slots = pl.ds(pl.multiple_of(t * Mt, Mt), Mt)
        own_lat = pl.ds(pl.multiple_of(M + t * Lt, Lt), Lt)
        for m, ref in enumerate((kall, vall)):
            ref[pl.ds(s * Kt, Mt), pl.ds(0, I)] = pairs[own_slots, pl.ds(lanes + m * I, I)]
            ref[pl.ds(s * Kt + Mt, Lt), pl.ds(0, I)] = pairs[own_lat, pl.ds(lanes + m * I, I)]
    gather_near(wo_x)
    gather_near(up_x)
    gather_near(dn_x)
    start(feed_near)
    gather_done(wo_x)
    start(wo_c)
    arrive(wq_z)
    start(qk_x[0][0])
    start(v_x[0][0])
    gather_done(up_x)
    gather_done(dn_x)
    start(feed_far)

    def heads_wo():
        return jnp.concatenate([wo_b[k].reshape(D, I) for k in range(T)], axis=1)

    arrive(wo_c)
    arrive(att_z)
    att_all = jnp.concatenate([att[k].reshape(S * L, I) for k in range(T)], axis=1)
    res[...] = lat[...].astype(F32) + nt(att_all, heads_wo())
    for b in range(S * L // ROWS):
        rows = pl.ds(b * ROWS, ROWS)
        unit, _ = unit_rows(res[rows, :])
        hin[rows, :] = (unit * fgain[...] + fshift[...]).astype(BF16)

    arrive(feed_near)
    arrive(feed_far)

    def feed(b, carry):
        cols = pl.ds(pl.multiple_of(b * BLOCK, BLOCK), BLOCK)
        before = nn(hin[...], up_b[:, :, :, cols].reshape(D, BLOCK))
        cdf = 0.5 * (1.0 + lax.erf(before * SQRT_HALF))
        act[:, cols] = (before * cdf).astype(BF16)
        slope = cdf + before * INV_ROOT_TWO_PI * jnp.exp(-0.5 * before * before)
        act_grad = nn(cot[...], dn_b[:, :, :, cols].reshape(D, BLOCK)).astype(BF16)
        bgr[:, cols] = (act_grad.astype(F32) * slope).astype(BF16)
        return carry

    lax.fori_loop(0, F // BLOCK, feed, 0, unroll=4)
    gather_rest(qk_x)
    gather_rest(v_x)

    def back_to_width(left, weight, out, b):
        block = nt(left[...], weight[pl.ds(b * n, n)].reshape(BLOCK, F))
        block = block.astype(BF16)
        for s in range(S):
            for u in range(T):
                first = s * L + u * Lt
                out[u, pl.ds(s * Lt, Lt), pl.ds(b * BLOCK, BLOCK)] = block[first : first + Lt]

    for b in range(blocks):
        back_to_width(bgr, up_b, hg, b)
    hg_z = over_z(lambda k: (hg.at[lax.rem(t + k, T)], hgr.at[k - 1]))
    start(hg_z)

    def feed_weights(left, right, out, b):
        block = tn(left[:, pl.ds(b * BLOCK, BLOCK)], right[...]).astype(BF16)
        out[pl.ds(b * n, n)] = block.reshape(n, 2, R, F)

    for b in range(blocks):
        feed_weights(hin, bgr, st_up, b)
    st_up_c = over_core(st_up.at[:, other], cr_up)
    start(st_up_c)
    for b in range(blocks):
        feed_weights(cot, act, st_dn, b)
    st_dn_c = over_core(st_dn.at[:, other], cr_dn)
    start(st_dn_c)
    for b in range(blocks):
        back_to_width(act, dn_b, fp, b)

    up_g = scatter_steps(lambda chip: st_up.at[chip, core], lambda at: xr_up.at[at], y_first)
    dn_g = scatter_steps(lambda chip: st_dn.at[chip, core], lambda at: xr_dn.at[at], x_first)

    def feed_core(copy, st, came, steps):
        arrive(copy)
        sent = steps[0][0]
        for m in subsets(range(bits)):
            chip = flip(c, m)
            st[chip, core] = (st[chip, core].astype(F32) + came[chip].astype(F32)).astype(BF16)
        start(sent)

    def feed_step(st, land, steps):
        for step in range(1, len(steps)):
            arrive(steps[step - 1][0])
            for chip, at in steps[step - 1][1]:
                st[chip, core] = (st[chip, core].astype(F32) + land[at].astype(F32)).astype(BF16)
            start(steps[step][0])

    def feed_last(st, land, steps, out):
        arrive(steps[-1][0])
        out[...] = st[c, core].astype(F32) + land[steps[-1][1][0][1]].astype(F32)

    feed_core(st_up_c, st_up, cr_up, up_g)
    feed_core(st_dn_c, st_dn, cr_dn, dn_g)

    for gather in (qk_x, v_x):
        gather_near(gather)
        gather_done(gather)
    start(wq_c)
    own_copy.wait()
    arrive(wq_c)
    for k in range(1, T):
        qall[:, pl.ds(k * I, I)] = nn(latn[...], head_weights(k, (0,))).astype(BF16)
    half_rows = S * Kt // 2

    def all_pairs(i, carry):
        k = lax.div(i, 2)
        rows = pl.ds(pl.multiple_of(lax.rem(i, 2) * half_rows, 16), half_rows)
        lanes = pl.ds(pl.multiple_of(k * I, I), I)
        pair = nn(ctx[rows, :], head_weights(k, (1, 2))).astype(BF16)
        kall[rows, lanes] = pair[:, :I]
        vall[rows, lanes] = pair[:, I:]
        return carry

    lax.fori_loop(2, 2 * T, all_pairs, 0)
    arrive(lse_z)
    slot_of = lax.broadcasted_iota(jnp.int32, (Kt, 1), 0)

    def group(g, s):
        rows = pl.ds(pl.multiple_of(s * Kt, 16), Kt)
        lat_rows = pl.ds(pl.multiple_of(s * L, L), L)
        return rows, pl.ds(g * GI, GI), lat_rows

    def joined(g, pick):
        return jnp.concatenate([pick(g * G + j) for j in range(G)], axis=1)

    for g in range(groups):

        def probabilities(s, carry, g=g):
            rows, lanes, lat_rows = group(g, s)
            scores = nt(kall[rows, lanes], spread(qall[lat_rows, lanes])) * scale_factor
            valid = (slot_of + t * Mt < counts[s] * PATCH) | (slot_of >= Mt)
            scores = jnp.where(valid, scores, NEGATIVE)
            pall[g * S + s] = jnp.exp(scores - joined(g, lambda k: lse[k, pl.ds(s, 1), :]))
            return carry

        lax.fori_loop(0, S, probabilities, 0, unroll=2)

    arrive(hg_z)
    feed_gain_part = jnp.zeros((1, D), F32)
    feed_shift_part = jnp.zeros((1, D), F32)
    for s in range(S):
        own = pl.ds(pl.multiple_of(s * L + t * Lt, Lt), Lt)
        unit, scale_inv = unit_rows(res[own, :])
        upstream = hg[t, pl.ds(s * Lt, Lt), :].astype(F32)
        for k in range(1, T):
            upstream = upstream + hgr[k - 1, pl.ds(s * Lt, Lt), :].astype(F32)
        back = cot[own, :].astype(F32) + norm_back(unit, scale_inv, fgain[...], upstream)
        feed_gain_part = feed_gain_part + jnp.sum(upstream * unit, axis=0, keepdims=True)
        feed_shift_part = feed_shift_part + jnp.sum(upstream, axis=0, keepdims=True)
        rgr[pl.ds(s * Lt, Lt), :] = back
        og[pl.ds(s * Lt, Lt), :] = back.astype(BF16)
    vst[...] = jnp.concatenate(
        [jnp.zeros((4, D), F32), feed_gain_part, feed_shift_part, jnp.zeros((2, D), F32)], axis=0
    )
    dos[0] = nn(og[...], heads_wo()).astype(BF16)
    turns = list(range(groups))[::-1]
    group_heads = [range(g * G, (g + 1) * G) for g in range(groups)]
    do_z = over_z(lambda k: (dos.at[0], dos.at[k]))
    start(do_z)

    att_own = jnp.concatenate([att[k, :, my_rows(), :].reshape(S * Lt, I) for k in range(T)], axis=1)
    for b in range(blocks):
        block = tn(og[:, pl.ds(b * BLOCK, BLOCK)], att_own).astype(BF16)
        for k in range(T):
            st_o[k, pl.ds(b * n, n)] = block[:, k * I : (k + 1) * I].reshape(n, 2, R, I)
    st_o_c = over_core(st_o.at[:, :, other], cr_o)
    start(st_o_c)

    def heads_core(st, came, ks, steps):
        for m in subsets(range(bits)):
            chip = flip(c, m)
            for k in ks:
                st[k, chip, core] = (st[k, chip, core].astype(F32) + came[k, chip].astype(F32)).astype(BF16)
        start(steps[0][0])

    def heads_step(st, land, ks, steps):
        for step in range(1, len(steps)):
            arrive(steps[step - 1][0])
            for chip, at in steps[step - 1][1]:
                for j, k in enumerate(ks):
                    st[k, chip, core] = (st[k, chip, core].astype(F32) + land[at, j].astype(F32)).astype(BF16)
            start(steps[step][0])

    def heads_last(st, land, ks, steps, held, came):
        arrive(steps[-1][0])
        at = steps[-1][1][0][1]
        for j, k in enumerate(ks):
            held[k] = (st[k, c, core].astype(F32) + land[at, j].astype(F32)).astype(BF16)
        i = row("z")
        copies = [
            remote(held.at[k], came.at[T - k - 1], zs.at[i, k - 1], zr.at[i, T - k - 1], (d, head(k)))
            for k in ks
            if k
        ]
        start(copies)
        return copies

    orders = (x_first, y_first)
    o_heads = [range(g * T // 2, (g + 1) * T // 2) for g in range(2)]
    o_steps = [
        scatter_steps(
            lambda chip, g=g: st_o.at[pl.ds(g * T // 2, T // 2), chip, core], lambda at, g=g: xr_o.at[g, at], orders[g]
        )
        for g in range(2)
    ]
    arrive(st_o_c)
    for g in range(2):
        heads_core(st_o, cr_o, o_heads[g], o_steps[g])

    arrive(do_z)
    for m in range(T):
        for k in range(T):
            lanes = pl.ds((k - m) % T * I, I)
            dob[k, :, my_rows(T - m), :] = dos[m, :, lanes].reshape(S, Lt, I)

    def attend_back(s, carry, g):
        rows, lanes, lat_rows = group(g, s)
        keys = kall[rows, lanes]
        queries = spread(qall[lat_rows, lanes])
        grads = spread(joined(g, lambda k: dob[k, s]))
        outs = spread(joined(g, lambda k: att[k, s]))
        product = grads.astype(F32) * outs.astype(F32)
        inner = lax.dot_general(
            jnp.ones((8, GI), F32),
            product,
            (((1,), (1,)), ((), ())),
            preferred_element_type=F32,
            precision=lax.Precision.HIGHEST,
        )[:1]
        probs = pall[g * S + s]
        score_grad = (probs * (nt(vall[rows, lanes], grads) - inner)).astype(BF16)
        pairs[rows, lanes] = (nn(score_grad, queries) * scale_factor).astype(BF16)
        pairs[rows, pl.ds(T * I + g * GI, GI)] = nn(probs.astype(BF16), grads).astype(BF16)
        query_grad = (gather_heads(tn(score_grad, keys)) * scale_factor).astype(BF16)
        for j in range(G):
            for u in range(T):
                rows_u = pl.ds(pl.multiple_of(s * Lt, Lt), Lt)
                dqb[u, g * G + j, rows_u, :] = query_grad[u * Lt : (u + 1) * Lt, j * I : (j + 1) * I]
        return carry

    def group_weights(g):
        query_part = jnp.concatenate(
            [
                jnp.concatenate([dqb[u, g * G + j, pl.ds(s * Lt, Lt), :] for s in range(S) for u in range(T)], axis=0)
                for j in range(G)
            ],
            axis=1,
        )
        all_rows = pl.ds(0, S * Kt)
        part = jnp.concatenate(
            [pairs[all_rows, pl.ds(g * GI, GI)], pairs[all_rows, pl.ds(T * I + g * GI, GI)]], axis=1
        )
        for b in range(blocks):
            cols = pl.ds(b * BLOCK, BLOCK)
            block = tn(ctx[:, cols], part).astype(BF16)
            query_block = tn(latn[:, cols], query_part).astype(BF16)
            for j in range(G):
                lanes = slice(j * I, (j + 1) * I)
                pieces = (query_block[:, lanes], block[:, lanes], block[:, GI:][:, lanes])
                for m, piece in enumerate(pieces):
                    st_qkv[g * G + j, pl.ds(b * n, n), :, :, pl.ds(m * I, I)] = piece.reshape(n, 2, R, I)
        ks = pl.ds(g * G, G)
        copy = over_core(st_qkv.at[ks, :, other], cr_qkv.at[ks])
        start(copy)
        return copy

    q_steps = [
        scatter_steps(lambda chip, k=k: st_qkv.at[pl.ds(k, 1), chip, core], lambda at, k=k: xr_qkv.at[k, at], orders[k % 2])
        for k in range(T)
    ]
    q_c, dq_z = {}, []

    def group_core(g):
        arrive(q_c[g])
        for k in group_heads[g]:
            heads_core(st_qkv, cr_qkv, (k,), q_steps[k])

    def group_step(g):
        for k in group_heads[g]:
            heads_step(st_qkv, xr_qkv.at[k], (k,), q_steps[k])

    def group_last(g):
        out = []
        for k in group_heads[g]:
            out += heads_last(st_qkv, xr_qkv.at[k], (k,), q_steps[k], zb_qkv, zr_qkv)
        return out

    fp_z = over_z(lambda k: (fp.at[lax.rem(t + k, T)], fpr.at[k - 1]))
    if groups > 1:
        start(fp_z)
        feed_step(st_up, xr_up, up_g)
        feed_step(st_dn, xr_dn, dn_g)
    def new_rows():
        arrive(fp_z)
        for s in range(S):
            own = pl.ds(pl.multiple_of(s * L + t * Lt, Lt), Lt)
            total = fp[t, pl.ds(s * Lt, Lt), :].astype(F32)
            for k in range(1, T):
                total = total + fpr[k - 1, pl.ds(s * Lt, Lt), :].astype(F32)
            new_lat[s, my_rows(), :] = (res[own, :] + total).astype(BF16)

    nl_hop, nl_end = line_share(lambda rows: new_lat.at[:, rows, :])
    for turn, g in enumerate(turns):
        if turn <= 1:
            if turn == 0 and groups > 1:
                lax.fori_loop(0, S // 2, functools.partial(attend_back, g=g), 0, unroll=2)
                lax.fori_loop(S // 2, S, functools.partial(attend_back, g=g), 0, unroll=2)
            else:
                lax.fori_loop(0, S // 2, functools.partial(attend_back, g=g), 0, unroll=2)
                if turn:
                    group_core(turns[turn - 1])
                else:
                    start(fp_z)
                lax.fori_loop(S // 2, S, functools.partial(attend_back, g=g), 0, unroll=2)
        else:
            group_core(turns[turn - 1])
            lax.fori_loop(0, S, functools.partial(attend_back, g=g), 0, unroll=2)
        ks = pl.ds(g * G, G)
        now = over_z(lambda m, ks=ks: (dqb.at[lax.rem(t + m, T), ks], dqr.at[m - 1, ks]))
        start(now)
        dq_z += now
        if turn == groups - 1:
            new_rows()
            nl_hop(1)
        q_c[g] = group_weights(g)
    if groups == 1:
        feed_step(st_up, xr_up, up_g)
        feed_step(st_dn, xr_dn, dn_g)
    for g in range(2):
        heads_step(st_o, xr_o.at[g], o_heads[g], o_steps[g])

    acc[...] = jnp.zeros_like(acc)

    def width(s, rows):
        return jnp.concatenate([pall[s % 2 * blocks + b, rows, :] for b in range(blocks)], axis=1)

    def width_weights(b):
        return jnp.concatenate(
            [wq_b[k, m, pl.ds(b * n, n)].reshape(BLOCK, I) for m in (1, 2) for k in range(T)], axis=1
        )

    def media_width(s):
        for b in range(blocks):
            pall[s % 2 * blocks + b] = nt(pairs[pl.ds(s * Kt, Kt), pl.ds(0, 2 * T * I)], width_weights(b))

    lat_pairs = jnp.concatenate(
        [pairs[pl.ds(s * Kt + Mt, Lt), pl.ds(0, 2 * T * I)] for s in range(S)], axis=0
    )
    for b in range(blocks):
        mgl[:, pl.ds(b * BLOCK, BLOCK)] = nt(lat_pairs, width_weights(b))

    def media_rows(s):
        for b in range(Mt // ROWS):
            rows = pl.ds(b * ROWS, ROWS)
            unit, scale_inv = unit_rows(mown[s, rows, :].astype(F32))
            upstream = width(s, rows)
            mown[s, rows, :] = norm_back(unit, scale_inv, mgain[...], upstream).astype(BF16)
            acc[0] += fold(upstream * unit)
            acc[1] += fold(upstream)
        pltpu.make_async_copy(mown.at[s], media_grad.at[s], osem.at[s]).start()

    media_width(0)
    media_width(1)
    group_core(turns[-1])
    media_rows(0)
    nl_hop(2)

    arrive(dq_z)
    upstream_all = mgl[...]
    for k in range(T):
        total = dqb[t, k].astype(F32)
        for m in range(1, T):
            total = total + dqr[m - 1, (k - m) % T].astype(F32)
        weights = head_weights(k, (0,))
        upstream_all = upstream_all + nt(total.astype(BF16), weights)
    mgl[...] = upstream_all
    lat_gain_part = jnp.zeros((1, D), F32)
    lat_shift_part = jnp.zeros((1, D), F32)
    for s in range(S):
        own = pl.ds(pl.multiple_of(s * L + t * Lt, Lt), Lt)
        unit, scale_inv = unit_rows(lat[own, :].astype(F32))
        upstream = mgl[pl.ds(s * Lt, Lt), :]
        back = rgr[pl.ds(s * Lt, Lt), :] + norm_back(unit, scale_inv, lgain[...], upstream)
        lat_grad[s, my_rows(), :] = back.astype(BF16)
        lat_gain_part = lat_gain_part + jnp.sum(upstream * unit, axis=0, keepdims=True)
        lat_shift_part = lat_shift_part + jnp.sum(upstream, axis=0, keepdims=True)
    lg_hop, lg_end = line_share(lambda rows: lat_grad.at[:, rows, :])
    lg_hop(1)

    for g in turns[:-1]:
        group_step(g)
    o_z = []
    for g in range(2):
        o_z += heads_last(st_o, xr_o.at[g], o_heads[g], o_steps[g], zb_o, zr_o)
    for s in range(1, S):
        if s + 1 < S:
            media_width(s + 1)
        media_rows(s)
    for h in range(3, T):
        nl_hop(h)
    group_step(turns[-1])
    q_z = []
    for g in turns[:-1]:
        q_z += group_last(g)
    lg_hop(2)

    vst[...] += jnp.concatenate(
        [
            jnp.sum(acc[0], axis=0, keepdims=True),
            jnp.sum(acc[1], axis=0, keepdims=True),
            lat_gain_part,
            lat_shift_part,
            jnp.zeros((4, D), F32),
        ],
        axis=0,
    )
    vec_c = over_core(vst, vcr)
    start(vec_c)
    arrive(vec_c)
    vx[c] = vst[...] + vcr[...]
    vec_row = row("x")

    def vec_x(j, chip):
        return remote(vx.at[chip], vx.at[chip], xs.at[vec_row, j - 1], xr.at[vec_row, j - 1], x_dev(j))

    lax.fori_loop(1, C, lambda j, carry: (vec_x(j, c).start(), carry)[1], 0)

    feed_last(st_up, xr_up, up_g, g_up)
    feed_last(st_dn, xr_dn, dn_g, g_dn)
    q_z += group_last(turns[-1])
    lax.fori_loop(1, C, lambda j, carry: (vec_x(j, lax.rem(c - j + C, C)).wait_recv(), carry)[1], 0)
    vz[t] = lax.fori_loop(1, C, lambda j, value: value + vx[j], vx[0])
    v_z = over_z(lambda k: (vz.at[t], vz.at[t]))
    i = count["z"] - 1
    v_in = [remote(vz.at[head(k)], vz.at[head(k)], zs.at[i, k - 1], zr.at[i, k - 1], z_dev(k)) for k in range(1, T)]
    start(v_z)
    for h in range(3, T):
        lg_hop(h)
    arrive(v_in)
    g_vec[...] = lax.fori_loop(1, T, lambda k, value: value + vz[k], vz[0])
    arrive(o_z)
    total = zb_o[0].astype(F32)
    for k in range(1, T):
        total = total + zr_o[k - 1].astype(F32)
    g_o[...] = total
    arrive(q_z)
    total = zb_qkv[0].astype(F32)
    for k in range(1, T):
        total = total + zr_qkv[k - 1].astype(F32)
    g_qkv[...] = total

    nl_end()
    lg_end()
    for copy in started:
        copy.wait_send()
    lax.fori_loop(1, C, lambda j, carry: (vec_x(j, c).wait_send(), carry)[1], 0)
    for s in range(S):
        pltpu.make_async_copy(mown.at[s], media_grad.at[s], osem.at[s]).wait()


def hand_out(z, *refs):
    ins, outs, held, results, sem_in, sem_out = refs[:8], refs[8:23], refs[23:31], refs[31:38], refs[38], refs[39]
    order = (1, 0, 2, 5, 6, 3, 4, 7)
    loads = {i: pltpu.make_async_copy(ins[i], held[i], sem_in.at[i]) for i in order}
    stores = []

    def store(src, i):
        copy = pltpu.make_async_copy(src, outs[i], sem_out.at[i])
        copy.start()
        stores.append(copy)

    for i in order:
        loads[i].start()
    new_lat, media_grad, lat_grad, g_qkv, g_o, g_up, g_dn, g_vec = held
    loads[5].wait()
    store(g_up, 7)
    loads[6].wait()
    results[0][...] = g_dn[...].T
    store(results[0], 8)
    loads[0].wait()
    store(new_lat, 0)
    loads[2].wait()
    store(lat_grad, 2)
    loads[1].wait()
    store(media_grad, 1)
    loads[3].wait()
    for m in range(3):
        store(g_qkv.at[:, pl.ds(m * z.I, z.I)], 3 + m)
    loads[4].wait()
    results[1][...] = g_o[...].T
    store(results[1], 6)
    loads[7].wait()
    for m in range(2):
        store(g_vec.at[pl.ds(m, 1)], 9 + m)
    first = lax.axis_index("dp") * z.R
    row = lax.broadcasted_iota(jnp.int32, (z.D, z.R), 0)
    col = lax.broadcasted_iota(jnp.int32, (z.D, z.R), 1)
    pick = jnp.where(row == col + first, 1.0, 0.0).astype(F32)
    own = lax.dot_general(
        g_vec[...], pick, (((1,), (0,)), ((), ())), preferred_element_type=F32, precision=lax.Precision.HIGHEST
    )
    for m in range(4):
        results[2 + m][...] = own[2 + m : 3 + m]
        store(results[2 + m], 11 + m)
    for copy in stores:
        copy.wait()


def solution(mesh):
    T, N = mesh.shape["tensor"], mesh.shape["dp"]

    def on_device(
        media_tokens,
        latents,
        image_counts,
        media_gain,
        media_shift,
        latent_gain,
        latent_shift,
        feed_gain,
        feed_shift,
        query_weight,
        key_weight,
        value_weight,
        output_weight,
        up_weight,
        down_weight,
        cotangent,
    ):
        samples, slots, width = media_tokens.shape
        z = Sizes(T, N, samples, latents.shape[1], slots, width, up_weight.shape[1], query_weight.shape[1])
        S, L, D, F, I, R, C = z.S, z.L, z.D, z.F, z.I, z.R, z.C
        row = lambda v: v.reshape(1, D)
        vmem = pl.BlockSpec(memory_space=pltpu.VMEM)
        hbm = pl.BlockSpec(memory_space=pl.ANY)
        V = pltpu.VMEM
        scratch = [
            V((S * L, D), BF16),
            V((S * L, D), BF16),
            V((F, R), BF16),
            V((I, D), BF16),
            V((T, 3, C, 2, R, I), BF16),
            V((T, C, 2, R, I), BF16),
            V((C, 2, R, F), BF16),
            V((C, 2, R, F), BF16),
            V((SLOTS_IN_FLIGHT, z.Mt, D), BF16),
            V((S, z.Mt, D), BF16),
            V((2, z.Mt, D), BF16),
            V((S * z.Kt, D), BF16),
            V((S * L, D), BF16),
            V((T, S, L, I), BF16),
            V((T, max(S, 8), z.q), F32),
            V((S * L, T * I), BF16),
            V((S * z.Kt, T * I), BF16),
            V((S * z.Kt, T * I), BF16),
            V((max(T // z.G * S, 2 * D // BLOCK), z.Kt, z.G * z.q), F32),
            V((max(z.K, S * z.Kt), max(S, T) * 2 * I), BF16),
            V((S * L, D), F32),
            V((S * L, D), BF16),
            V((S * L, F), BF16),
            V((S * L, F), BF16),
            V((T, S * z.Lt, D), BF16),
            V((T - 1, S * z.Lt, D), BF16),
            V((T, S * z.Lt, D), BF16),
            V((T - 1, S * z.Lt, D), BF16),
            V((S * z.Lt, D), BF16),
            V((S * z.Lt, D), F32),
            V((T, S, L, I), BF16),
            V((T, S * z.Lt, T * I), BF16),
            V((T, T, S * z.Lt, I), BF16),
            V((T - 1, T, S * z.Lt, I), BF16),
            V((C, 2, R, F), BF16),
            V((C, 2, R, F), BF16),
            V((T, C, 2, R, I), BF16),
            V((T, C, 2, R, 3 * I), BF16),
            V((C, R, F), BF16),
            V((C, R, F), BF16),
            V((T, C, R, I), BF16),
            V((T, C, R, 3 * I), BF16),
            V((max(C - 1, 1), R, F), BF16),
            V((max(C - 1, 1), R, F), BF16),
            V((2, max(C - 1, 1), T // 2, R, I), BF16),
            V((T, max(C - 1, 1), 1, R, 3 * I), BF16),
            V((T, R, I), BF16),
            V((T, R, 3 * I), BF16),
            V((T - 1, R, I), BF16),
            V((T - 1, R, 3 * I), BF16),
            V((S * z.Lt, D), F32),
            V((2, 8, D), F32),
            V((8, D), F32),
            V((8, D), F32),
            V((C, 8, D), F32),
            V((T, 8, D), F32),
            pltpu.SemaphoreType.DMA((8,)),
            pltpu.SemaphoreType.DMA((SLOTS_IN_FLIGHT + 1,)),
            pltpu.SemaphoreType.DMA((S,)),
            pltpu.SemaphoreType.DMA((24, T - 1)),
            pltpu.SemaphoreType.DMA((24, T - 1)),
            pltpu.SemaphoreType.DMA((14, max(C - 1, 1))),
            pltpu.SemaphoreType.DMA((14, max(C - 1, 1))),
            pltpu.SemaphoreType.DMA((8 + 2 * C,)),
            pltpu.SemaphoreType.DMA((8 + 2 * C,)),
        ]
        shape = jax.ShapeDtypeStruct
        outs = pl.pallas_call(
            functools.partial(layer_kernel, z),
            out_shape=[
                shape((S, L, D), BF16),
                shape((S, z.Mt, D), BF16),
                shape((S, L, D), BF16),
                shape((R, 3 * I), F32),
                shape((R, I), F32),
                shape((R, F), F32),
                shape((R, F), F32),
                shape((8, D), F32),
            ],
            in_specs=[pl.BlockSpec(memory_space=pltpu.SMEM)] + [hbm] * 3 + [vmem] * 6 + [hbm] * 6,
            out_specs=[vmem, hbm] + [vmem] * 6,
            scratch_shapes=scratch,
            compiler_params=pltpu.CompilerParams(
                collective_id=0, has_side_effects=True, vmem_limit_bytes=63 * 1024 * 1024
            ),
            name="resampler_layer",
        )(
            image_counts,
            media_tokens,
            latents.reshape(S * L, D),
            cotangent.reshape(S * L, D),
            row(media_gain),
            row(media_shift),
            row(latent_gain),
            row(latent_shift),
            row(feed_gain),
            row(feed_shift),
            query_weight.reshape(C, 2, R, I),
            key_weight.reshape(C, 2, R, I),
            value_weight.reshape(C, 2, R, I),
            output_weight,
            up_weight,
            down_weight,
        )
        final = pl.pallas_call(
            functools.partial(hand_out, z),
            out_shape=[
                shape((S, L, D), BF16),
                shape((S, z.Mt, D), BF16),
                shape((S, L, D), BF16),
                shape((R, I), F32),
                shape((R, I), F32),
                shape((R, I), F32),
                shape((I, R), F32),
                shape((R, F), F32),
                shape((F, R), F32),
                shape((1, D), F32),
                shape((1, D), F32),
            ]
            + [shape((1, R), F32)] * 4,
            in_specs=[hbm] * 8,
            out_specs=[hbm] * 15,
            scratch_shapes=[V(out.shape, out.dtype) for out in outs]
            + [V((F, R), F32), V((I, R), F32)]
            + [V((1, R), F32)] * 5
            + [pltpu.SemaphoreType.DMA((8,)), pltpu.SemaphoreType.DMA((15,))],
            name="hand_out",
        )(*outs)
        return tuple(final[:9]) + tuple(v.reshape(-1) for v in final[9:])

    placed = (
        P("dp", None, None),
        P("dp", None, None),
        P("dp"),
        P(),
        P(),
        P(),
        P(),
        P(),
        P(),
        P(None, "tensor"),
        P(None, "tensor"),
        P(None, "tensor"),
        P("tensor", None),
        P("dp", "tensor"),
        P("tensor", "dp"),
        P("dp", None, None),
    )
    return jax.shard_map(
        on_device,
        mesh=mesh,
        in_specs=placed,
        out_specs=(
            P("dp", None, None),
            P("dp", "tensor", None),
            P("dp", None, None),
            P("dp", "tensor"),
            P("dp", "tensor"),
            P("dp", "tensor"),
            P("tensor", "dp"),
            P("dp", "tensor"),
            P("tensor", "dp"),
            P(),
            P(),
            P("dp"),
            P("dp"),
            P("dp"),
            P("dp"),
        ),
        check_vma=False,
    )
```

```python
import functools

import jax
import jax.numpy as jnp
from jax import lax
from jax.experimental import pallas as pl
from jax.experimental.pallas import tpu as pltpu
from jax.sharding import PartitionSpec as P

HEAD_DIM = 64
PATCH = 256
EPSILON = 1e-05
NEGATIVE = -1e30
SQRT_HALF = 0.7071067811865476
INV_ROOT_TWO_PI = 0.3989422804014327
F32 = jnp.float32
BF16 = jnp.bfloat16
MESH = pl.DeviceIdType.MESH
BLOCK = 256
ROWS = 32
SLOTS_IN_FLIGHT = 3


def nn(left, right):
    return lax.dot_general(left, right, (((1,), (0,)), ((), ())), preferred_element_type=F32)


def nt(left, right):
    return lax.dot_general(left, right, (((1,), (1,)), ((), ())), preferred_element_type=F32)


def tn(left, right):
    return lax.dot_general(left, right, (((0,), (0,)), ((), ())), preferred_element_type=F32)


def unit_rows(x):
    centre = x - jnp.mean(x, axis=-1, keepdims=True)
    scale_inv = lax.rsqrt(jnp.mean(centre * centre, axis=-1, keepdims=True) + EPSILON)
    return centre * scale_inv, scale_inv


def norm_back(unit, scale_inv, gain, upstream):
    scaled = upstream * gain
    inner = scaled - jnp.mean(scaled, axis=-1, keepdims=True)
    inner = inner - unit * jnp.mean(scaled * unit, axis=-1, keepdims=True)
    return inner * scale_inv


def fold(x):
    return jnp.sum(x.reshape(x.shape[0] // 8, 8, x.shape[1]), axis=0)


class Sizes:
    def __init__(self, tensor, dp, samples, lat, slots, width, hidden, inner):
        self.T, self.N, self.C = tensor, dp, dp // 2
        self.S, self.L, self.M, self.D = samples, lat, slots, width
        self.F, self.I = hidden, inner
        self.R = width // dp
        self.Lt, self.Mt = lat // tensor, slots // tensor
        self.Kt = self.Lt + self.Mt
        self.K = lat + slots
        self.H = inner // HEAD_DIM
        self.q = self.H * lat
        self.G = min(2, tensor)


def layer_kernel(
    z,
    counts,
    media,
    lat_h,
    cot_h,
    mgain,
    mshift,
    lgain,
    lshift,
    fgain,
    fshift,
    wq,
    wk,
    wv,
    wo,
    up,
    dn,
    new_lat,
    media_grad,
    lat_grad,
    g_qkv,
    g_o,
    g_up,
    g_dn,
    g_vec,
    lat,
    cot,
    dn_v,
    wo_v,
    wq_b,
    wo_b,
    up_b,
    dn_b,
    mbuf,
    mown,
    xn,
    ctx,
    latn,
    att,
    lse,
    qall,
    kall,
    vall,
    pall,
    pairs,
    res,
    hin,
    act,
    bgr,
    hg,
    hgr,
    fp,
    fpr,
    og,
    rgr,
    dob,
    dos,
    dqb,
    dqr,
    st_up,
    st_dn,
    st_o,
    st_qkv,
    cr_up,
    cr_dn,
    cr_o,
    cr_qkv,
    xr_up,
    xr_dn,
    xr_o,
    xr_qkv,
    zb_o,
    zb_qkv,
    zr_o,
    zr_qkv,
    mgl,
    acc,
    vst,
    vcr,
    vx,
    vz,
    lsem,
    msem,
    osem,
    zs,
    zr,
    xs,
    xr,
    cs,
    cr,
):
    T, N, C, S, L, M, D = z.T, z.N, z.C, z.S, z.L, z.M, z.D
    F, I, R, Lt, Mt, Kt, G = z.F, z.I, z.R, z.Lt, z.Mt, z.Kt, z.G
    GI = G * I
    groups = T // G
    scale_factor = HEAD_DIM ** (-0.5)
    t = lax.axis_index("tensor")
    d = lax.axis_index("dp")
    c = lax.div(d, 2)
    core = lax.rem(d, 2)
    other = 1 - core
    n = BLOCK // (2 * R)
    blocks = D // BLOCK
    count = {"z": 0, "x": 0, "c": 0}
    started = []

    def row(kind):
        count[kind] += 1
        return count[kind] - 1

    def start(copies):
        for copy in copies:
            copy.start()
        started.extend(copies)

    def arrive(copies):
        for copy in copies:
            copy.wait_recv()

    def z_dev(k):
        return (d, lax.rem(t + k, T))

    def x_dev(j):
        return (2 * lax.rem(c + j, C) + core, t)

    core_dev = (d + 1 - 2 * core, t)

    def head(k):
        return lax.rem(t - k + T, T)

    def my_rows(k=0):
        return pl.ds(pl.multiple_of(lax.rem(t + k, T) * Lt, Lt), Lt)

    def remote(src, dst, send, recv, dev):
        return pltpu.make_async_remote_copy(
            src_ref=src, dst_ref=dst, send_sem=send, recv_sem=recv, device_id=dev, device_id_type=MESH
        )

    def over_z(pick):
        i = row("z")
        return [remote(*pick(k), zs.at[i, k - 1], zr.at[i, k - 1], z_dev(k)) for k in range(1, T)]

    def line_share(pick):
        ways = []
        for step in (1, -1):
            i = row("z")
            hops = []
            for h in range(1, T):
                owner, fresh = t - step * (h - 1), t - step * h
                beyond = t + step
                sends = (owner >= 0) & (owner < T) & (beyond >= 0) & (beyond < T)
                comes = (fresh >= 0) & (fresh < T)
                mine, theirs = pick(my_rows(T - step * (h - 1))), pick(my_rows(T - step * h))
                dev = (d, lax.rem(t + step + T, T))
                sems = (zs.at[i, h - 1], zr.at[i, h - 1])
                hops.append((sends, remote(mine, mine, *sems, dev), comes, remote(theirs, theirs, *sems, dev)))
            ways.append(hops)

        def hop(h, last=False):
            if h >= T and not last:
                return
            for hops in ways:
                if h > 1:
                    pl.when(hops[h - 2][2])(hops[h - 2][3].wait_recv)
                if h < T:
                    pl.when(hops[h - 1][0])(hops[h - 1][1].start)

        def end():
            hop(T, last=True)
            for hops in ways:
                for sends, copy, _, _ in hops:
                    pl.when(sends)(copy.wait_send)

        return hop, end

    def over_core(src, dst):
        i = row("c")
        return [remote(src, dst, cs.at[i], cr.at[i], core_dev)]

    bits = C.bit_length() - 1
    x_first = list(range(bits))
    y_first = x_first[::-1]

    def flip(chip, mask):
        for bit in range(bits):
            if mask >> bit & 1:
                chip = chip + (1 - 2 * lax.rem(lax.div(chip, 1 << bit), 2)) * (1 << bit)
        return chip

    def subsets(order):
        masks = [0]
        for bit in order:
            masks = masks + [m | 1 << bit for m in masks]
        return masks

    def gather_steps(view, order):
        i, at, rests = row("x"), 0, []
        firsts = ([], [])
        for step, bit in enumerate(order):
            peer = flip(c, 1 << bit)
            dev = (2 * peer + core, t)
            rest = ([], [])
            for m in subsets(order[:step]):
                sems = (xs.at[i, at], xr.at[i, at])
                mine, theirs = view(flip(c, m)), view(flip(peer, m))
                out, came = rest if m else firsts
                out.append(remote(mine, mine, *sems, dev))
                came.append(remote(theirs, theirs, *sems, dev))
                at += 1
            if step:
                rests.append(rest)
        return firsts, rests

    def gather_rest(gather):
        firsts, rests = gather
        for step, rest in enumerate(rests):
            arrive([firsts[1][step]])
            if step:
                arrive(rests[step - 1][1])
            start(rest[0])

    def gather_near(gather):
        arrive([gather[0][1][-1]])

    def gather_done(gather):
        if gather[1]:
            arrive(gather[1][-1][1])

    def scatter_steps(view, land, order):
        i, at, steps = row("x"), 0, []
        for step, bit in enumerate(order):
            peer = flip(c, 1 << bit)
            dev = (2 * peer + core, t)
            out, keep = [], []
            for m in subsets(order[step + 1 :]):
                out.append(remote(view(flip(peer, m)), land(at), xs.at[i, at], xr.at[i, at], dev))
                keep.append((flip(c, m), at))
                at += 1
            steps.append((out, keep))
        return steps

    n_tiles = S * T

    def tile_copy(i):
        slot = lax.rem(i, SLOTS_IN_FLIGHT)
        s, r = lax.div(i, T), lax.rem(i, T)
        return pltpu.make_async_copy(
            media.at[s, pl.ds(pl.multiple_of(r * Mt, Mt), Mt)], mbuf.at[slot], msem.at[slot]
        )

    own_copy = pltpu.make_async_copy(
        media.at[:, pl.ds(pl.multiple_of(t * Mt, Mt), Mt)], mown, msem.at[SLOTS_IN_FLIGHT]
    )
    barrier = pltpu.get_barrier_semaphore()

    def greet(dev):
        pl.semaphore_signal(barrier, inc=1, device_id=dev, device_id_type=MESH)

    for k in range(1, T):
        greet(z_dev(k))
    lax.fori_loop(1, C, lambda j, carry: (greet(x_dev(j)), carry)[1], 0)
    greet(core_dev)
    loads = [
        pltpu.make_async_copy(src, dst, lsem.at[i])
        for i, (src, dst) in enumerate(
            [(up, up_b.at[c, core]), (dn, dn_v), (wo, wo_v)]
            + [(w, wq_b.at[0, m]) for m, w in enumerate((wq, wk, wv))]
            + [(lat_h, lat), (cot_h, cot)]
        )
    ]
    for copy in loads:
        copy.start()
    for i in range(min(SLOTS_IN_FLIGHT, n_tiles)):
        tile_copy(i).start()
    for copy in loads[:3]:
        copy.wait()
    dn_b[c, core] = dn_v[...].T
    wo_b[0] = wo_v[...].T.reshape(C, 2, R, I)
    pl.semaphore_wait(barrier, T + C - 1)

    foreign = pl.ds(1, T - 1)
    up_x = gather_steps(lambda chip: up_b.at[chip, core], x_first)
    dn_x = gather_steps(lambda chip: dn_b.at[chip, core], y_first)
    wo_x = gather_steps(lambda chip: wo_b.at[foreign, chip, core], x_first)
    qk_x = gather_steps(lambda chip: wq_b.at[foreign, pl.ds(0, 2), chip, core], x_first)
    v_x = gather_steps(lambda chip: wq_b.at[foreign, 2, chip, core], y_first)
    wo_z = over_z(lambda k: (wo_b.at[0, c, core], wo_b.at[k, c, core]))
    wq_z = over_z(lambda k: (wq_b.at[0, :, c, core], wq_b.at[k, :, c, core]))
    near = [0] + [1 << bit for bit in range(bits)]
    far = [m for m in range(C) if m not in near]

    def relay(ref, masks):
        return [copy for m in masks for copy in over_core(ref.at[flip(c, m), core], ref.at[flip(c, m), core])]

    feed_near = relay(up_b, near) + relay(dn_b, near)
    feed_far = relay(up_b, far) + relay(dn_b, far)
    wo_c = over_core(wo_b.at[foreign, :, core], wo_b.at[foreign, :, core])
    wq_c = over_core(wq_b.at[foreign, :, :, core], wq_b.at[foreign, :, :, core])

    for way in range(bits):
        start([up_x[0][0][way], dn_x[0][0][way]])
    start(wo_z)
    for copy in loads[3:]:
        copy.wait()
    start(wq_z)
    own_copy.start()

    for b in range(S * L // ROWS):
        rows = pl.ds(b * ROWS, ROWS)
        unit, _ = unit_rows(lat[rows, :].astype(F32))
        latn[rows, :] = (unit * lgain[...] + lshift[...]).astype(BF16)
    def head_weights(k, ms):
        return jnp.concatenate([wq_b[k, m].reshape(D, I) for m in ms], axis=1)

    own_qkv = nn(latn[...], head_weights(0, range(3))).astype(BF16)
    qall[:, pl.ds(0, I)] = own_qkv[:, :I]
    for s in range(S):
        pairs[pl.ds(M, L), pl.ds(s * 2 * I, 2 * I)] = own_qkv[s * L : (s + 1) * L, I:]
        ctx[pl.ds(s * Kt + Mt, Lt), :] = latn[pl.ds(pl.multiple_of(s * L + t * Lt, Lt), Lt), :]

    def tile_norm(i, half):
        slot = lax.rem(i, SLOTS_IN_FLIGHT)
        for b in range(Mt // ROWS):
            rows = pl.ds(b * ROWS, ROWS)
            unit, _ = unit_rows(mbuf[slot, rows, :].astype(F32))
            xn[half, rows, :] = (unit * mgain[...] + mshift[...]).astype(BF16)

    def tile_pair(i, half):
        s, r = lax.div(i, T), lax.rem(i, T)
        pair = nn(xn[half], head_weights(0, (1, 2)))
        lanes = pl.ds(pl.multiple_of(s * 2 * I, 2 * I), 2 * I)
        pairs[pl.ds(pl.multiple_of(r * Mt, Mt), Mt), lanes] = pair.astype(BF16)

    def tile_keep(i, half):
        s, r = lax.div(i, T), lax.rem(i, T)

        @pl.when(r == t)
        def _():
            ctx[pl.ds(pl.multiple_of(s * Kt, 16), Mt), :] = xn[half]

    def tile_next(i):
        @pl.when(i + SLOTS_IN_FLIGHT < n_tiles)
        def _():
            tile_copy(i + SLOTS_IN_FLIGHT).start()

    tile_copy(0).wait()
    tile_norm(0, 0)
    tile_next(0)

    def two_tiles(j, carry):
        i = 2 * j
        tile_copy(i + 1).wait()

        @pl.when(i + 2 < n_tiles)
        def _():
            tile_copy(i + 2).wait()

        tile_keep(i, 0)
        tile_pair(i, 0)
        tile_norm(i + 1, 1)
        tile_keep(i + 1, 1)
        tile_pair(i + 1, 1)
        tile_norm(lax.rem(i + 2, n_tiles), 0)
        tile_next(i + 1)
        tile_next(i + 2)
        return carry

    first = n_tiles // 8
    lax.fori_loop(0, first, two_tiles, 0)
    arrive(wo_z)
    start(wo_x[0][0])
    lax.fori_loop(first, n_tiles // 2, two_tiles, 0)
    gather_rest(up_x)
    gather_rest(dn_x)
    gather_rest(wo_x)

    def spread(x):
        lane_head = lax.broadcasted_iota(jnp.int32, (1, x.shape[1]), 1) // HEAD_DIM
        zero = jnp.zeros_like(x)
        return jnp.concatenate(
            [jnp.where(lane_head == h, x, zero) for h in range(x.shape[1] // HEAD_DIM)], axis=0
        )

    def gather_heads(x):
        lane_head = lax.broadcasted_iota(jnp.int32, (1, x.shape[1]), 1) // HEAD_DIM
        out = x[:L]
        for h in range(1, x.shape[1] // HEAD_DIM):
            out = jnp.where(lane_head == h, x[h * L : (h + 1) * L], out)
        return out

    att_z = []
    for s in range(S):
        keys = pairs[pl.ds(0, z.K), pl.ds(s * 2 * I, I)]
        values = pairs[pl.ds(0, z.K), pl.ds(s * 2 * I + I, I)]
        scores = nt(keys, spread(qall[pl.ds(s * L, L), pl.ds(0, I)])) * scale_factor
        slot = lax.broadcasted_iota(jnp.int32, (z.K, 1), 0)
        valid = (slot < counts[s] * PATCH) | (slot >= M)
        scores = jnp.where(valid, scores, NEGATIVE)
        largest = jnp.max(scores, axis=0, keepdims=True)
        total = largest + jnp.log(jnp.sum(jnp.exp(scores - largest), axis=0, keepdims=True))
        probs = jnp.exp(scores - total).astype(BF16)
        att[0, s] = gather_heads(tn(probs, values)).astype(BF16)
        lse[0, pl.ds(s, 1), :] = total
        if s % 2 == 1:
            now = over_z(lambda k, s=s: (att.at[0, pl.ds(s - 1, 2)], att.at[k, pl.ds(s - 1, 2)]))
            start(now)
            att_z += now
    lse_z = over_z(lambda k: (lse.at[0], lse.at[k]))
    start(lse_z)

    for s in range(S):
        lanes = s * 2 * I
        own_slots = pl.ds(pl.multiple_of(t * Mt, Mt), Mt)
        own_lat = pl.ds(pl.multiple_of(M + t * Lt, Lt), Lt)
        for m, ref in enumerate((kall, vall)):
            ref[pl.ds(s * Kt, Mt), pl.ds(0, I)] = pairs[own_slots, pl.ds(lanes + m * I, I)]
            ref[pl.ds(s * Kt + Mt, Lt), pl.ds(0, I)] = pairs[own_lat, pl.ds(lanes + m * I, I)]
    gather_near(wo_x)
    gather_near(up_x)
    gather_near(dn_x)
    start(feed_near)
    gather_done(wo_x)
    start(wo_c)
    arrive(wq_z)
    start(qk_x[0][0])
    start(v_x[0][0])
    gather_done(up_x)
    gather_done(dn_x)
    start(feed_far)

    def heads_wo():
        return jnp.concatenate([wo_b[k].reshape(D, I) for k in range(T)], axis=1)

    arrive(wo_c)
    arrive(att_z)
    att_all = jnp.concatenate([att[k].reshape(S * L, I) for k in range(T)], axis=1)
    res[...] = lat[...].astype(F32) + nt(att_all, heads_wo())
    for b in range(S * L // ROWS):
        rows = pl.ds(b * ROWS, ROWS)
        unit, _ = unit_rows(res[rows, :])
        hin[rows, :] = (unit * fgain[...] + fshift[...]).astype(BF16)

    arrive(feed_near)
    arrive(feed_far)

    def feed(b, carry):
        cols = pl.ds(pl.multiple_of(b * BLOCK, BLOCK), BLOCK)
        before = nn(hin[...], up_b[:, :, :, cols].reshape(D, BLOCK))
        cdf = 0.5 * (1.0 + lax.erf(before * SQRT_HALF))
        act[:, cols] = (before * cdf).astype(BF16)
        slope = cdf + before * INV_ROOT_TWO_PI * jnp.exp(-0.5 * before * before)
        act_grad = nn(cot[...], dn_b[:, :, :, cols].reshape(D, BLOCK)).astype(BF16)
        bgr[:, cols] = (act_grad.astype(F32) * slope).astype(BF16)
        return carry

    lax.fori_loop(0, F // BLOCK, feed, 0, unroll=2)
    gather_rest(qk_x)
    gather_rest(v_x)

    def back_to_width(left, weight, out, b):
        block = nt(left[...], weight[pl.ds(b * n, n)].reshape(BLOCK, F))
        block = block.astype(BF16)
        for s in range(S):
            for u in range(T):
                first = s * L + u * Lt
                out[u, pl.ds(s * Lt, Lt), pl.ds(b * BLOCK, BLOCK)] = block[first : first + Lt]

    for b in range(blocks):
        back_to_width(bgr, up_b, hg, b)
    hg_z = over_z(lambda k: (hg.at[lax.rem(t + k, T)], hgr.at[k - 1]))
    start(hg_z)

    def feed_weights(left, right, out, b):
        block = tn(left[:, pl.ds(b * BLOCK, BLOCK)], right[...]).astype(BF16)
        out[pl.ds(b * n, n)] = block.reshape(n, 2, R, F)

    for b in range(blocks):
        feed_weights(hin, bgr, st_up, b)
    st_up_c = over_core(st_up.at[:, other], cr_up)
    start(st_up_c)
    for b in range(blocks):
        feed_weights(cot, act, st_dn, b)
    st_dn_c = over_core(st_dn.at[:, other], cr_dn)
    start(st_dn_c)
    for b in range(blocks):
        back_to_width(act, dn_b, fp, b)

    up_g = scatter_steps(lambda chip: st_up.at[chip, core], lambda at: xr_up.at[at], y_first)
    dn_g = scatter_steps(lambda chip: st_dn.at[chip, core], lambda at: xr_dn.at[at], x_first)

    def feed_core(copy, st, came, steps):
        arrive(copy)
        sent = steps[0][0]
        for m in subsets(range(bits)):
            chip = flip(c, m)
            st[chip, core] = (st[chip, core].astype(F32) + came[chip].astype(F32)).astype(BF16)
        start(sent)

    def feed_step(st, land, steps):
        for step in range(1, len(steps)):
            arrive(steps[step - 1][0])
            for chip, at in steps[step - 1][1]:
                st[chip, core] = (st[chip, core].astype(F32) + land[at].astype(F32)).astype(BF16)
            start(steps[step][0])

    def feed_last(st, land, steps, out):
        arrive(steps[-1][0])
        out[...] = st[c, core].astype(F32) + land[steps[-1][1][0][1]].astype(F32)

    feed_core(st_up_c, st_up, cr_up, up_g)
    feed_core(st_dn_c, st_dn, cr_dn, dn_g)

    for gather in (qk_x, v_x):
        gather_near(gather)
        gather_done(gather)
    start(wq_c)
    own_copy.wait()
    arrive(wq_c)
    for k in range(1, T):
        qall[:, pl.ds(k * I, I)] = nn(latn[...], head_weights(k, (0,))).astype(BF16)
    half_rows = S * Kt // 2

    def all_pairs(i, carry):
        k = lax.div(i, 2)
        rows = pl.ds(pl.multiple_of(lax.rem(i, 2) * half_rows, 16), half_rows)
        lanes = pl.ds(pl.multiple_of(k * I, I), I)
        pair = nn(ctx[rows, :], head_weights(k, (1, 2))).astype(BF16)
        kall[rows, lanes] = pair[:, :I]
        vall[rows, lanes] = pair[:, I:]
        return carry

    lax.fori_loop(2, 2 * T, all_pairs, 0)
    arrive(lse_z)
    slot_of = lax.broadcasted_iota(jnp.int32, (Kt, 1), 0)

    def group(g, s):
        rows = pl.ds(pl.multiple_of(s * Kt, 16), Kt)
        lat_rows = pl.ds(pl.multiple_of(s * L, L), L)
        return rows, pl.ds(g * GI, GI), lat_rows

    def joined(g, pick):
        return jnp.concatenate([pick(g * G + j) for j in range(G)], axis=1)

    for g in range(groups):

        def probabilities(s, carry, g=g):
            rows, lanes, lat_rows = group(g, s)
            scores = nt(kall[rows, lanes], spread(qall[lat_rows, lanes])) * scale_factor
            valid = (slot_of + t * Mt < counts[s] * PATCH) | (slot_of >= Mt)
            scores = jnp.where(valid, scores, NEGATIVE)
            pall[g * S + s] = jnp.exp(scores - joined(g, lambda k: lse[k, pl.ds(s, 1), :]))
            return carry

        lax.fori_loop(0, S, probabilities, 0, unroll=2)

    arrive(hg_z)
    feed_gain_part = jnp.zeros((1, D), F32)
    feed_shift_part = jnp.zeros((1, D), F32)
    for s in range(S):
        own = pl.ds(pl.multiple_of(s * L + t * Lt, Lt), Lt)
        unit, scale_inv = unit_rows(res[own, :])
        upstream = hg[t, pl.ds(s * Lt, Lt), :].astype(F32)
        for k in range(1, T):
            upstream = upstream + hgr[k - 1, pl.ds(s * Lt, Lt), :].astype(F32)
        back = cot[own, :].astype(F32) + norm_back(unit, scale_inv, fgain[...], upstream)
        feed_gain_part = feed_gain_part + jnp.sum(upstream * unit, axis=0, keepdims=True)
        feed_shift_part = feed_shift_part + jnp.sum(upstream, axis=0, keepdims=True)
        rgr[pl.ds(s * Lt, Lt), :] = back
        og[pl.ds(s * Lt, Lt), :] = back.astype(BF16)
    vst[...] = jnp.concatenate(
        [jnp.zeros((4, D), F32), feed_gain_part, feed_shift_part, jnp.zeros((2, D), F32)], axis=0
    )
    dos[0] = nn(og[...], heads_wo()).astype(BF16)
    turns = list(range(groups))[::-1]
    group_heads = [range(g * G, (g + 1) * G) for g in range(groups)]
    do_z = over_z(lambda k: (dos.at[0], dos.at[k]))
    start(do_z)

    att_own = jnp.concatenate([att[k, :, my_rows(), :].reshape(S * Lt, I) for k in range(T)], axis=1)
    for b in range(blocks):
        block = tn(og[:, pl.ds(b * BLOCK, BLOCK)], att_own).astype(BF16)
        for k in range(T):
            st_o[k, pl.ds(b * n, n)] = block[:, k * I : (k + 1) * I].reshape(n, 2, R, I)
    st_o_c = over_core(st_o.at[:, :, other], cr_o)
    start(st_o_c)

    def heads_core(st, came, ks, steps):
        for m in subsets(range(bits)):
            chip = flip(c, m)
            for k in ks:
                st[k, chip, core] = (st[k, chip, core].astype(F32) + came[k, chip].astype(F32)).astype(BF16)
        start(steps[0][0])

    def heads_step(st, land, ks, steps):
        for step in range(1, len(steps)):
            arrive(steps[step - 1][0])
            for chip, at in steps[step - 1][1]:
                for j, k in enumerate(ks):
                    st[k, chip, core] = (st[k, chip, core].astype(F32) + land[at, j].astype(F32)).astype(BF16)
            start(steps[step][0])

    def heads_last(st, land, ks, steps, held, came):
        arrive(steps[-1][0])
        at = steps[-1][1][0][1]
        for j, k in enumerate(ks):
            held[k] = (st[k, c, core].astype(F32) + land[at, j].astype(F32)).astype(BF16)
        i = row("z")
        copies = [
            remote(held.at[k], came.at[T - k - 1], zs.at[i, k - 1], zr.at[i, T - k - 1], (d, head(k)))
            for k in ks
            if k
        ]
        start(copies)
        return copies

    orders = (x_first, y_first)
    o_heads = [range(g * T // 2, (g + 1) * T // 2) for g in range(2)]
    o_steps = [
        scatter_steps(
            lambda chip, g=g: st_o.at[pl.ds(g * T // 2, T // 2), chip, core], lambda at, g=g: xr_o.at[g, at], orders[g]
        )
        for g in range(2)
    ]
    arrive(st_o_c)
    for g in range(2):
        heads_core(st_o, cr_o, o_heads[g], o_steps[g])

    arrive(do_z)
    for m in range(T):
        for k in range(T):
            lanes = pl.ds((k - m) % T * I, I)
            dob[k, :, my_rows(T - m), :] = dos[m, :, lanes].reshape(S, Lt, I)

    def attend_back(s, carry, g):
        rows, lanes, lat_rows = group(g, s)
        keys = kall[rows, lanes]
        queries = spread(qall[lat_rows, lanes])
        grads = spread(joined(g, lambda k: dob[k, s]))
        outs = spread(joined(g, lambda k: att[k, s]))
        product = grads.astype(F32) * outs.astype(F32)
        inner = lax.dot_general(
            jnp.ones((8, GI), F32),
            product,
            (((1,), (1,)), ((), ())),
            preferred_element_type=F32,
            precision=lax.Precision.HIGHEST,
        )[:1]
        probs = pall[g * S + s]
        score_grad = (probs * (nt(vall[rows, lanes], grads) - inner)).astype(BF16)
        pairs[rows, lanes] = (nn(score_grad, queries) * scale_factor).astype(BF16)
        pairs[rows, pl.ds(T * I + g * GI, GI)] = nn(probs.astype(BF16), grads).astype(BF16)
        query_grad = (gather_heads(tn(score_grad, keys)) * scale_factor).astype(BF16)
        for j in range(G):
            for u in range(T):
                rows_u = pl.ds(pl.multiple_of(s * Lt, Lt), Lt)
                dqb[u, g * G + j, rows_u, :] = query_grad[u * Lt : (u + 1) * Lt, j * I : (j + 1) * I]
        return carry

    def group_weights(g):
        query_part = jnp.concatenate(
            [
                jnp.concatenate([dqb[u, g * G + j, pl.ds(s * Lt, Lt), :] for s in range(S) for u in range(T)], axis=0)
                for j in range(G)
            ],
            axis=1,
        )
        all_rows = pl.ds(0, S * Kt)
        part = jnp.concatenate(
            [pairs[all_rows, pl.ds(g * GI, GI)], pairs[all_rows, pl.ds(T * I + g * GI, GI)]], axis=1
        )
        for b in range(blocks):
            cols = pl.ds(b * BLOCK, BLOCK)
            block = tn(ctx[:, cols], part).astype(BF16)
            query_block = tn(latn[:, cols], query_part).astype(BF16)
            for j in range(G):
                lanes = slice(j * I, (j + 1) * I)
                pieces = (query_block[:, lanes], block[:, lanes], block[:, GI:][:, lanes])
                for m, piece in enumerate(pieces):
                    st_qkv[g * G + j, pl.ds(b * n, n), :, :, pl.ds(m * I, I)] = piece.reshape(n, 2, R, I)
        ks = pl.ds(g * G, G)
        copy = over_core(st_qkv.at[ks, :, other], cr_qkv.at[ks])
        start(copy)
        return copy

    q_steps = [
        scatter_steps(lambda chip, k=k: st_qkv.at[pl.ds(k, 1), chip, core], lambda at, k=k: xr_qkv.at[k, at], orders[k % 2])
        for k in range(T)
    ]
    q_c, dq_z = {}, []

    def group_core(g):
        arrive(q_c[g])
        for k in group_heads[g]:
            heads_core(st_qkv, cr_qkv, (k,), q_steps[k])

    def group_step(g):
        for k in group_heads[g]:
            heads_step(st_qkv, xr_qkv.at[k], (k,), q_steps[k])

    def group_last(g):
        out = []
        for k in group_heads[g]:
            out += heads_last(st_qkv, xr_qkv.at[k], (k,), q_steps[k], zb_qkv, zr_qkv)
        return out

    fp_z = over_z(lambda k: (fp.at[lax.rem(t + k, T)], fpr.at[k - 1]))
    if groups > 1:
        start(fp_z)
        feed_step(st_up, xr_up, up_g)
        feed_step(st_dn, xr_dn, dn_g)
    def new_rows():
        arrive(fp_z)
        for s in range(S):
            own = pl.ds(pl.multiple_of(s * L + t * Lt, Lt), Lt)
            total = fp[t, pl.ds(s * Lt, Lt), :].astype(F32)
            for k in range(1, T):
                total = total + fpr[k - 1, pl.ds(s * Lt, Lt), :].astype(F32)
            new_lat[s, my_rows(), :] = (res[own, :] + total).astype(BF16)

    nl_hop, nl_end = line_share(lambda rows: new_lat.at[:, rows, :])
    for turn, g in enumerate(turns):
        if turn <= 1:
            if turn == 0 and groups > 1:
                lax.fori_loop(0, S // 2, functools.partial(attend_back, g=g), 0, unroll=2)
                lax.fori_loop(S // 2, S, functools.partial(attend_back, g=g), 0, unroll=2)
            else:
                lax.fori_loop(0, S // 2, functools.partial(attend_back, g=g), 0, unroll=2)
                if turn:
                    group_core(turns[turn - 1])
                else:
                    start(fp_z)
                lax.fori_loop(S // 2, S, functools.partial(attend_back, g=g), 0, unroll=2)
        else:
            group_core(turns[turn - 1])
            lax.fori_loop(0, S, functools.partial(attend_back, g=g), 0, unroll=2)
        ks = pl.ds(g * G, G)
        now = over_z(lambda m, ks=ks: (dqb.at[lax.rem(t + m, T), ks], dqr.at[m - 1, ks]))
        start(now)
        dq_z += now
        if turn == groups - 1:
            new_rows()
            nl_hop(1)
        q_c[g] = group_weights(g)
    if groups == 1:
        feed_step(st_up, xr_up, up_g)
        feed_step(st_dn, xr_dn, dn_g)
    for g in range(2):
        heads_step(st_o, xr_o.at[g], o_heads[g], o_steps[g])

    acc[...] = jnp.zeros_like(acc)

    def width(s, rows):
        return jnp.concatenate([pall[s % 2 * blocks + b, rows, :] for b in range(blocks)], axis=1)

    def width_weights(b):
        return jnp.concatenate(
            [wq_b[k, m, pl.ds(b * n, n)].reshape(BLOCK, I) for m in (1, 2) for k in range(T)], axis=1
        )

    def media_width(s):
        for b in range(blocks):
            pall[s % 2 * blocks + b] = nt(pairs[pl.ds(s * Kt, Kt), pl.ds(0, 2 * T * I)], width_weights(b))

    lat_pairs = jnp.concatenate(
        [pairs[pl.ds(s * Kt + Mt, Lt), pl.ds(0, 2 * T * I)] for s in range(S)], axis=0
    )
    for b in range(blocks):
        mgl[:, pl.ds(b * BLOCK, BLOCK)] = nt(lat_pairs, width_weights(b))

    def media_rows(s):
        for b in range(Mt // ROWS):
            rows = pl.ds(b * ROWS, ROWS)
            unit, scale_inv = unit_rows(mown[s, rows, :].astype(F32))
            upstream = width(s, rows)
            mown[s, rows, :] = norm_back(unit, scale_inv, mgain[...], upstream).astype(BF16)
            acc[0] += fold(upstream * unit)
            acc[1] += fold(upstream)
        pltpu.make_async_copy(mown.at[s], media_grad.at[s], osem.at[s]).start()

    media_width(0)
    media_width(1)
    group_core(turns[-1])
    media_rows(0)
    nl_hop(2)

    arrive(dq_z)
    upstream_all = mgl[...]
    for k in range(T):
        total = dqb[t, k].astype(F32)
        for m in range(1, T):
            total = total + dqr[m - 1, (k - m) % T].astype(F32)
        weights = head_weights(k, (0,))
        upstream_all = upstream_all + nt(total.astype(BF16), weights)
    mgl[...] = upstream_all
    lat_gain_part = jnp.zeros((1, D), F32)
    lat_shift_part = jnp.zeros((1, D), F32)
    for s in range(S):
        own = pl.ds(pl.multiple_of(s * L + t * Lt, Lt), Lt)
        unit, scale_inv = unit_rows(lat[own, :].astype(F32))
        upstream = mgl[pl.ds(s * Lt, Lt), :]
        back = rgr[pl.ds(s * Lt, Lt), :] + norm_back(unit, scale_inv, lgain[...], upstream)
        lat_grad[s, my_rows(), :] = back.astype(BF16)
        lat_gain_part = lat_gain_part + jnp.sum(upstream * unit, axis=0, keepdims=True)
        lat_shift_part = lat_shift_part + jnp.sum(upstream, axis=0, keepdims=True)
    lg_hop, lg_end = line_share(lambda rows: lat_grad.at[:, rows, :])
    lg_hop(1)

    for g in turns[:-1]:
        group_step(g)
    o_z = []
    for g in range(2):
        o_z += heads_last(st_o, xr_o.at[g], o_heads[g], o_steps[g], zb_o, zr_o)
    for s in range(1, S):
        if s + 1 < S:
            media_width(s + 1)
        media_rows(s)
    for h in range(3, T):
        nl_hop(h)
    group_step(turns[-1])
    q_z = []
    for g in turns[:-1]:
        q_z += group_last(g)
    lg_hop(2)

    vst[...] += jnp.concatenate(
        [
            jnp.sum(acc[0], axis=0, keepdims=True),
            jnp.sum(acc[1], axis=0, keepdims=True),
            lat_gain_part,
            lat_shift_part,
            jnp.zeros((4, D), F32),
        ],
        axis=0,
    )
    vec_c = over_core(vst, vcr)
    start(vec_c)
    arrive(vec_c)
    vx[c] = vst[...] + vcr[...]
    vec_row = row("x")

    def vec_x(j, chip):
        return remote(vx.at[chip], vx.at[chip], xs.at[vec_row, j - 1], xr.at[vec_row, j - 1], x_dev(j))

    lax.fori_loop(1, C, lambda j, carry: (vec_x(j, c).start(), carry)[1], 0)

    feed_last(st_up, xr_up, up_g, g_up)
    feed_last(st_dn, xr_dn, dn_g, g_dn)
    q_z += group_last(turns[-1])
    lax.fori_loop(1, C, lambda j, carry: (vec_x(j, lax.rem(c - j + C, C)).wait_recv(), carry)[1], 0)
    vz[t] = lax.fori_loop(1, C, lambda j, value: value + vx[j], vx[0])
    v_z = over_z(lambda k: (vz.at[t], vz.at[t]))
    i = count["z"] - 1
    v_in = [remote(vz.at[head(k)], vz.at[head(k)], zs.at[i, k - 1], zr.at[i, k - 1], z_dev(k)) for k in range(1, T)]
    start(v_z)
    for h in range(3, T):
        lg_hop(h)
    arrive(v_in)
    g_vec[...] = lax.fori_loop(1, T, lambda k, value: value + vz[k], vz[0])
    arrive(o_z)
    total = zb_o[0].astype(F32)
    for k in range(1, T):
        total = total + zr_o[k - 1].astype(F32)
    g_o[...] = total
    arrive(q_z)
    total = zb_qkv[0].astype(F32)
    for k in range(1, T):
        total = total + zr_qkv[k - 1].astype(F32)
    g_qkv[...] = total

    nl_end()
    lg_end()
    for copy in started:
        copy.wait_send()
    lax.fori_loop(1, C, lambda j, carry: (vec_x(j, c).wait_send(), carry)[1], 0)
    for s in range(S):
        pltpu.make_async_copy(mown.at[s], media_grad.at[s], osem.at[s]).wait()


def hand_out(z, *refs):
    ins, outs, held, results, sem_in, sem_out = refs[:8], refs[8:23], refs[23:31], refs[31:38], refs[38], refs[39]
    order = (1, 0, 2, 5, 6, 3, 4, 7)
    loads = {i: pltpu.make_async_copy(ins[i], held[i], sem_in.at[i]) for i in order}
    stores = []

    def store(src, i):
        copy = pltpu.make_async_copy(src, outs[i], sem_out.at[i])
        copy.start()
        stores.append(copy)

    for i in order:
        loads[i].start()
    new_lat, media_grad, lat_grad, g_qkv, g_o, g_up, g_dn, g_vec = held
    loads[5].wait()
    store(g_up, 7)
    loads[6].wait()
    results[0][...] = g_dn[...].T
    store(results[0], 8)
    loads[0].wait()
    store(new_lat, 0)
    loads[2].wait()
    store(lat_grad, 2)
    loads[1].wait()
    store(media_grad, 1)
    loads[3].wait()
    for m in range(3):
        store(g_qkv.at[:, pl.ds(m * z.I, z.I)], 3 + m)
    loads[4].wait()
    results[1][...] = g_o[...].T
    store(results[1], 6)
    loads[7].wait()
    for m in range(2):
        store(g_vec.at[pl.ds(m, 1)], 9 + m)
    first = lax.axis_index("dp") * z.R
    row = lax.broadcasted_iota(jnp.int32, (z.D, z.R), 0)
    col = lax.broadcasted_iota(jnp.int32, (z.D, z.R), 1)
    pick = jnp.where(row == col + first, 1.0, 0.0).astype(F32)
    own = lax.dot_general(
        g_vec[...], pick, (((1,), (0,)), ((), ())), preferred_element_type=F32, precision=lax.Precision.HIGHEST
    )
    for m in range(4):
        results[2 + m][...] = own[2 + m : 3 + m]
        store(results[2 + m], 11 + m)
    for copy in stores:
        copy.wait()


def solution(mesh):
    T, N = mesh.shape["tensor"], mesh.shape["dp"]

    def on_device(
        media_tokens,
        latents,
        image_counts,
        media_gain,
        media_shift,
        latent_gain,
        latent_shift,
        feed_gain,
        feed_shift,
        query_weight,
        key_weight,
        value_weight,
        output_weight,
        up_weight,
        down_weight,
        cotangent,
    ):
        samples, slots, width = media_tokens.shape
        z = Sizes(T, N, samples, latents.shape[1], slots, width, up_weight.shape[1], query_weight.shape[1])
        S, L, D, F, I, R, C = z.S, z.L, z.D, z.F, z.I, z.R, z.C
        row = lambda v: v.reshape(1, D)
        vmem = pl.BlockSpec(memory_space=pltpu.VMEM)
        hbm = pl.BlockSpec(memory_space=pl.ANY)
        V = pltpu.VMEM
        scratch = [
            V((S * L, D), BF16),
            V((S * L, D), BF16),
            V((F, R), BF16),
            V((I, D), BF16),
            V((T, 3, C, 2, R, I), BF16),
            V((T, C, 2, R, I), BF16),
            V((C, 2, R, F), BF16),
            V((C, 2, R, F), BF16),
            V((SLOTS_IN_FLIGHT, z.Mt, D), BF16),
            V((S, z.Mt, D), BF16),
            V((2, z.Mt, D), BF16),
            V((S * z.Kt, D), BF16),
            V((S * L, D), BF16),
            V((T, S, L, I), BF16),
            V((T, max(S, 8), z.q), F32),
            V((S * L, T * I), BF16),
            V((S * z.Kt, T * I), BF16),
            V((S * z.Kt, T * I), BF16),
            V((max(T // z.G * S, 2 * D // BLOCK), z.Kt, z.G * z.q), F32),
            V((max(z.K, S * z.Kt), max(S, T) * 2 * I), BF16),
            V((S * L, D), F32),
            V((S * L, D), BF16),
            V((S * L, F), BF16),
            V((S * L, F), BF16),
            V((T, S * z.Lt, D), BF16),
            V((T - 1, S * z.Lt, D), BF16),
            V((T, S * z.Lt, D), BF16),
            V((T - 1, S * z.Lt, D), BF16),
            V((S * z.Lt, D), BF16),
            V((S * z.Lt, D), F32),
            V((T, S, L, I), BF16),
            V((T, S * z.Lt, T * I), BF16),
            V((T, T, S * z.Lt, I), BF16),
            V((T - 1, T, S * z.Lt, I), BF16),
            V((C, 2, R, F), BF16),
            V((C, 2, R, F), BF16),
            V((T, C, 2, R, I), BF16),
            V((T, C, 2, R, 3 * I), BF16),
            V((C, R, F), BF16),
            V((C, R, F), BF16),
            V((T, C, R, I), BF16),
            V((T, C, R, 3 * I), BF16),
            V((max(C - 1, 1), R, F), BF16),
            V((max(C - 1, 1), R, F), BF16),
            V((2, max(C - 1, 1), T // 2, R, I), BF16),
            V((T, max(C - 1, 1), 1, R, 3 * I), BF16),
            V((T, R, I), BF16),
            V((T, R, 3 * I), BF16),
            V((T - 1, R, I), BF16),
            V((T - 1, R, 3 * I), BF16),
            V((S * z.Lt, D), F32),
            V((2, 8, D), F32),
            V((8, D), F32),
            V((8, D), F32),
            V((C, 8, D), F32),
            V((T, 8, D), F32),
            pltpu.SemaphoreType.DMA((8,)),
            pltpu.SemaphoreType.DMA((SLOTS_IN_FLIGHT + 1,)),
            pltpu.SemaphoreType.DMA((S,)),
            pltpu.SemaphoreType.DMA((24, T - 1)),
            pltpu.SemaphoreType.DMA((24, T - 1)),
            pltpu.SemaphoreType.DMA((14, max(C - 1, 1))),
            pltpu.SemaphoreType.DMA((14, max(C - 1, 1))),
            pltpu.SemaphoreType.DMA((8 + 2 * C,)),
            pltpu.SemaphoreType.DMA((8 + 2 * C,)),
        ]
        shape = jax.ShapeDtypeStruct
        outs = pl.pallas_call(
            functools.partial(layer_kernel, z),
            out_shape=[
                shape((S, L, D), BF16),
                shape((S, z.Mt, D), BF16),
                shape((S, L, D), BF16),
                shape((R, 3 * I), F32),
                shape((R, I), F32),
                shape((R, F), F32),
                shape((R, F), F32),
                shape((8, D), F32),
            ],
            in_specs=[pl.BlockSpec(memory_space=pltpu.SMEM)] + [hbm] * 3 + [vmem] * 6 + [hbm] * 6,
            out_specs=[vmem, hbm] + [vmem] * 6,
            scratch_shapes=scratch,
            compiler_params=pltpu.CompilerParams(
                collective_id=0, has_side_effects=True, vmem_limit_bytes=63 * 1024 * 1024
            ),
            name="resampler_layer",
        )(
            image_counts,
            media_tokens,
            latents.reshape(S * L, D),
            cotangent.reshape(S * L, D),
            row(media_gain),
            row(media_shift),
            row(latent_gain),
            row(latent_shift),
            row(feed_gain),
            row(feed_shift),
            query_weight.reshape(C, 2, R, I),
            key_weight.reshape(C, 2, R, I),
            value_weight.reshape(C, 2, R, I),
            output_weight,
            up_weight,
            down_weight,
        )
        final = pl.pallas_call(
            functools.partial(hand_out, z),
            out_shape=[
                shape((S, L, D), BF16),
                shape((S, z.Mt, D), BF16),
                shape((S, L, D), BF16),
                shape((R, I), F32),
                shape((R, I), F32),
                shape((R, I), F32),
                shape((I, R), F32),
                shape((R, F), F32),
                shape((F, R), F32),
                shape((1, D), F32),
                shape((1, D), F32),
            ]
            + [shape((1, R), F32)] * 4,
            in_specs=[hbm] * 8,
            out_specs=[hbm] * 15,
            scratch_shapes=[V(out.shape, out.dtype) for out in outs]
            + [V((F, R), F32), V((I, R), F32)]
            + [V((1, R), F32)] * 5
            + [pltpu.SemaphoreType.DMA((8,)), pltpu.SemaphoreType.DMA((15,))],
            name="hand_out",
        )(*outs)
        return tuple(final[:9]) + tuple(v.reshape(-1) for v in final[9:])

    placed = (
        P("dp", None, None),
        P("dp", None, None),
        P("dp"),
        P(),
        P(),
        P(),
        P(),
        P(),
        P(),
        P(None, "tensor"),
        P(None, "tensor"),
        P(None, "tensor"),
        P("tensor", None),
        P("dp", "tensor"),
        P("tensor", "dp"),
        P("dp", None, None),
    )
    return jax.shard_map(
        on_device,
        mesh=mesh,
        in_specs=placed,
        out_specs=(
            P("dp", None, None),
            P("dp", "tensor", None),
            P("dp", None, None),
            P("dp", "tensor"),
            P("dp", "tensor"),
            P("dp", "tensor"),
            P("tensor", "dp"),
            P("dp", "tensor"),
            P("tensor", "dp"),
            P(),
            P(),
            P("dp"),
            P("dp"),
            P("dp"),
            P("dp"),
        ),
        check_vma=False,
    )
```
